32 devices in a mesh: dp: 2 (over y), expert: 16 (over z, x, core).
Axes of the slice: x: 2, y: 2, z: 4, core: 2. Of those that a mesh axis runs over, the one named last changes fastest.
Arguments:
- tokens: bfloat16 [4096, 2048], P(('dp', 'expert')), may hold values from -6 to 6
- cotangent: bfloat16 [4096, 2048], P(('dp', 'expert')), may hold values from -6 to 6
- routes: int32 [4096, 2], P(('dp', 'expert')), may hold values from 0 to 15, all different within a row; in each aligned block of 128 rows (0 to 127, 128 to 255, ...) at most 24 rows name the same one
- gates: float32 [4096, 2], P(('dp', 'expert')), may hold values from 0.1 to 1
- w_gate: bfloat16 [16, 2048, 768], P('expert', None, 'dp'), may hold values from -0.125 to 0.125
- w_up: bfloat16 [16, 2048, 768], P('expert', None, 'dp'), may hold values from -0.125 to 0.125
- w_down: bfloat16 [16, 768, 2048], P('expert', 'dp'), may hold values from -0.21875 to 0.21875
Outputs:
- mixed: bfloat16 [4096, 2048], P(('dp', 'expert'))
- token_grad: bfloat16 [4096, 2048], P(('dp', 'expert'))
- gate_grad: float32 [4096, 2], P(('dp', 'expert'))
The draws below stay inside these ranges and needn't reach their ends.
Inputs may be any that keep to these rules, and one draw needn't show every extreme that they name: `routes`: each row names 2 different experts. In each aligned block of 128 rows (the rows of one device), no expert is named by more than 24 rows, a bound that some block reaches.
All inputs are finite; a program needn't handle non-finite values.
Results may differ from the reference program's by a relative error of at most 0.014.
Values may be sent and summed in bfloat16 or wider, within the bound.
No kernel may reach another device: no remote copies, remote signals or barrier semaphores. Data moves between devices by JAX's collectives and lax.ppermute only.
A program may use at most 64 MiB of HBM per device.

```python
import math
import jax
import jax.numpy as jnp
import numpy as np
from jax import lax

D = 2048
FF = 768
TOP = 2
TOK_DEV = 128
EXPERTS = 16
CAP = 24
TOKENS = 4096
N_DP = 2
N_EXPERT = 16


def level_of(own_key, dims, cuts, low, largest):
    gain, own = 1.0, jax.random.fold_in(own_key, 6)
    for axis_at, blocks in cuts:
        steps = jnp.exp(jax.random.uniform(jax.random.fold_in(own, axis_at), (blocks,), jnp.float32, low / len(cuts), largest / len(cuts)))
        gain = gain * jnp.repeat(steps, dims[axis_at] // blocks).reshape([-1 if axis == axis_at else 1 for axis in range(len(dims))])
    return gain


def routed_block(rng, own, number, rows, amount, top, most, slope):
    order = jax.random.permutation(rng, amount)
    crowded, common = shares(amount, rows * top, most, slope, True), shares(amount, rows * top, most, slope, False)
    places = jnp.arange(amount)

    def named(lengths, rotation):
        used = int((lengths > 0).sum())
        fixed = max(1, used // 4)
        passed = fixed + (places - fixed + rotation * (used - fixed)) % max(1, amount - fixed)
        return jnp.zeros((amount,), jnp.int32).at[order[jnp.where(places < fixed, places, passed)]].set(jnp.asarray(lengths, jnp.int32))

    lengths = jnp.where(number % 4 == 0, named(crowded, number // 4), named(common, number - number // 4 - 1))
    mixed = jax.random.permutation(jax.random.fold_in(own, 3), amount)
    source_of, taker = mixed[0:amount // 2 * 2:2], mixed[1:amount // 2 * 2:2]
    margin = jnp.minimum(lengths[source_of] - 1, most - lengths[taker]) // 2
    margin = jnp.where((source_of == order[0]) | (taker == order[0]) | (lengths[taker] == 0), 0, jnp.maximum(margin, 0))
    passed = jax.random.randint(jax.random.fold_in(own, 4), (amount // 2,), 0, 1 << 20) % (margin + 1)
    lengths = lengths.at[source_of].add(-passed).at[taker].add(passed)
    items = jnp.searchsorted(jnp.cumsum(lengths), jnp.arange(rows * top), side="right").astype(jnp.int32)
    grid = items.reshape(top, rows).T
    grid = grid[jax.random.permutation(jax.random.fold_in(own, 1), rows)]
    rotation = jax.random.randint(jax.random.fold_in(own, 2), (rows, 1), 0, top)
    return jnp.take_along_axis(grid, (jnp.arange(top)[None, :] + rotation) % top, axis=1)


def shares(number_of, total, most, slope, full):
    loads = [(1 << 20) // math.isqrt(standing ** slope) + 1 for standing in range(1, number_of + 1)]
    largest = most if full else min(most, max(-(-total // number_of), total * loads[0] // sum(loads)))
    least = 1 if total - largest >= number_of - 1 else 0
    given, surplus = [largest] + [least] * (number_of - 1), total - largest - least * (number_of - 1)
    while surplus > 0:
        candidates = [i for i in range(1, number_of) if given[i] < largest] or [i for i in range(1, number_of) if given[i] < most]
        mass, remaining = sum([loads[i] for i in candidates]), surplus
        for i in candidates:
            addition = min(most - given[i], max(1, remaining * loads[i] // mass), surplus)
            given[i] = given[i] + addition
            surplus = surplus - addition
    return np.array(given)


def noise(key, dims, spread, most, split=(), held_as=jnp.bfloat16):
    array = jax.random.normal(key, dims, jnp.float32) * spread
    if len(split) > 0:
        array = level_of(key, dims, split, -0.22, 0.18) * array
    return jnp.clip(array, min=-most, max=most).astype(held_as)


def setup_inputs(seed: int = 0) -> dict:
    key_of = jax.random.split(jax.random.key(seed), 8)
    tokens = noise(key_of[0], (TOKENS, D), 1.0, 6.0, ((0, 32),))
    cotangent = noise(key_of[1], (TOKENS, D), 1.0, 6.0, ((0, 32),))
    routes_keys = jax.random.split(jax.random.fold_in(key_of[2], 1), TOKENS // TOK_DEV)
    routes_turns = jax.random.permutation(jax.random.fold_in(key_of[2], 3), TOKENS // TOK_DEV)
    routes = jax.vmap(lambda own, number: routed_block(jax.random.fold_in(key_of[2], 2), own, number, TOK_DEV, EXPERTS, TOP, CAP, 2))(routes_keys, routes_turns).reshape((TOKENS, TOP))
    gates = jnp.clip(jnp.exp(math.log(1.0) - 2.3025851 * jax.random.uniform(key_of[3], (TOKENS, TOP), jnp.float32) ** level_of(key_of[3], (TOKENS, TOP), ((0, 32),), -0.2, 0.2)), 0.1, 1.0)
    w_gate = noise(key_of[4], (EXPERTS, D, FF), D ** -0.5, 0.125, ((0, 16), (2, 2)))
    w_up = noise(key_of[5], (EXPERTS, D, FF), D ** -0.5, 0.125, ((0, 16), (2, 2)))
    w_down = noise(key_of[6], (EXPERTS, FF, D), FF ** -0.5, 0.21875, ((0, 16), (1, 2)))
    return {"tokens": tokens, "cotangent": cotangent, "routes": routes, "gates": gates, "w_gate": w_gate, "w_up": w_up, "w_down": w_down}


def expert_rows(rows, back_rows, weight_rows, gate_w, up_w, down_w):
    pre_gate = jnp.dot(rows, gate_w, preferred_element_type=jnp.float32)
    pre_up = jnp.dot(rows, up_w, preferred_element_type=jnp.float32)
    sig = jax.nn.sigmoid(pre_gate)
    act = pre_gate * sig
    hidden = (act * pre_up).astype(jnp.bfloat16)
    raw_out = jnp.dot(hidden, down_w, preferred_element_type=jnp.float32)
    slot_out = (weight_rows[:, None] * raw_out).astype(jnp.bfloat16)
    back_hidden = jnp.dot(back_rows, down_w.T, preferred_element_type=jnp.float32)
    gate_part = jnp.sum(hidden.astype(jnp.float32) * back_hidden, axis=1)
    scaled = weight_rows[:, None] * back_hidden
    back_gate = (scaled * pre_up * sig * (1.0 + pre_gate * (1.0 - sig))).astype(jnp.bfloat16)
    back_up = (scaled * act).astype(jnp.bfloat16)
    slot_grad = jnp.dot(back_gate, gate_w.T, preferred_element_type=jnp.float32)
    slot_grad = (slot_grad + jnp.dot(back_up, up_w.T, preferred_element_type=jnp.float32)).astype(jnp.bfloat16)
    return slot_out, slot_grad, gate_part


def reference(tokens, cotangent, routes, gates, w_gate, w_up, w_down):
    slots = TOKENS * TOP
    most_rows = N_DP * N_EXPERT * CAP
    expert_ids = routes.reshape(slots).astype(jnp.int32)
    onehot = (expert_ids[:, None] == jnp.arange(EXPERTS, dtype=jnp.int32)[None, :]).astype(jnp.int32)
    slot_rank = jnp.sum(onehot * (jnp.cumsum(onehot, axis=0) - onehot), axis=1).astype(jnp.int32)
    table = jnp.full((EXPERTS * most_rows,), slots, jnp.int32)
    table = table.at[expert_ids * most_rows + slot_rank].set(jnp.arange(slots, dtype=jnp.int32))
    table = table.reshape(EXPERTS, most_rows)
    padded_tok = jnp.concatenate([tokens, jnp.zeros((1, D), jnp.bfloat16)], axis=0)
    padded_cot = jnp.concatenate([cotangent, jnp.zeros((1, D), jnp.bfloat16)], axis=0)
    padded_gate = jnp.concatenate([gates.reshape(slots), jnp.zeros((1,), jnp.float32)], axis=0)

    def one_expert(carry, item):
        out_acc, grad_acc, gate_acc = carry
        gate_w, up_w, down_w, row_table = item
        tok_index = jnp.where(row_table < slots, row_table // TOP, TOKENS).astype(jnp.int32)
        slot_out, slot_grad, gate_part = expert_rows(padded_tok[tok_index], padded_cot[tok_index],
                                                     padded_gate[row_table], gate_w, up_w, down_w)
        out_acc = out_acc.at[tok_index].add(slot_out.astype(jnp.float32))
        grad_acc = grad_acc.at[tok_index].add(slot_grad.astype(jnp.float32))
        gate_acc = gate_acc.at[row_table].add(gate_part)
        return (out_acc, grad_acc, gate_acc), None

    start = (jnp.zeros((TOKENS + 1, D), jnp.float32), jnp.zeros((TOKENS + 1, D), jnp.float32),
             jnp.zeros((slots + 1,), jnp.float32))
    (out_acc, grad_acc, gate_acc), _ = lax.scan(one_expert, start, (w_gate, w_up, w_down, table))
    mixed = out_acc[:TOKENS].astype(jnp.bfloat16)
    token_grad = grad_acc[:TOKENS].astype(jnp.bfloat16)
    gate_grad = gate_acc[:slots].reshape(TOKENS, TOP)
    return mixed, token_grad, gate_grad
```

```python
import functools

import jax
import jax.numpy as jnp
from jax import lax
from jax.experimental import pallas as pl
from jax.experimental.pallas import tpu as pltpu
from jax.sharding import PartitionSpec as P

BF16 = jnp.bfloat16
F32 = jnp.float32
VMEM_BYTES = 48 << 20


def dot(a, b, dims):
    return lax.dot_general(a, b, ((dims[:1], dims[1:]), ((), ())), preferred_element_type=F32)


def place_kernel(experts, capacity, routes_ref, tokens_ref, slots_ref, place_ref):
    tok_rows, top_count = routes_ref.shape
    routes = routes_ref[...]
    lanes = lax.broadcasted_iota(jnp.int32, (tok_rows, experts), 1)
    named = [lanes == routes[:, k : k + 1] for k in range(top_count)]
    chosen = sum(n.astype(F32) for n in named)
    earlier = (
        lax.broadcasted_iota(jnp.int32, (tok_rows, tok_rows), 1)
        < lax.broadcasted_iota(jnp.int32, (tok_rows, tok_rows), 0)
    ).astype(F32)
    rank = dot(earlier.astype(BF16), chosen.astype(BF16), (1, 0))
    slot_lanes = lax.broadcasted_iota(jnp.int32, (tok_rows, experts * capacity), 1)
    total = None
    for k in range(top_count):
        own = jnp.sum(jnp.where(named[k], rank, 0.0), axis=1, keepdims=True)
        slot = routes[:, k : k + 1] * capacity + own.astype(jnp.int32)
        mark = (slot_lanes == slot).astype(F32)
        place_ref[k * tok_rows : (k + 1) * tok_rows, :] = mark.astype(BF16)
        total = mark if total is None else total + mark
    slots_ref[...] = dot(total.astype(BF16), tokens_ref[...], (0, 0)).astype(BF16)


def spread_kernel(top_count, place_ref, rows_ref, slots_ref):
    tok_rows = rows_ref.shape[0]
    total = sum(
        place_ref[k * tok_rows : (k + 1) * tok_rows, :].astype(F32) for k in range(top_count)
    )
    slots_ref[...] = dot(total.astype(BF16), rows_ref[...], (0, 0)).astype(BF16)


def forward_kernel(parts, *refs):
    rows_ref = refs[0]
    gate_refs, up_refs, down_refs = (refs[1 + i * parts : 1 + (i + 1) * parts] for i in range(3))
    out_ref, by_gate_ref, by_up_ref, hidden_ref = refs[1 + 3 * parts :]
    width = rows_ref.shape[1]
    for i in range(parts):
        rows = rows_ref[...]
        pre_gate = dot(rows, gate_refs[i][...], (1, 0))
        pre_up = dot(rows, up_refs[i][...], (1, 0))
        sig = jax.nn.sigmoid(pre_gate)
        act = pre_gate * sig
        hidden_ref[i] = (act * pre_up).astype(BF16)
        by_gate_ref[i] = pre_up * sig * (1.0 + pre_gate * (1.0 - sig))
        by_up_ref[i] = act
    tile = min(512, width)
    for d in range(0, width, tile):
        out_ref[:, d : d + tile] = sum(
            dot(hidden_ref[i], down_refs[i][:, d : d + tile], (1, 0)) for i in range(parts)
        ).astype(BF16)


def backward_kernel(parts, *refs):
    rows_ref = refs[0]
    gate_refs, up_refs, down_refs = (refs[1 + i * parts : 1 + (i + 1) * parts] for i in range(3))
    by_gate_ref, by_up_ref, out_ref, back_gate_ref, back_up_ref = refs[1 + 3 * parts :]
    width = rows_ref.shape[1]
    for i in range(parts):
        back_hidden = dot(rows_ref[...], down_refs[i][...], (1, 1))
        back_gate_ref[i] = (back_hidden * by_gate_ref[i]).astype(BF16)
        back_up_ref[i] = (back_hidden * by_up_ref[i]).astype(BF16)
    tile = min(512, width)
    for d in range(0, width, tile):
        out_ref[:, d : d + tile] = sum(
            dot(back_gate_ref[i], gate_refs[i][d : d + tile, :], (1, 1))
            + dot(back_up_ref[i], up_refs[i][d : d + tile, :], (1, 1))
            for i in range(parts)
        ).astype(BF16)


def mix_kernel(place_ref, gates_ref, slots_ref, cotangent_ref, mixed_ref, gate_grad_ref):
    tok_rows, top_count = gates_ref.shape
    total, grads = None, []
    for k in range(top_count):
        raw = dot(place_ref[k * tok_rows : (k + 1) * tok_rows, :], slots_ref[...], (1, 0))
        grads.append(jnp.sum(raw * cotangent_ref[...].astype(F32), axis=1, keepdims=True))
        part = raw * gates_ref[:, k : k + 1]
        total = part if total is None else total + part
    mixed_ref[...] = total.astype(BF16)
    gate_grad_ref[...] = jnp.concatenate(grads, axis=1)


def sum_kernel(place_ref, gates_ref, slots_ref, out_ref):
    tok_rows, top_count = gates_ref.shape
    total = None
    for k in range(top_count):
        raw = dot(place_ref[k * tok_rows : (k + 1) * tok_rows, :], slots_ref[...], (1, 0))
        part = raw * gates_ref[:, k : k + 1]
        total = part if total is None else total + part
    out_ref[...] = total.astype(BF16)


def call(kernel, outs, flops, scratch=()):
    def run(*args):
        moved = sum(a.size * a.dtype.itemsize for a in (*args, *outs))
        return pl.pallas_call(
            kernel,
            out_shape=outs,
            scratch_shapes=scratch,
            compiler_params=pltpu.CompilerParams(vmem_limit_bytes=VMEM_BYTES),
            cost_estimate=pl.CostEstimate(flops=flops, bytes_accessed=moved, transcendentals=0),
        )(*args)

    return run


def body(tokens, cotangent, routes, gates, w_gate, w_up, w_down):
    tok_rows, width = tokens.shape
    top_count = routes.shape[1]
    parts, experts = lax.axis_size("dp"), lax.axis_size("expert")
    hidden = w_gate.shape[2]
    capacity = max(2, 3 * tok_rows * top_count // (2 * experts))
    slots = experts * capacity
    axes = ("dp", "expert")

    def device(g, j):
        return g * experts + j

    swap = [
        (device(g, parts * q + r), device(r, parts * q + g))
        for g in range(parts)
        for q in range(experts // parts)
        for r in range(parts)
    ]
    groups = [
        [device(e % parts, e // parts * parts + c) for e in range(experts)] for c in range(parts)
    ]

    def whole_expert(weight):
        own = lax.ppermute(weight[0], axes, swap)
        shares = [own]
        for step in range(1, parts):
            turn = [(j, j // parts * parts + (j + step) % parts) for j in range(experts)]
            shares.append(lax.ppermute(own, "expert", turn))
        return shares

    def exchange(rows):
        return lax.all_to_all(
            rows.reshape(experts, capacity, width),
            axes,
            split_axis=0,
            concat_axis=0,
            axis_index_groups=groups,
            tiled=True,
        ).reshape(slots, width)

    spread_flops = 2 * slots * tok_rows * width
    dot_flops = 2 * slots * width * hidden * parts
    slot_shape = jax.ShapeDtypeStruct((slots, width), BF16)
    unit_shape = jax.ShapeDtypeStruct((parts, slots, hidden), F32)
    token_shape = jax.ShapeDtypeStruct((tok_rows, width), BF16)
    unit_scratch = pltpu.VMEM((parts, slots, hidden), BF16)

    gate_w, up_w, down_w = whole_expert(w_gate), whole_expert(w_up), whole_expert(w_down)
    x_slots, place = call(
        functools.partial(place_kernel, experts, capacity),
        (slot_shape, jax.ShapeDtypeStruct((top_count * tok_rows, slots), BF16)),
        spread_flops,
    )(routes, tokens)
    x_rows = exchange(x_slots)
    (dy_slots,) = call(functools.partial(spread_kernel, top_count), (slot_shape,), spread_flops)(
        place, cotangent
    )
    dy_rows = exchange(dy_slots)
    out_rows, by_gate, by_up = call(
        functools.partial(forward_kernel, parts),
        (slot_shape, unit_shape, unit_shape),
        3 * dot_flops,
        [unit_scratch],
    )(x_rows, *gate_w, *up_w, *down_w)
    out_slots = exchange(out_rows)
    (grad_rows,) = call(
        functools.partial(backward_kernel, parts),
        (slot_shape,),
        3 * dot_flops,
        [unit_scratch, unit_scratch],
    )(dy_rows, *gate_w, *up_w, *down_w, by_gate, by_up)
    grad_slots = exchange(grad_rows)
    mixed, gate_grad = call(
        mix_kernel,
        (token_shape, jax.ShapeDtypeStruct(gates.shape, F32)),
        2 * spread_flops,
    )(place, gates, out_slots, cotangent)
    (token_grad,) = call(sum_kernel, (token_shape,), 2 * spread_flops)(place, gates, grad_slots)
    return (mixed, token_grad, gate_grad)


def solution(mesh):
    rows, weights = P(("dp", "expert"), None), P("expert", None, "dp")
    return jax.shard_map(
        body,
        mesh=mesh,
        in_specs=(rows, rows, rows, rows, weights, weights, P("expert", "dp", None)),
        out_specs=(rows, rows, rows),
        check_vma=False,
    )
```

```python
import functools

import jax
import jax.numpy as jnp
from jax import lax
from jax.experimental import pallas as pl
from jax.experimental.pallas import tpu as pltpu
from jax.sharding import PartitionSpec as P

BF16 = jnp.bfloat16
F32 = jnp.float32
VMEM_BYTES = 48 << 20


def dot(a, b, dims):
    return lax.dot_general(a, b, ((dims[:1], dims[1:]), ((), ())), preferred_element_type=F32)


def tiles(width):
    tile = min(512, width)
    return [slice(d, d + tile) for d in range(0, width, tile)]


def join(lane_refs, rows_ref):
    capacity = lane_refs[0].shape[0]
    for b in range(0, len(lane_refs), 2):
        pair = [ref[...].astype(F32) for ref in lane_refs[b : b + 2]]
        rows_ref[b * capacity : (b + 2) * capacity, :] = jnp.concatenate(pair, axis=0).astype(BF16)


def part(rows, lane_refs, columns):
    capacity = lane_refs[0].shape[0]
    for b, ref in enumerate(lane_refs):
        ref[:, columns] = rows[b * capacity : (b + 1) * capacity, :].astype(BF16)


def place_kernel(lanes, capacity, routes_ref, tokens_ref, *refs):
    lane_refs, place_ref = refs[:lanes], refs[lanes]
    tok_rows, top_count = routes_ref.shape
    routes = routes_ref[...]
    numbers = lax.broadcasted_iota(jnp.int32, (tok_rows, lanes), 1)
    named = [numbers == routes[:, k : k + 1] for k in range(top_count)]
    chosen = sum(n.astype(F32) for n in named)
    earlier = (
        lax.broadcasted_iota(jnp.int32, (tok_rows, tok_rows), 1)
        < lax.broadcasted_iota(jnp.int32, (tok_rows, tok_rows), 0)
    ).astype(F32)
    rank = dot(earlier.astype(BF16), chosen.astype(BF16), (1, 0))
    slot_numbers = lax.broadcasted_iota(jnp.int32, (tok_rows, lanes * capacity), 1)
    total = None
    for k in range(top_count):
        own = jnp.sum(jnp.where(named[k], rank, 0.0), axis=1, keepdims=True)
        slot = routes[:, k : k + 1] * capacity + own.astype(jnp.int32)
        mark = (slot_numbers == slot).astype(F32)
        place_ref[k * tok_rows : (k + 1) * tok_rows, :] = mark.astype(BF16)
        total = mark if total is None else total + mark
    total = total.astype(BF16)
    for columns in tiles(tokens_ref.shape[1]):
        part(dot(total, tokens_ref[:, columns], (0, 0)), lane_refs, columns)


def spread_kernel(top_count, place_ref, rows_ref, *lane_refs):
    tok_rows = rows_ref.shape[0]
    total = sum(
        place_ref[k * tok_rows : (k + 1) * tok_rows, :].astype(F32) for k in range(top_count)
    ).astype(BF16)
    for columns in tiles(rows_ref.shape[1]):
        part(dot(total, rows_ref[:, columns], (0, 0)), lane_refs, columns)


def forward_kernel(lanes, parts, *refs):
    lane_refs, refs = refs[:lanes], refs[lanes:]
    gate_refs, up_refs, down_refs = (refs[i * parts : (i + 1) * parts] for i in range(3))
    out_refs, refs = refs[3 * parts : 3 * parts + lanes], refs[3 * parts + lanes :]
    by_gate_ref, by_up_ref, rows_ref, hidden_ref = refs
    join(lane_refs, rows_ref)
    for i in range(parts):
        pre_gate = dot(rows_ref[...], gate_refs[i][...], (1, 0))
        pre_up = dot(rows_ref[...], up_refs[i][...], (1, 0))
        sig = jax.nn.sigmoid(pre_gate)
        act = pre_gate * sig
        hidden_ref[i] = (act * pre_up).astype(BF16)
        by_gate_ref[i] = pre_up * sig * (1.0 + pre_gate * (1.0 - sig))
        by_up_ref[i] = act
    for columns in tiles(rows_ref.shape[1]):
        rows = sum(dot(hidden_ref[i], down_refs[i][:, columns], (1, 0)) for i in range(parts))
        part(rows, out_refs, columns)


def backward_kernel(lanes, parts, *refs):
    lane_refs, refs = refs[:lanes], refs[lanes:]
    gate_refs, up_refs, down_refs = (refs[i * parts : (i + 1) * parts] for i in range(3))
    by_gate_ref, by_up_ref = refs[3 * parts : 3 * parts + 2]
    out_refs, refs = refs[3 * parts + 2 : 3 * parts + 2 + lanes], refs[3 * parts + 2 + lanes :]
    rows_ref, back_gate_ref, back_up_ref = refs
    join(lane_refs, rows_ref)
    for i in range(parts):
        back_hidden = dot(rows_ref[...], down_refs[i][...], (1, 1))
        back_gate_ref[i] = (back_hidden * by_gate_ref[i]).astype(BF16)
        back_up_ref[i] = (back_hidden * by_up_ref[i]).astype(BF16)
    for columns in tiles(rows_ref.shape[1]):
        rows = sum(
            dot(back_gate_ref[i], gate_refs[i][columns, :], (1, 1))
            + dot(back_up_ref[i], up_refs[i][columns, :], (1, 1))
            for i in range(parts)
        )
        part(rows, out_refs, columns)


def mix_kernel(lanes, place_ref, gates_ref, cotangent_ref, *refs):
    mixed_ref, gate_grad_ref, rows_ref = refs[lanes:]
    tok_rows, top_count = gates_ref.shape
    join(refs[:lanes], rows_ref)
    total, grads = None, []
    for k in range(top_count):
        raw = dot(place_ref[k * tok_rows : (k + 1) * tok_rows, :], rows_ref[...], (1, 0))
        grads.append(jnp.sum(raw * cotangent_ref[...].astype(F32), axis=1, keepdims=True))
        term = raw * gates_ref[:, k : k + 1]
        total = term if total is None else total + term
    mixed_ref[...] = total.astype(BF16)
    gate_grad_ref[...] = jnp.concatenate(grads, axis=1)


def sum_kernel(lanes, place_ref, gates_ref, *refs):
    out_ref, rows_ref = refs[lanes:]
    tok_rows, top_count = gates_ref.shape
    join(refs[:lanes], rows_ref)
    total = None
    for k in range(top_count):
        raw = dot(place_ref[k * tok_rows : (k + 1) * tok_rows, :], rows_ref[...], (1, 0))
        term = raw * gates_ref[:, k : k + 1]
        total = term if total is None else total + term
    out_ref[...] = total.astype(BF16)


def call(kernel, outs, flops, scratch=()):
    def run(*args):
        moved = sum(a.size * a.dtype.itemsize for a in (*args, *outs))
        return pl.pallas_call(
            kernel,
            out_shape=tuple(outs),
            scratch_shapes=scratch,
            compiler_params=pltpu.CompilerParams(vmem_limit_bytes=VMEM_BYTES),
            cost_estimate=pl.CostEstimate(flops=flops, bytes_accessed=moved, transcendentals=0),
        )(*args)

    return run


def body(tokens, cotangent, routes, gates, w_gate, w_up, w_down):
    tok_rows, width = tokens.shape
    top_count = routes.shape[1]
    parts, experts = lax.axis_size("dp"), lax.axis_size("expert")
    hidden = w_gate.shape[2]
    capacity = max(2, 3 * tok_rows * top_count // (2 * experts))
    capacity = -(-capacity // 8) * 8
    slots = experts * capacity
    axes = ("dp", "expert")

    def device(g, j):
        return g * experts + j

    def home(e, c):
        return device((e + 1) % parts, e // parts * parts + c)

    swap = [(device(g, e), home(e, g)) for g in range(parts) for e in range(experts)]

    def whole_expert(weight):
        own = lax.ppermute(weight[0], axes, swap)
        shares = [own]
        for step in range(1, parts):
            turn = [(j, j // parts * parts + (j + step) % parts) for j in range(experts)]
            shares.append(lax.ppermute(own, "expert", turn))
        return shares

    def exchange(lane_rows):
        received = [lane_rows[0]]
        for b in range(1, experts):
            pairs = [(home(e, c), home(e ^ b, c)) for c in range(parts) for e in range(experts)]
            received.append(lax.ppermute(lane_rows[b], axes, pairs))
        return received

    spread_flops = 2 * slots * tok_rows * width
    dot_flops = 2 * slots * width * hidden * parts
    lane_shapes = [jax.ShapeDtypeStruct((capacity, width), BF16)] * experts
    place_shape = jax.ShapeDtypeStruct((top_count * tok_rows, slots), BF16)
    unit_shape = jax.ShapeDtypeStruct((parts, slots, hidden), F32)
    token_shape = jax.ShapeDtypeStruct((tok_rows, width), BF16)
    unit_scratch = pltpu.VMEM((parts, slots, hidden), BF16)
    row_scratch = pltpu.VMEM((slots, width), BF16)

    gate_w, up_w, down_w = whole_expert(w_gate), whole_expert(w_up), whole_expert(w_down)
    column = lax.axis_index("expert")
    place_here = column // parts * parts + (lax.axis_index("dp") + parts - 1) % parts
    *x_lanes, place = call(
        functools.partial(place_kernel, experts, capacity),
        [*lane_shapes, place_shape],
        spread_flops,
    )(routes ^ place_here, tokens)
    x_rows = exchange(x_lanes)
    dy_lanes = call(functools.partial(spread_kernel, top_count), lane_shapes, spread_flops)(
        place, cotangent
    )
    dy_rows = exchange(dy_lanes)
    *out_rows, by_gate, by_up = call(
        functools.partial(forward_kernel, experts, parts),
        [*lane_shapes, unit_shape, unit_shape],
        3 * dot_flops,
        [row_scratch, unit_scratch],
    )(*x_rows, *gate_w, *up_w, *down_w)
    out_lanes = exchange(out_rows)
    grad_rows = call(
        functools.partial(backward_kernel, experts, parts),
        lane_shapes,
        3 * dot_flops,
        [row_scratch, unit_scratch, unit_scratch],
    )(*dy_rows, *gate_w, *up_w, *down_w, by_gate, by_up)
    grad_lanes = exchange(grad_rows)
    mixed, gate_grad = call(
        functools.partial(mix_kernel, experts),
        [token_shape, jax.ShapeDtypeStruct(gates.shape, F32)],
        2 * spread_flops,
        [row_scratch],
    )(place, gates, cotangent, *out_lanes)
    (token_grad,) = call(
        functools.partial(sum_kernel, experts), [token_shape], 2 * spread_flops, [row_scratch]
    )(place, gates, *grad_lanes)
    return (mixed, token_grad, gate_grad)


def solution(mesh):
    rows, weights = P(("dp", "expert"), None), P("expert", None, "dp")
    return jax.shard_map(
        body,
        mesh=mesh,
        in_specs=(rows, rows, rows, rows, weights, weights, P("expert", "dp", None)),
        out_specs=(rows, rows, rows),
        check_vma=False,
    )
```

```python
import functools

import jax
import jax.numpy as jnp
from jax import lax
from jax.experimental import pallas as pl
from jax.experimental.pallas import tpu as pltpu
from jax.sharding import PartitionSpec as P

BF16 = jnp.bfloat16
F32 = jnp.float32
VMEM_BYTES = 48 << 20


def dot(a, b, dims):
    return lax.dot_general(a, b, ((dims[:1], dims[1:]), ((), ())), preferred_element_type=F32)


def tiles(width):
    tile = min(512, width)
    return [slice(d, d + tile) for d in range(0, width, tile)]


def join(lanes, rows_ref):
    for b in range(0, len(lanes), 2):
        pair = jnp.concatenate([lane[...].astype(F32) for lane in lanes[b : b + 2]], axis=0)
        start = b * pair.shape[0] // 2
        rows_ref[start : start + pair.shape[0], :] = pair.astype(BF16)


def part(rows, lanes, columns):
    capacity = lanes[0].shape[0]
    for b, lane in enumerate(lanes):
        lane[:, columns] = rows[b * capacity : (b + 1) * capacity, :].astype(BF16)


def by_difference(rows_ref, here_ref):
    return [rows_ref.at[here_ref[0] ^ b] for b in range(rows_ref.shape[0])]


def place_kernel(here_ref, routes_ref, tokens_ref, slots_ref, place_ref):
    lanes, capacity, width = slots_ref.shape
    tok_rows, top_count = routes_ref.shape
    routes = routes_ref[...] ^ here_ref[0]
    numbers = lax.broadcasted_iota(jnp.int32, (tok_rows, lanes), 1)
    named = [numbers == routes[:, k : k + 1] for k in range(top_count)]
    chosen = sum(n.astype(F32) for n in named)
    earlier = (
        lax.broadcasted_iota(jnp.int32, (tok_rows, tok_rows), 1)
        < lax.broadcasted_iota(jnp.int32, (tok_rows, tok_rows), 0)
    ).astype(F32)
    rank = dot(earlier.astype(BF16), chosen.astype(BF16), (1, 0))
    slot_numbers = lax.broadcasted_iota(jnp.int32, (tok_rows, lanes * capacity), 1)
    total = None
    for k in range(top_count):
        own = jnp.sum(jnp.where(named[k], rank, 0.0), axis=1, keepdims=True)
        slot = routes[:, k : k + 1] * capacity + own.astype(jnp.int32)
        mark = (slot_numbers == slot).astype(F32)
        place_ref[k * tok_rows : (k + 1) * tok_rows, :] = mark.astype(BF16)
        total = mark if total is None else total + mark
    total = total.astype(BF16)
    slot_lanes = by_difference(slots_ref, here_ref)
    for columns in tiles(width):
        part(dot(total, tokens_ref[:, columns], (0, 0)), slot_lanes, columns)


def spread_kernel(top_count, here_ref, place_ref, rows_ref, slots_ref):
    tok_rows = rows_ref.shape[0]
    slot_lanes = by_difference(slots_ref, here_ref)
    total = sum(
        place_ref[k * tok_rows : (k + 1) * tok_rows, :].astype(F32) for k in range(top_count)
    ).astype(BF16)
    for columns in tiles(rows_ref.shape[1]):
        part(dot(total, rows_ref[:, columns], (0, 0)), slot_lanes, columns)


def forward_kernel(parts, here_ref, lanes_ref, *refs):
    lanes = lanes_ref.shape[0]
    gate_refs, up_refs, down_refs = (refs[i * parts : (i + 1) * parts] for i in range(3))
    out_refs, refs = refs[3 * parts : 3 * parts + lanes], refs[3 * parts + lanes :]
    by_gate_ref, by_up_ref, rows_ref, hidden_ref = refs
    join(by_difference(lanes_ref, here_ref), rows_ref)
    for i in range(parts):
        pre_gate = dot(rows_ref[...], gate_refs[i][...], (1, 0))
        pre_up = dot(rows_ref[...], up_refs[i][...], (1, 0))
        sig = jax.nn.sigmoid(pre_gate)
        act = pre_gate * sig
        hidden_ref[i] = (act * pre_up).astype(BF16)
        by_gate_ref[i] = pre_up * sig * (1.0 + pre_gate * (1.0 - sig))
        by_up_ref[i] = act
    for columns in tiles(rows_ref.shape[1]):
        rows = sum(dot(hidden_ref[i], down_refs[i][:, columns], (1, 0)) for i in range(parts))
        part(rows, out_refs, columns)


def backward_kernel(parts, here_ref, lanes_ref, *refs):
    lanes = lanes_ref.shape[0]
    gate_refs, up_refs, down_refs = (refs[i * parts : (i + 1) * parts] for i in range(3))
    by_gate_ref, by_up_ref = refs[3 * parts : 3 * parts + 2]
    out_refs, refs = refs[3 * parts + 2 : 3 * parts + 2 + lanes], refs[3 * parts + 2 + lanes :]
    rows_ref, back_gate_ref, back_up_ref = refs
    join(by_difference(lanes_ref, here_ref), rows_ref)
    for i in range(parts):
        back_hidden = dot(rows_ref[...], down_refs[i][...], (1, 1))
        back_gate_ref[i] = (back_hidden * by_gate_ref[i]).astype(BF16)
        back_up_ref[i] = (back_hidden * by_up_ref[i]).astype(BF16)
    for columns in tiles(rows_ref.shape[1]):
        rows = sum(
            dot(back_gate_ref[i], gate_refs[i][columns, :], (1, 1))
            + dot(back_up_ref[i], up_refs[i][columns, :], (1, 1))
            for i in range(parts)
        )
        part(rows, out_refs, columns)


def mix_kernel(lanes, place_ref, gates_ref, cotangent_ref, *refs):
    mixed_ref, gate_grad_ref, rows_ref = refs[lanes:]
    tok_rows, top_count = gates_ref.shape
    join(refs[:lanes], rows_ref)
    total, grads = None, []
    for k in range(top_count):
        raw = dot(place_ref[k * tok_rows : (k + 1) * tok_rows, :], rows_ref[...], (1, 0))
        grads.append(jnp.sum(raw * cotangent_ref[...].astype(F32), axis=1, keepdims=True))
        term = raw * gates_ref[:, k : k + 1]
        total = term if total is None else total + term
    mixed_ref[...] = total.astype(BF16)
    gate_grad_ref[...] = jnp.concatenate(grads, axis=1)


def sum_kernel(lanes, place_ref, gates_ref, *refs):
    out_ref, rows_ref = refs[lanes:]
    tok_rows, top_count = gates_ref.shape
    join(refs[:lanes], rows_ref)
    total = None
    for k in range(top_count):
        raw = dot(place_ref[k * tok_rows : (k + 1) * tok_rows, :], rows_ref[...], (1, 0))
        term = raw * gates_ref[:, k : k + 1]
        total = term if total is None else total + term
    out_ref[...] = total.astype(BF16)


def call(kernel, outs, flops, scratch=()):
    def run(*args):
        moved = sum(a.size * a.dtype.itemsize for a in (*args, *outs))
        spaces = [pltpu.SMEM if a.shape == (1,) else pltpu.VMEM for a in args]
        return pl.pallas_call(
            kernel,
            out_shape=tuple(outs),
            in_specs=[pl.BlockSpec(memory_space=space) for space in spaces],
            scratch_shapes=scratch,
            compiler_params=pltpu.CompilerParams(vmem_limit_bytes=VMEM_BYTES),
            cost_estimate=pl.CostEstimate(flops=flops, bytes_accessed=moved, transcendentals=0),
        )(*args)

    return run


def body(tokens, cotangent, routes, gates, w_gate, w_up, w_down):
    tok_rows, width = tokens.shape
    top_count = routes.shape[1]
    parts, experts = lax.axis_size("dp"), lax.axis_size("expert")
    hidden = w_gate.shape[2]
    capacity = max(2, 3 * tok_rows * top_count // (2 * experts))
    capacity = -(-capacity // 8) * 8
    slots = experts * capacity
    axes = ("dp", "expert")

    def device(g, j):
        return g * experts + j

    def home(e, c):
        return device((e + 1) % parts, e // parts * parts + c)

    swap = [(device(g, e), home(e, g)) for g in range(parts) for e in range(experts)]

    def whole_expert(weight):
        own = lax.ppermute(weight[0], axes, swap)
        shares = [own]
        for step in range(1, parts):
            turn = [(j, j // parts * parts + (j + step) % parts) for j in range(experts)]
            shares.append(lax.ppermute(own, "expert", turn))
        return shares

    def send(slot_rows):
        groups = [[home(e, c) for e in range(experts)] for c in range(parts)]
        return lax.all_to_all(slot_rows, axes, 0, 0, axis_index_groups=groups, tiled=True)

    def send_back(lane_rows):
        received = [lane_rows[0]]
        for b in range(1, experts):
            pairs = [(home(e, c), home(e ^ b, c)) for c in range(parts) for e in range(experts)]
            received.append(lax.ppermute(lane_rows[b], axes, pairs))
        return received

    spread_flops = 2 * slots * tok_rows * width
    dot_flops = 2 * slots * width * hidden * parts
    lane_shapes = [jax.ShapeDtypeStruct((capacity, width), BF16)] * experts
    slot_shape = jax.ShapeDtypeStruct((experts, capacity, width), BF16)
    place_shape = jax.ShapeDtypeStruct((top_count * tok_rows, slots), BF16)
    unit_shape = jax.ShapeDtypeStruct((parts, slots, hidden), F32)
    token_shape = jax.ShapeDtypeStruct((tok_rows, width), BF16)
    unit_scratch = pltpu.VMEM((parts, slots, hidden), BF16)
    row_scratch = pltpu.VMEM((slots, width), BF16)

    gate_w, up_w, down_w = whole_expert(w_gate), whole_expert(w_up), whole_expert(w_down)
    column = lax.axis_index("expert")
    here = column // parts * parts + (lax.axis_index("dp") + parts - 1) % parts
    here = here.astype(jnp.int32).reshape(1)
    x_slots, place = call(place_kernel, [slot_shape, place_shape], spread_flops)(
        here, routes, tokens
    )
    x_rows = send(x_slots)
    (dy_slots,) = call(
        functools.partial(spread_kernel, top_count), [slot_shape], spread_flops
    )(here, place, cotangent)
    dy_rows = send(dy_slots)
    *out_rows, by_gate, by_up = call(
        functools.partial(forward_kernel, parts),
        [*lane_shapes, unit_shape, unit_shape],
        3 * dot_flops,
        [row_scratch, unit_scratch],
    )(here, x_rows, *gate_w, *up_w, *down_w)
    out_lanes = send_back(out_rows)
    grad_rows = call(
        functools.partial(backward_kernel, parts),
        lane_shapes,
        3 * dot_flops,
        [row_scratch, unit_scratch, unit_scratch],
    )(here, dy_rows, *gate_w, *up_w, *down_w, by_gate, by_up)
    grad_lanes = send_back(grad_rows)
    mixed, gate_grad = call(
        functools.partial(mix_kernel, experts),
        [token_shape, jax.ShapeDtypeStruct(gates.shape, F32)],
        2 * spread_flops,
        [row_scratch],
    )(place, gates, cotangent, *out_lanes)
    (token_grad,) = call(
        functools.partial(sum_kernel, experts), [token_shape], 2 * spread_flops, [row_scratch]
    )(place, gates, *grad_lanes)
    return (mixed, token_grad, gate_grad)


def solution(mesh):
    rows, weights = P(("dp", "expert"), None), P("expert", None, "dp")
    return jax.shard_map(
        body,
        mesh=mesh,
        in_specs=(rows, rows, rows, rows, weights, weights, P("expert", "dp", None)),
        out_specs=(rows, rows, rows),
        check_vma=False,
    )
```

```python
import functools

import jax
import jax.numpy as jnp
from jax import lax
from jax.experimental import pallas as pl
from jax.experimental.pallas import tpu as pltpu
from jax.sharding import PartitionSpec as P

BF16 = jnp.bfloat16
F32 = jnp.float32
VMEM_BYTES = 40 << 20


def dot(a, b, dims):
    return lax.dot_general(a, b, ((dims[:1], dims[1:]), ((), ())), preferred_element_type=F32)


def tiles(width):
    tile = min(512, width)
    return [slice(d, d + tile) for d in range(0, width, tile)]


def fetch(sources, targets, sems):
    copies = [pltpu.make_async_copy(s, t, sems.at[i]) for i, (s, t) in enumerate(zip(sources, targets))]
    for copy in copies:
        copy.start()
    return copies


def store(columns, index, stage_ref, out_ref, sems):
    copy = pltpu.make_async_copy(stage_ref.at[:, columns], out_ref.at[:, columns], sems.at[index])
    copy.start()
    return copy


def place_kernel(experts, routes_ref, tokens_ref, slots_ref, place_ref):
    slots, width = slots_ref.shape
    tok_rows, top_count = routes_ref.shape
    routes = routes_ref[...]
    numbers = lax.broadcasted_iota(jnp.int32, (tok_rows, experts), 1)
    named = [numbers == routes[:, k : k + 1] for k in range(top_count)]
    chosen = sum(n.astype(F32) for n in named)
    earlier = (
        lax.broadcasted_iota(jnp.int32, (tok_rows, tok_rows), 1)
        < lax.broadcasted_iota(jnp.int32, (tok_rows, tok_rows), 0)
    ).astype(F32)
    rank = dot(earlier.astype(BF16), chosen.astype(BF16), (1, 0))
    slot_numbers = lax.broadcasted_iota(jnp.int32, (tok_rows, slots), 1)
    total = None
    for k in range(top_count):
        own = jnp.sum(jnp.where(named[k], rank, 0.0), axis=1, keepdims=True)
        slot = routes[:, k : k + 1] * (slots // experts) + own.astype(jnp.int32)
        mark = (slot_numbers == slot).astype(F32)
        place_ref[k * tok_rows : (k + 1) * tok_rows, :] = mark.astype(BF16)
        total = mark if total is None else total + mark
    total = total.astype(BF16)
    for columns in tiles(width):
        slots_ref[:, columns] = dot(total, tokens_ref[:, columns], (0, 0)).astype(BF16)


def spread_kernel(top_count, place_ref, rows_ref, slots_ref):
    tok_rows = rows_ref.shape[0]
    total = sum(
        place_ref[k * tok_rows : (k + 1) * tok_rows, :].astype(F32) for k in range(top_count)
    ).astype(BF16)
    for columns in tiles(rows_ref.shape[1]):
        slots_ref[:, columns] = dot(total, rows_ref[:, columns], (0, 0)).astype(BF16)


def hidden_kernel(parts, rows_ref, *refs):
    sources, refs = [rows_ref, *refs[: 2 * parts]], refs[2 * parts :]
    hidden_ref, by_gate_ref, by_up_ref, sems, *targets = refs
    copies = fetch(sources, targets, sems)
    rows_ref, weights = targets[0], targets[1:]
    copies[0].wait()
    for i in range(parts):
        copies[1 + 2 * i].wait()
        pre_gate = dot(rows_ref[...], weights[2 * i][...], (1, 0))
        copies[2 + 2 * i].wait()
        pre_up = dot(rows_ref[...], weights[2 * i + 1][...], (1, 0))
        sig = jax.nn.sigmoid(pre_gate)
        act = pre_gate * sig
        hidden_ref[i] = (act * pre_up).astype(BF16)
        by_gate_ref[i] = pre_up * sig * (1.0 + pre_gate * (1.0 - sig))
        by_up_ref[i] = act


def out_kernel(parts, hidden_ref, *refs):
    sources, refs = refs[:parts], refs[parts:]
    out_ref, sems, out_sems, stage_ref, *weights = refs
    copies = fetch(sources, weights, sems)
    for copy in copies:
        copy.wait()
    sent = []
    for d, columns in enumerate(tiles(out_ref.shape[1])):
        stage_ref[:, columns] = sum(
            dot(hidden_ref[i], weights[i][:, columns], (1, 0)) for i in range(parts)
        ).astype(BF16)
        sent.append(store(columns, d, stage_ref, out_ref, out_sems))
    for copy in sent:
        copy.wait()


def backward_kernel(parts, by_gate_ref, by_up_ref, rows_ref, *refs):
    sources, refs = [rows_ref, *refs[: 3 * parts]], refs[3 * parts :]
    out_ref, sems, out_sems, back_gate_ref, back_up_ref, stage_ref, *targets = refs
    copies = fetch(sources, targets, sems)
    rows_ref, down, gate, up = targets[0], *(targets[1 + i * parts : 1 + (i + 1) * parts] for i in range(3))
    copies[0].wait()
    for i in range(parts):
        copies[1 + i].wait()
        back_hidden = dot(rows_ref[...], down[i][...], (1, 1))
        back_gate_ref[i] = (back_hidden * by_gate_ref[i]).astype(BF16)
        back_up_ref[i] = (back_hidden * by_up_ref[i]).astype(BF16)
    for copy in copies[1 + parts :]:
        copy.wait()
    sent = []
    for d, columns in enumerate(tiles(out_ref.shape[1])):
        stage_ref[:, columns] = sum(
            dot(back_gate_ref[i], gate[i][columns, :], (1, 1))
            + dot(back_up_ref[i], up[i][columns, :], (1, 1))
            for i in range(parts)
        ).astype(BF16)
        sent.append(store(columns, d, stage_ref, out_ref, out_sems))
    for copy in sent:
        copy.wait()


def mix_kernel(place_ref, gates_ref, cotangent_ref, slots_ref, mixed_ref, gate_grad_ref):
    tok_rows, top_count = gates_ref.shape
    total, grads = None, []
    for k in range(top_count):
        raw = dot(place_ref[k * tok_rows : (k + 1) * tok_rows, :], slots_ref[...], (1, 0))
        grads.append(jnp.sum(raw * cotangent_ref[...].astype(F32), axis=1, keepdims=True))
        term = raw * gates_ref[:, k : k + 1]
        total = term if total is None else total + term
    mixed_ref[...] = total.astype(BF16)
    gate_grad_ref[...] = jnp.concatenate(grads, axis=1)


def sum_kernel(place_ref, gates_ref, slots_ref, out_ref):
    tok_rows, top_count = gates_ref.shape
    total = None
    for k in range(top_count):
        raw = dot(place_ref[k * tok_rows : (k + 1) * tok_rows, :], slots_ref[...], (1, 0))
        term = raw * gates_ref[:, k : k + 1]
        total = term if total is None else total + term
    out_ref[...] = total.astype(BF16)


def call(kernel, outs, flops, scratch=(), far=(), far_out=False):
    def run(*args):
        moved = sum(a.size * a.dtype.itemsize for a in (*args, *outs))
        spaces = [pl.ANY if i in far else pltpu.VMEM for i in range(len(args))]
        return pl.pallas_call(
            kernel,
            out_shape=tuple(outs),
            in_specs=[pl.BlockSpec(memory_space=space) for space in spaces],
            out_specs=tuple(
                pl.BlockSpec(memory_space=pl.ANY if far_out else pltpu.VMEM) for _ in outs
            ),
            scratch_shapes=scratch,
            compiler_params=pltpu.CompilerParams(vmem_limit_bytes=VMEM_BYTES),
            cost_estimate=pl.CostEstimate(flops=flops, bytes_accessed=moved, transcendentals=0),
        )(*args)

    return run


def body(tokens, cotangent, routes, gates, w_gate, w_up, w_down):
    tok_rows, width = tokens.shape
    top_count = routes.shape[1]
    parts, experts = lax.axis_size("dp"), lax.axis_size("expert")
    hidden = w_gate.shape[2]
    capacity = max(2, 3 * tok_rows * top_count // (2 * experts))
    slots = experts * capacity
    axes = ("dp", "expert")

    def device(g, j):
        return g * experts + j

    def home(e, c):
        return device((e + 1) % parts, e // parts * parts + c)

    swap = [(device(g, e), home(e, g)) for g in range(parts) for e in range(experts)]
    groups = [[home(e, c) for e in range(experts)] for c in range(parts)]

    def whole_expert(weight):
        own = lax.ppermute(weight[0], axes, swap)
        shares = [own]
        for step in range(1, parts):
            turn = [(j, j // parts * parts + (j + step) % parts) for j in range(experts)]
            shares.append(lax.ppermute(own, "expert", turn))
        return shares

    def exchange(rows):
        return lax.all_to_all(
            rows.reshape(experts, capacity, width), axes, 0, 0, axis_index_groups=groups, tiled=True
        ).reshape(slots, width)

    spread_flops = 2 * slots * tok_rows * width
    dot_flops = 2 * slots * width * hidden * parts
    slot_shape = jax.ShapeDtypeStruct((slots, width), BF16)
    place_shape = jax.ShapeDtypeStruct((top_count * tok_rows, slots), BF16)
    unit_shape = jax.ShapeDtypeStruct((parts, slots, hidden), F32)
    hidden_shape = jax.ShapeDtypeStruct((parts, slots, hidden), BF16)
    token_shape = jax.ShapeDtypeStruct((tok_rows, width), BF16)
    hidden_scratch = pltpu.VMEM((parts, slots, hidden), BF16)
    row_scratch = pltpu.VMEM((slots, width), BF16)
    in_scratch = pltpu.VMEM((width, hidden), BF16)
    down_scratch = pltpu.VMEM((hidden, width), BF16)
    out_sems = pltpu.SemaphoreType.DMA((len(tiles(width)),))

    gate_w, up_w, down_w = whole_expert(w_gate), whole_expert(w_up), whole_expert(w_down)
    x_slots, place = call(
        functools.partial(place_kernel, experts), [slot_shape, place_shape], spread_flops
    )(routes, tokens)
    x_rows = exchange(x_slots)
    (dy_slots,) = call(
        functools.partial(spread_kernel, top_count), [slot_shape], spread_flops
    )(place, cotangent)
    dy_rows = exchange(dy_slots)
    hidden_rows, by_gate, by_up = call(
        functools.partial(hidden_kernel, parts),
        [hidden_shape, unit_shape, unit_shape],
        2 * dot_flops,
        [pltpu.SemaphoreType.DMA((1 + 2 * parts,)), row_scratch] + [in_scratch] * (2 * parts),
        far=range(1 + 2 * parts),
    )(x_rows, *(w for pair in zip(gate_w, up_w) for w in pair))
    (out_rows,) = call(
        functools.partial(out_kernel, parts),
        [slot_shape],
        dot_flops,
        [pltpu.SemaphoreType.DMA((parts,)), out_sems, row_scratch] + [down_scratch] * parts,
        far=range(1, 1 + parts),
        far_out=True,
    )(hidden_rows, *down_w)
    out_slots = exchange(out_rows)
    (grad_rows,) = call(
        functools.partial(backward_kernel, parts),
        [slot_shape],
        3 * dot_flops,
        [pltpu.SemaphoreType.DMA((1 + 3 * parts,)), out_sems, hidden_scratch, hidden_scratch]
        + [row_scratch] * 2
        + [down_scratch] * parts
        + [in_scratch] * (2 * parts),
        far=range(2, 3 + 3 * parts),
        far_out=True,
    )(by_gate, by_up, dy_rows, *down_w, *gate_w, *up_w)
    grad_slots = exchange(grad_rows)
    mixed, gate_grad = call(
        mix_kernel, [token_shape, jax.ShapeDtypeStruct(gates.shape, F32)], 2 * spread_flops
    )(place, gates, cotangent, out_slots)
    (token_grad,) = call(sum_kernel, [token_shape], 2 * spread_flops)(place, gates, grad_slots)
    return (mixed, token_grad, gate_grad)


def solution(mesh):
    rows, weights = P(("dp", "expert"), None), P("expert", None, "dp")
    return jax.shard_map(
        body,
        mesh=mesh,
        in_specs=(rows, rows, rows, rows, weights, weights, P("expert", "dp", None)),
        out_specs=(rows, rows, rows),
        check_vma=False,
    )
```

```python
import functools

import jax
import jax.numpy as jnp
from jax import lax
from jax.experimental import pallas as pl
from jax.experimental.pallas import tpu as pltpu
from jax.sharding import PartitionSpec as P

BF16 = jnp.bfloat16
F32 = jnp.float32
VMEM_BYTES = 40 << 20


def dot(a, b, dims):
    return lax.dot_general(a, b, ((dims[:1], dims[1:]), ((), ())), preferred_element_type=F32)


def tiles(width):
    tile = min(512, width)
    return [slice(d, d + tile) for d in range(0, width, tile)]


def fetch(sources, targets, sems):
    copies = [pltpu.make_async_copy(s, t, sems.at[i]) for i, (s, t) in enumerate(zip(sources, targets))]
    for copy in copies:
        copy.start()
    return copies


def store(stage_ref, out_ref, sem):
    copy = pltpu.make_async_copy(stage_ref, out_ref, sem)
    copy.start()
    return copy


def place_kernel(experts, routes_ref, tokens_ref, slots_ref, place_ref):
    slots, width = slots_ref.shape
    tok_rows, top_count = routes_ref.shape
    routes = routes_ref[...]
    numbers = lax.broadcasted_iota(jnp.int32, (tok_rows, experts), 1)
    named = [numbers == routes[:, k : k + 1] for k in range(top_count)]
    chosen = sum(n.astype(F32) for n in named)
    earlier = (
        lax.broadcasted_iota(jnp.int32, (tok_rows, tok_rows), 1)
        < lax.broadcasted_iota(jnp.int32, (tok_rows, tok_rows), 0)
    ).astype(F32)
    rank = dot(earlier.astype(BF16), chosen.astype(BF16), (1, 0))
    slot_numbers = lax.broadcasted_iota(jnp.int32, (tok_rows, slots), 1)
    total = None
    for k in range(top_count):
        own = jnp.sum(jnp.where(named[k], rank, 0.0), axis=1, keepdims=True)
        slot = routes[:, k : k + 1] * (slots // experts) + own.astype(jnp.int32)
        mark = (slot_numbers == slot).astype(F32)
        place_ref[k * tok_rows : (k + 1) * tok_rows, :] = mark.astype(BF16)
        total = mark if total is None else total + mark
    total = total.astype(BF16)
    for columns in tiles(width):
        slots_ref[:, columns] = dot(total, tokens_ref[:, columns], (0, 0)).astype(BF16)


def spread_kernel(top_count, place_ref, rows_ref, _, slots_ref):
    tok_rows = rows_ref.shape[0]
    total = sum(
        place_ref[k * tok_rows : (k + 1) * tok_rows, :].astype(F32) for k in range(top_count)
    ).astype(BF16)
    for columns in tiles(rows_ref.shape[1]):
        slots_ref[:, columns] = dot(total, rows_ref[:, columns], (0, 0)).astype(BF16)


def forward_kernel(parts, *refs):
    sources, refs = refs[: 1 + 3 * parts], refs[1 + 3 * parts :]
    out_ref, by_gate_ref, by_up_ref, sems, out_sems = refs[:5]
    stage_ref, by_gate_stage, by_up_stage, hidden_ref, *targets = refs[5:]
    copies = fetch(sources, targets, sems)
    rows_ref, weights = targets[0], targets[1:]
    sent = []
    copies[0].wait()
    for i in range(parts):
        copies[1 + 2 * i].wait()
        pre_gate = dot(rows_ref[...], weights[2 * i][...], (1, 0))
        copies[2 + 2 * i].wait()
        pre_up = dot(rows_ref[...], weights[2 * i + 1][...], (1, 0))
        sig = jax.nn.sigmoid(pre_gate)
        act = pre_gate * sig
        hidden_ref[i] = (act * pre_up).astype(BF16)
        by_gate_stage[i] = pre_up * sig * (1.0 + pre_gate * (1.0 - sig))
        by_up_stage[i] = act
    sent.append(store(by_gate_stage, by_gate_ref, out_sems.at[0]))
    sent.append(store(by_up_stage, by_up_ref, out_sems.at[1]))
    for copy in copies[1 + 2 * parts :]:
        copy.wait()
    down = weights[2 * parts :]
    for columns in tiles(out_ref.shape[1]):
        stage_ref[:, columns] = sum(
            dot(hidden_ref[i], down[i][:, columns], (1, 0)) for i in range(parts)
        ).astype(BF16)
        sem = out_sems.at[len(sent)]
        sent.append(store(stage_ref.at[:, columns], out_ref.at[:, columns], sem))
    for copy in sent:
        copy.wait()


def backward_kernel(parts, *refs):
    sources, refs = refs[: 3 + 3 * parts], refs[3 + 3 * parts :]
    out_ref, sems, out_sems, back_gate_ref, back_up_ref, stage_ref, *targets = refs
    copies = fetch(sources, targets, sems)
    rows_ref, targets = targets[0], targets[1:]
    down, (by_gate_ref, by_up_ref) = targets[:parts], targets[parts : parts + 2]
    gate, up = targets[parts + 2 : 2 * parts + 2], targets[2 * parts + 2 :]
    for copy in copies[: 3 + parts]:
        copy.wait()
    for i in range(parts):
        back_hidden = dot(rows_ref[...], down[i][...], (1, 1))
        back_gate_ref[i] = (back_hidden * by_gate_ref[i]).astype(BF16)
        back_up_ref[i] = (back_hidden * by_up_ref[i]).astype(BF16)
    for copy in copies[3 + parts :]:
        copy.wait()
    sent = []
    for columns in tiles(out_ref.shape[1]):
        stage_ref[:, columns] = sum(
            dot(back_gate_ref[i], gate[i][columns, :], (1, 1))
            + dot(back_up_ref[i], up[i][columns, :], (1, 1))
            for i in range(parts)
        ).astype(BF16)
        sem = out_sems.at[len(sent)]
        sent.append(store(stage_ref.at[:, columns], out_ref.at[:, columns], sem))
    for copy in sent:
        copy.wait()


def mix_kernel(place_ref, gates_ref, cotangent_ref, slots_ref, mixed_ref, gate_grad_ref):
    tok_rows, top_count = gates_ref.shape
    total, grads = None, []
    for k in range(top_count):
        raw = dot(place_ref[k * tok_rows : (k + 1) * tok_rows, :], slots_ref[...], (1, 0))
        grads.append(jnp.sum(raw * cotangent_ref[...].astype(F32), axis=1, keepdims=True))
        term = raw * gates_ref[:, k : k + 1]
        total = term if total is None else total + term
    mixed_ref[...] = total.astype(BF16)
    gate_grad_ref[...] = jnp.concatenate(grads, axis=1)


def sum_kernel(place_ref, gates_ref, slots_ref, out_ref):
    tok_rows, top_count = gates_ref.shape
    total = None
    for k in range(top_count):
        raw = dot(place_ref[k * tok_rows : (k + 1) * tok_rows, :], slots_ref[...], (1, 0))
        term = raw * gates_ref[:, k : k + 1]
        total = term if total is None else total + term
    out_ref[...] = total.astype(BF16)


def call(kernel, outs, flops, scratch=(), far=(), far_out=False):
    def run(*args):
        moved = sum(a.size * a.dtype.itemsize for a in (*args, *outs))
        spaces = [pltpu.HBM if i in far else pltpu.VMEM for i in range(len(args))]
        return pl.pallas_call(
            kernel,
            out_shape=tuple(outs),
            in_specs=[pl.BlockSpec(memory_space=space) for space in spaces],
            out_specs=tuple(
                pl.BlockSpec(memory_space=pltpu.HBM if far_out else pltpu.VMEM) for _ in outs
            ),
            scratch_shapes=scratch,
            compiler_params=pltpu.CompilerParams(vmem_limit_bytes=VMEM_BYTES),
            cost_estimate=pl.CostEstimate(flops=flops, bytes_accessed=moved, transcendentals=0),
        )(*args)

    return run


def body(tokens, cotangent, routes, gates, w_gate, w_up, w_down):
    tok_rows, width = tokens.shape
    top_count = routes.shape[1]
    parts, experts = lax.axis_size("dp"), lax.axis_size("expert")
    hidden = w_gate.shape[2]
    capacity = max(2, 3 * tok_rows * top_count // (2 * experts))
    slots = experts * capacity
    axes = ("dp", "expert")

    def device(g, j):
        return g * experts + j

    def home(e, c):
        return device((e + 1) % parts, e // parts * parts + c)

    swap = [(device(g, e), home(e, g)) for g in range(parts) for e in range(experts)]
    groups = [[home(e, c) for e in range(experts)] for c in range(parts)]

    def whole_expert(weight):
        own = lax.ppermute(weight[0], axes, swap)
        shares = [own]
        for step in range(1, parts):
            turn = [(j, j // parts * parts + (j + step) % parts) for j in range(experts)]
            shares.append(lax.ppermute(own, "expert", turn))
        return shares

    def exchange(rows):
        return lax.all_to_all(
            rows.reshape(experts, capacity, width), axes, 0, 0, axis_index_groups=groups, tiled=True
        ).reshape(slots, width)

    spread_flops = 2 * slots * tok_rows * width
    dot_flops = 2 * slots * width * hidden * parts
    slot_shape = jax.ShapeDtypeStruct((slots, width), BF16)
    place_shape = jax.ShapeDtypeStruct((top_count * tok_rows, slots), BF16)
    unit_shape = jax.ShapeDtypeStruct((parts, slots, hidden), F32)
    token_shape = jax.ShapeDtypeStruct((tok_rows, width), BF16)
    hidden_scratch = pltpu.VMEM((parts, slots, hidden), BF16)
    row_scratch = pltpu.VMEM((slots, width), BF16)
    in_scratch = pltpu.VMEM((width, hidden), BF16)
    down_scratch = pltpu.VMEM((hidden, width), BF16)
    unit_stage = pltpu.VMEM((parts, slots, hidden), F32)

    def sems(number):
        return pltpu.SemaphoreType.DMA((number,))

    gate_w, up_w, down_w = whole_expert(w_gate), whole_expert(w_up), whole_expert(w_down)
    x_slots, place = call(
        functools.partial(place_kernel, experts), [slot_shape, place_shape], spread_flops
    )(routes, tokens)
    x_rows = exchange(x_slots)
    (dy_slots,) = call(
        functools.partial(spread_kernel, top_count), [slot_shape], spread_flops, far=(2,)
    )(place, cotangent, gate_w[0])
    dy_rows = exchange(dy_slots)
    out_rows, by_gate, by_up = call(
        functools.partial(forward_kernel, parts),
        [slot_shape, unit_shape, unit_shape],
        3 * dot_flops,
        [sems(1 + 3 * parts), sems(2 + len(tiles(width))), row_scratch, unit_stage, unit_stage]
        + [hidden_scratch, row_scratch]
        + [in_scratch] * (2 * parts)
        + [down_scratch] * parts,
        far=range(1 + 3 * parts),
        far_out=True,
    )(x_rows, *(w for pair in zip(gate_w, up_w) for w in pair), *down_w)
    out_slots = exchange(out_rows)
    (grad_rows,) = call(
        functools.partial(backward_kernel, parts),
        [slot_shape],
        3 * dot_flops,
        [sems(3 + 3 * parts), sems(len(tiles(width))), hidden_scratch, hidden_scratch]
        + [row_scratch] * 2
        + [down_scratch] * parts
        + [unit_stage] * 2
        + [in_scratch] * (2 * parts),
        far=range(3 + 3 * parts),
        far_out=True,
    )(dy_rows, *down_w, by_gate, by_up, *gate_w, *up_w)
    grad_slots = exchange(grad_rows)
    mixed, gate_grad = call(
        mix_kernel, [token_shape, jax.ShapeDtypeStruct(gates.shape, F32)], 2 * spread_flops
    )(place, gates, cotangent, out_slots)
    (token_grad,) = call(sum_kernel, [token_shape], 2 * spread_flops)(place, gates, grad_slots)
    return (mixed, token_grad, gate_grad)


def solution(mesh):
    rows, weights = P(("dp", "expert"), None), P("expert", None, "dp")
    return jax.shard_map(
        body,
        mesh=mesh,
        in_specs=(rows, rows, rows, rows, weights, weights, P("expert", "dp", None)),
        out_specs=(rows, rows, rows),
        check_vma=False,
    )
```

```python
import functools

import jax
import jax.numpy as jnp
from jax import lax
from jax.experimental import pallas as pl
from jax.experimental.pallas import tpu as pltpu
from jax.sharding import PartitionSpec as P

BF16 = jnp.bfloat16
F32 = jnp.float32
VMEM_BYTES = 60 << 20


def dot(a, b, dims):
    return lax.dot_general(a, b, ((dims[:1], dims[1:]), ((), ())), preferred_element_type=F32)


def tiles(width):
    tile = min(512, width)
    return [slice(d, d + tile) for d in range(0, width, tile)]


def fetch(sources, targets, sems):
    copies = [pltpu.make_async_copy(s, t, sems.at[i]) for i, (s, t) in enumerate(zip(sources, targets))]
    for copy in copies:
        copy.start()
    return copies


def store(stage_ref, out_ref, sem):
    copy = pltpu.make_async_copy(stage_ref, out_ref, sem)
    copy.start()
    return copy


def place_kernel(experts, routes_ref, tokens_ref, slots_ref, place_ref):
    slots, width = slots_ref.shape
    tok_rows, top_count = routes_ref.shape
    routes = routes_ref[...]
    numbers = lax.broadcasted_iota(jnp.int32, (tok_rows, experts), 1)
    named = [numbers == routes[:, k : k + 1] for k in range(top_count)]
    chosen = sum(n.astype(F32) for n in named)
    earlier = (
        lax.broadcasted_iota(jnp.int32, (tok_rows, tok_rows), 1)
        < lax.broadcasted_iota(jnp.int32, (tok_rows, tok_rows), 0)
    ).astype(F32)
    rank = dot(earlier.astype(BF16), chosen.astype(BF16), (1, 0))
    slot_numbers = lax.broadcasted_iota(jnp.int32, (tok_rows, slots), 1)
    total = None
    for k in range(top_count):
        own = jnp.sum(jnp.where(named[k], rank, 0.0), axis=1, keepdims=True)
        slot = routes[:, k : k + 1] * (slots // experts) + own.astype(jnp.int32)
        mark = (slot_numbers == slot).astype(F32)
        place_ref[k * tok_rows : (k + 1) * tok_rows, :] = mark.astype(BF16)
        total = mark if total is None else total + mark
    total = total.astype(BF16)
    for columns in tiles(width):
        slots_ref[:, columns] = dot(total, tokens_ref[:, columns], (0, 0)).astype(BF16)


def spread_kernel(top_count, place_ref, rows_ref, _, slots_ref):
    tok_rows = rows_ref.shape[0]
    total = sum(
        place_ref[k * tok_rows : (k + 1) * tok_rows, :].astype(F32) for k in range(top_count)
    ).astype(BF16)
    for columns in tiles(rows_ref.shape[1]):
        slots_ref[:, columns] = dot(total, rows_ref[:, columns], (0, 0)).astype(BF16)


def forward_kernel(parts, *refs):
    sources, refs = refs[: 1 + 3 * parts], refs[1 + 3 * parts :]
    out_ref, by_gate_ref, by_up_ref, sems, out_sems = refs[:5]
    stage_ref, by_gate_stage, by_up_stage, hidden_ref, *targets = refs[5:]
    copies = fetch(sources, targets, sems)
    rows_ref, weights = targets[0], targets[1:]
    sent = []
    copies[0].wait()
    for i in range(parts):
        copies[1 + 2 * i].wait()
        pre_gate = dot(rows_ref[...], weights[2 * i][...], (1, 0))
        copies[2 + 2 * i].wait()
        pre_up = dot(rows_ref[...], weights[2 * i + 1][...], (1, 0))
        sig = jax.nn.sigmoid(pre_gate)
        act = pre_gate * sig
        hidden_ref[i] = (act * pre_up).astype(BF16)
        by_gate_stage[i] = pre_up * sig * (1.0 + pre_gate * (1.0 - sig))
        by_up_stage[i] = act
    sent.append(store(by_gate_stage, by_gate_ref, out_sems.at[0]))
    sent.append(store(by_up_stage, by_up_ref, out_sems.at[1]))
    for copy in copies[1 + 2 * parts :]:
        copy.wait()
    down = weights[2 * parts :]
    for columns in tiles(out_ref.shape[1]):
        stage_ref[:, columns] = sum(
            dot(hidden_ref[i], down[i][:, columns], (1, 0)) for i in range(parts)
        ).astype(BF16)
        sem = out_sems.at[len(sent)]
        sent.append(store(stage_ref.at[:, columns], out_ref.at[:, columns], sem))
    for copy in sent:
        copy.wait()


def backward_kernel(parts, *refs):
    sources, refs = refs[: 3 + 3 * parts], refs[3 + 3 * parts :]
    out_ref, sems, out_sems, back_gate_ref, back_up_ref, stage_ref, *targets = refs
    copies = fetch(sources, targets, sems)
    rows_ref, targets = targets[0], targets[1:]
    down, (by_gate_ref, by_up_ref) = targets[:parts], targets[parts : parts + 2]
    gate, up = targets[parts + 2 : 2 * parts + 2], targets[2 * parts + 2 :]
    for copy in copies[: 3 + parts]:
        copy.wait()
    for i in range(parts):
        back_hidden = dot(rows_ref[...], down[i][...], (1, 1))
        back_gate_ref[i] = (back_hidden * by_gate_ref[i]).astype(BF16)
        back_up_ref[i] = (back_hidden * by_up_ref[i]).astype(BF16)
    for copy in copies[3 + parts :]:
        copy.wait()
    sent = []
    for columns in tiles(out_ref.shape[1]):
        stage_ref[:, columns] = sum(
            dot(back_gate_ref[i], gate[i][columns, :], (1, 1))
            + dot(back_up_ref[i], up[i][columns, :], (1, 1))
            for i in range(parts)
        ).astype(BF16)
        sem = out_sems.at[len(sent)]
        sent.append(store(stage_ref.at[:, columns], out_ref.at[:, columns], sem))
    for copy in sent:
        copy.wait()


def mix_kernel(place_ref, gates_ref, cotangent_ref, slots_ref, mixed_ref, gate_grad_ref):
    tok_rows, top_count = gates_ref.shape
    total, grads = None, []
    for k in range(top_count):
        raw = dot(place_ref[k * tok_rows : (k + 1) * tok_rows, :], slots_ref[...], (1, 0))
        grads.append(jnp.sum(raw * cotangent_ref[...].astype(F32), axis=1, keepdims=True))
        term = raw * gates_ref[:, k : k + 1]
        total = term if total is None else total + term
    mixed_ref[...] = total.astype(BF16)
    gate_grad_ref[...] = jnp.concatenate(grads, axis=1)


def sum_kernel(place_ref, gates_ref, slots_ref, out_ref):
    tok_rows, top_count = gates_ref.shape
    total = None
    for k in range(top_count):
        raw = dot(place_ref[k * tok_rows : (k + 1) * tok_rows, :], slots_ref[...], (1, 0))
        term = raw * gates_ref[:, k : k + 1]
        total = term if total is None else total + term
    out_ref[...] = total.astype(BF16)


def call(kernel, outs, flops, scratch=(), far=(), far_out=False):
    def run(*args):
        moved = sum(a.size * a.dtype.itemsize for a in (*args, *outs))
        spaces = [pltpu.HBM if i in far else pltpu.VMEM for i in range(len(args))]
        return pl.pallas_call(
            kernel,
            out_shape=tuple(outs),
            in_specs=[pl.BlockSpec(memory_space=space) for space in spaces],
            out_specs=tuple(
                pl.BlockSpec(memory_space=pltpu.HBM if far_out else pltpu.VMEM) for _ in outs
            ),
            scratch_shapes=scratch,
            compiler_params=pltpu.CompilerParams(vmem_limit_bytes=VMEM_BYTES),
            cost_estimate=pl.CostEstimate(flops=flops, bytes_accessed=moved, transcendentals=0),
        )(*args)

    return run


def body(tokens, cotangent, routes, gates, w_gate, w_up, w_down):
    tok_rows, width = tokens.shape
    top_count = routes.shape[1]
    parts, experts = lax.axis_size("dp"), lax.axis_size("expert")
    hidden = w_gate.shape[2]
    capacity = max(2, 3 * tok_rows * top_count // (2 * experts))
    slots = experts * capacity
    axes = ("dp", "expert")

    def device(g, j):
        return g * experts + j

    def home(e, c):
        return device((e + 1) % parts, e // parts * parts + c)

    swap = [(device(g, e), home(e, g)) for g in range(parts) for e in range(experts)]
    groups = [[home(e, c) for e in range(experts)] for c in range(parts)]

    def whole_expert(weight):
        own = lax.ppermute(weight[0], axes, swap)
        shares = [own]
        for step in range(1, parts):
            turn = [(j, j // parts * parts + (j + step) % parts) for j in range(experts)]
            shares.append(lax.ppermute(own, "expert", turn))
        return shares

    def exchange(rows):
        return lax.all_to_all(
            rows.reshape(experts, capacity, width), axes, 0, 0, axis_index_groups=groups, tiled=True
        ).reshape(slots, width)

    spread_flops = 2 * slots * tok_rows * width
    dot_flops = 2 * slots * width * hidden * parts
    slot_shape = jax.ShapeDtypeStruct((slots, width), BF16)
    place_shape = jax.ShapeDtypeStruct((top_count * tok_rows, slots), BF16)
    unit_shape = jax.ShapeDtypeStruct((parts, slots, hidden), F32)
    token_shape = jax.ShapeDtypeStruct((tok_rows, width), BF16)
    hidden_scratch = pltpu.VMEM((parts, slots, hidden), BF16)
    row_scratch = pltpu.VMEM((slots, width), BF16)
    in_scratch = pltpu.VMEM((width, hidden), BF16)
    down_scratch = pltpu.VMEM((hidden, width), BF16)
    unit_stage = pltpu.VMEM((parts, slots, hidden), F32)

    def sems(number):
        return pltpu.SemaphoreType.DMA((number,))

    gate_w, up_w, down_w = whole_expert(w_gate), whole_expert(w_up), whole_expert(w_down)
    x_slots, place = call(
        functools.partial(place_kernel, experts), [slot_shape, place_shape], spread_flops
    )(routes, tokens)
    x_rows = exchange(x_slots)
    (dy_slots,) = call(
        functools.partial(spread_kernel, top_count), [slot_shape], 256 * spread_flops, far=(2,)
    )(place, cotangent, gate_w[0])
    dy_rows = exchange(dy_slots)
    out_rows, by_gate, by_up = call(
        functools.partial(forward_kernel, parts),
        [slot_shape, unit_shape, unit_shape],
        3 * dot_flops,
        [sems(1 + 3 * parts), sems(2 + len(tiles(width))), row_scratch, unit_stage, unit_stage]
        + [hidden_scratch, row_scratch]
        + [in_scratch] * (2 * parts)
        + [down_scratch] * parts,
        far=range(1 + 3 * parts),
        far_out=True,
    )(x_rows, *(w for pair in zip(gate_w, up_w) for w in pair), *down_w)
    out_slots = exchange(out_rows)
    (grad_rows,) = call(
        functools.partial(backward_kernel, parts),
        [slot_shape],
        3 * dot_flops,
        [sems(3 + 3 * parts), sems(len(tiles(width))), hidden_scratch, hidden_scratch]
        + [row_scratch] * 2
        + [down_scratch] * parts
        + [unit_stage] * 2
        + [in_scratch] * (2 * parts),
        far=range(3 + 3 * parts),
        far_out=True,
    )(dy_rows, *down_w, by_gate, by_up, *gate_w, *up_w)
    grad_slots = exchange(grad_rows)
    mixed, gate_grad = call(
        mix_kernel, [token_shape, jax.ShapeDtypeStruct(gates.shape, F32)], 2 * spread_flops
    )(place, gates, cotangent, out_slots)
    (token_grad,) = call(sum_kernel, [token_shape], 2 * spread_flops)(place, gates, grad_slots)
    return (mixed, token_grad, gate_grad)


def solution(mesh):
    rows, weights = P(("dp", "expert"), None), P("expert", None, "dp")
    return jax.shard_map(
        body,
        mesh=mesh,
        in_specs=(rows, rows, rows, rows, weights, weights, P("expert", "dp", None)),
        out_specs=(rows, rows, rows),
        check_vma=False,
    )
```

```python
import functools

import jax
import jax.numpy as jnp
from jax import lax
from jax.experimental import pallas as pl
from jax.experimental.pallas import tpu as pltpu
from jax.sharding import PartitionSpec as P

BF16 = jnp.bfloat16
F32 = jnp.float32
VMEM_BYTES = 28 << 20


def dot(a, b, dims):
    return lax.dot_general(a, b, ((dims[:1], dims[1:]), ((), ())), preferred_element_type=F32)


def tiles(width):
    tile = min(512, width)
    return [slice(d, d + tile) for d in range(0, width, tile)]


def fetch(sources, targets, sems):
    copies = [pltpu.make_async_copy(s, t, sems.at[i]) for i, (s, t) in enumerate(zip(sources, targets))]
    for copy in copies:
        copy.start()
    return copies


def store(stage_ref, out_ref, sem):
    copy = pltpu.make_async_copy(stage_ref, out_ref, sem)
    copy.start()
    return copy


def place_kernel(experts, parts, plane_ref, routes_ref, tokens_ref, slots_ref, place_ref, near_ref):
    slots, width = slots_ref.shape
    capacity = slots // experts
    tok_rows, top_count = routes_ref.shape
    routes = routes_ref[...]
    home_plane, home_set = lax.rem(routes + 1, parts), lax.div(routes, parts)
    lanes = home_plane * (experts // parts) + home_set
    near_lanes = home_set * parts + lax.rem(home_plane + (parts - plane_ref[0]), parts)
    numbers = lax.broadcasted_iota(jnp.int32, (tok_rows, experts), 1)
    named = [numbers == routes[:, k : k + 1] for k in range(top_count)]
    chosen = sum(n.astype(F32) for n in named)
    earlier = (
        lax.broadcasted_iota(jnp.int32, (tok_rows, tok_rows), 1)
        < lax.broadcasted_iota(jnp.int32, (tok_rows, tok_rows), 0)
    ).astype(F32)
    rank = dot(earlier.astype(BF16), chosen.astype(BF16), (1, 0))
    slot_numbers = lax.broadcasted_iota(jnp.int32, (tok_rows, slots), 1)
    total, near = None, None
    for k in range(top_count):
        own = jnp.sum(jnp.where(named[k], rank, 0.0), axis=1, keepdims=True).astype(jnp.int32)
        mark, near_mark = (
            (slot_numbers == order[:, k : k + 1] * capacity + own).astype(F32)
            for order in (lanes, near_lanes)
        )
        place_ref[k * tok_rows : (k + 1) * tok_rows, :] = mark.astype(BF16)
        total = mark if total is None else total + mark
        near = near_mark if near is None else near + near_mark
    near_ref[...] = near.astype(BF16)
    total = total.astype(BF16)
    for columns in tiles(width):
        slots_ref[:, columns] = dot(total, tokens_ref[:, columns], (0, 0)).astype(BF16)


def spread_kernel(near_ref, rows_ref, _, slots_ref):
    for columns in tiles(rows_ref.shape[1]):
        slots_ref[:, columns] = dot(near_ref[...], rows_ref[:, columns], (0, 0)).astype(BF16)


def forward_kernel(parts, rows_ref, *refs):
    sources, refs = refs[: 3 * parts], refs[3 * parts :]
    out_ref, by_gate_ref, by_up_ref, sems, out_sems = refs[:5]
    stage_ref, by_gate_stage, by_up_stage, hidden_ref, *weights = refs[5:]
    copies = fetch(sources, weights, sems)
    sent = []
    for i in range(parts):
        copies[2 * i].wait()
        pre_gate = dot(rows_ref[...], weights[2 * i][...], (1, 0))
        copies[1 + 2 * i].wait()
        pre_up = dot(rows_ref[...], weights[2 * i + 1][...], (1, 0))
        sig = jax.nn.sigmoid(pre_gate)
        act = pre_gate * sig
        hidden_ref[i] = (act * pre_up).astype(BF16)
        by_gate_stage[i] = pre_up * sig * (1.0 + pre_gate * (1.0 - sig))
        by_up_stage[i] = act
    sent.append(store(by_gate_stage, by_gate_ref, out_sems.at[0]))
    sent.append(store(by_up_stage, by_up_ref, out_sems.at[1]))
    for copy in copies[2 * parts :]:
        copy.wait()
    down = weights[2 * parts :]
    for columns in tiles(out_ref.shape[1]):
        stage_ref[:, columns] = sum(
            dot(hidden_ref[i], down[i][:, columns], (1, 0)) for i in range(parts)
        ).astype(BF16)
        sem = out_sems.at[len(sent)]
        sent.append(store(stage_ref.at[:, columns], out_ref.at[:, columns], sem))
    for copy in sent:
        copy.wait()


def backward_kernel(parts, plane_ref, *refs):
    sources, refs = refs[: 2 + 4 * parts], refs[2 + 4 * parts :]
    out_ref, sems, out_sems, back_gate_ref, back_up_ref, stage_ref, rows_ref, *targets = refs
    share = rows_ref.shape[0] // parts
    places = [
        rows_ref.at[pl.ds(pl.multiple_of((plane_ref[0] + parts - i) % parts * share, share), share)]
        for i in range(parts)
    ]
    copies = fetch(sources, [*places, *targets], sems)
    down, (by_gate_ref, by_up_ref) = targets[:parts], targets[parts : parts + 2]
    gate, up = targets[parts + 2 : 2 * parts + 2], targets[2 * parts + 2 :]
    for copy in copies[: 2 + 2 * parts]:
        copy.wait()
    for i in range(parts):
        back_hidden = dot(rows_ref[...], down[i][...], (1, 1))
        back_gate_ref[i] = (back_hidden * by_gate_ref[i]).astype(BF16)
        back_up_ref[i] = (back_hidden * by_up_ref[i]).astype(BF16)
    for copy in copies[2 + 2 * parts :]:
        copy.wait()
    sent = []
    for columns in tiles(out_ref.shape[1]):
        stage_ref[:, columns] = sum(
            dot(back_gate_ref[i], gate[i][columns, :], (1, 1))
            + dot(back_up_ref[i], up[i][columns, :], (1, 1))
            for i in range(parts)
        ).astype(BF16)
        sem = out_sems.at[len(sent)]
        sent.append(store(stage_ref.at[:, columns], out_ref.at[:, columns], sem))
    for copy in sent:
        copy.wait()


def mix_kernel(place_ref, gates_ref, cotangent_ref, slots_ref, mixed_ref, gate_grad_ref):
    tok_rows, top_count = gates_ref.shape
    total, grads = None, []
    for k in range(top_count):
        raw = dot(place_ref[k * tok_rows : (k + 1) * tok_rows, :], slots_ref[...], (1, 0))
        grads.append(jnp.sum(raw * cotangent_ref[...].astype(F32), axis=1, keepdims=True))
        term = raw * gates_ref[:, k : k + 1]
        total = term if total is None else total + term
    mixed_ref[...] = total.astype(BF16)
    gate_grad_ref[...] = jnp.concatenate(grads, axis=1)


def sum_kernel(place_ref, gates_ref, slots_ref, out_ref):
    tok_rows, top_count = gates_ref.shape
    total = None
    for k in range(top_count):
        raw = dot(place_ref[k * tok_rows : (k + 1) * tok_rows, :], slots_ref[...], (1, 0))
        term = raw * gates_ref[:, k : k + 1]
        total = term if total is None else total + term
    out_ref[...] = total.astype(BF16)


def call(kernel, outs, flops, scratch=(), far=(), far_out=False):
    def run(*args):
        moved = sum(a.size * a.dtype.itemsize for a in (*args, *outs))
        spaces = [
            pltpu.SMEM if a.shape == (1,) else pl.ANY if i in far else pltpu.VMEM
            for i, a in enumerate(args)
        ]
        return pl.pallas_call(
            kernel,
            out_shape=tuple(outs),
            in_specs=[pl.BlockSpec(memory_space=space) for space in spaces],
            out_specs=tuple(
                pl.BlockSpec(memory_space=pl.ANY if far_out else pltpu.VMEM) for _ in outs
            ),
            scratch_shapes=scratch,
            compiler_params=pltpu.CompilerParams(vmem_limit_bytes=VMEM_BYTES),
            cost_estimate=pl.CostEstimate(flops=flops, bytes_accessed=moved, transcendentals=0),
        )(*args)

    return run


def body(tokens, cotangent, routes, gates, w_gate, w_up, w_down):
    tok_rows, width = tokens.shape
    top_count = routes.shape[1]
    parts, experts = lax.axis_size("dp"), lax.axis_size("expert")
    hidden = w_gate.shape[2]
    capacity = max(2, 3 * tok_rows * top_count // (2 * experts))
    slots = experts * capacity
    axes = ("dp", "expert")

    def device(g, j):
        return g * experts + j

    sets = experts // parts

    def home(e, c):
        return device((e + 1) % parts, e // parts * parts + c)

    swap = [(device(g, e), home(e, g)) for g in range(parts) for e in range(experts)]
    planes = [
        [[device(g, parts * q + c) for q in range(sets)] for g in range(parts)] for c in range(parts)
    ]
    everywhere = [[d for plane in planes[c] for d in plane] for c in range(parts)]
    in_plane = [plane for c in range(parts) for plane in planes[c]]

    def whole_expert(weight):
        own = lax.ppermute(weight[0], axes, swap)
        shares = [own]
        for step in range(1, parts):
            turn = [(j, j // parts * parts + (j + step) % parts) for j in range(experts)]
            shares.append(lax.ppermute(own, "expert", turn))
        return shares

    def exchange(rows):
        rows = rows.reshape(experts, capacity, width)
        return lax.all_to_all(
            rows, axes, 0, 0, axis_index_groups=everywhere, tiled=True
        ).reshape(slots, width)

    def exchange_late(rows):
        rows = rows.reshape(sets, parts * capacity, width)
        rows = lax.all_to_all(rows, axes, 0, 0, axis_index_groups=in_plane, tiled=True)
        rows = rows.reshape(sets, parts, capacity, width)
        shares = []
        for i in range(parts):
            share = rows[:, i].reshape(sets * capacity, width)
            if i > 0:
                share = lax.ppermute(share, "dp", [(g, (g + i) % parts) for g in range(parts)])
            shares.append(share)
        return shares

    spread_flops = 2 * slots * tok_rows * width
    dot_flops = 2 * slots * width * hidden * parts
    slot_shape = jax.ShapeDtypeStruct((slots, width), BF16)
    place_shape = jax.ShapeDtypeStruct((top_count * tok_rows, slots), BF16)
    unit_shape = jax.ShapeDtypeStruct((parts, slots, hidden), F32)
    token_shape = jax.ShapeDtypeStruct((tok_rows, width), BF16)
    hidden_scratch = pltpu.VMEM((parts, slots, hidden), BF16)
    row_scratch = pltpu.VMEM((slots, width), BF16)
    in_scratch = pltpu.VMEM((width, hidden), BF16)
    down_scratch = pltpu.VMEM((hidden, width), BF16)
    unit_stage = pltpu.VMEM((parts, slots, hidden), F32)

    def sems(number):
        return pltpu.SemaphoreType.DMA((number,))

    gate_w, up_w, down_w = whole_expert(w_gate), whole_expert(w_up), whole_expert(w_down)
    plane = lax.axis_index("dp").astype(jnp.int32).reshape(1)
    x_slots, place, near = call(
        functools.partial(place_kernel, experts, parts),
        [slot_shape, place_shape, jax.ShapeDtypeStruct((tok_rows, slots), BF16)],
        spread_flops,
    )(plane, routes, tokens)
    x_rows = exchange(x_slots)
    (dy_slots,) = call(spread_kernel, [slot_shape], 256 * spread_flops, far=(2,))(
        near, cotangent, gate_w[0]
    )
    dy_shares = exchange_late(dy_slots)
    out_rows, by_gate, by_up = call(
        functools.partial(forward_kernel, parts),
        [slot_shape, unit_shape, unit_shape],
        3 * dot_flops,
        [sems(3 * parts), sems(2 + len(tiles(width))), row_scratch, unit_stage, unit_stage]
        + [hidden_scratch]
        + [in_scratch] * (2 * parts)
        + [down_scratch] * parts,
        far=range(1, 1 + 3 * parts),
        far_out=True,
    )(x_rows, *(w for pair in zip(gate_w, up_w) for w in pair), *down_w)
    out_slots = exchange(out_rows)
    (grad_rows,) = call(
        functools.partial(backward_kernel, parts),
        [slot_shape],
        3 * dot_flops,
        [sems(2 + 4 * parts), sems(len(tiles(width))), hidden_scratch, hidden_scratch]
        + [row_scratch] * 2
        + [down_scratch] * parts
        + [unit_stage] * 2
        + [in_scratch] * (2 * parts),
        far=range(1, 3 + 4 * parts),
        far_out=True,
    )(plane, *dy_shares, *down_w, by_gate, by_up, *gate_w, *up_w)
    grad_slots = exchange(grad_rows)
    mixed, gate_grad = call(
        mix_kernel, [token_shape, jax.ShapeDtypeStruct(gates.shape, F32)], 2 * spread_flops
    )(place, gates, cotangent, out_slots)
    (token_grad,) = call(sum_kernel, [token_shape], 2 * spread_flops)(place, gates, grad_slots)
    return (mixed, token_grad, gate_grad)


def solution(mesh):
    rows, weights = P(("dp", "expert"), None), P("expert", None, "dp")
    return jax.shard_map(
        body,
        mesh=mesh,
        in_specs=(rows, rows, rows, rows, weights, weights, P("expert", "dp", None)),
        out_specs=(rows, rows, rows),
        check_vma=False,
    )
```

```python
import functools

import jax
import jax.numpy as jnp
from jax import lax
from jax.experimental import pallas as pl
from jax.experimental.pallas import tpu as pltpu
from jax.sharding import PartitionSpec as P

BF16 = jnp.bfloat16
F32 = jnp.float32
SMALL_VMEM, LARGE_VMEM = 12 << 20, 60 << 20


def dot(a, b, dims):
    return lax.dot_general(a, b, ((dims[:1], dims[1:]), ((), ())), preferred_element_type=F32)


def tiles(width):
    tile = min(512, width)
    return [slice(d, d + tile) for d in range(0, width, tile)]


def fetch(sources, targets, sems):
    copies = [pltpu.make_async_copy(s, t, sems.at[i]) for i, (s, t) in enumerate(zip(sources, targets))]
    for copy in copies:
        copy.start()
    return copies


def store(stage_ref, out_ref, sem):
    copy = pltpu.make_async_copy(stage_ref, out_ref, sem)
    copy.start()
    return copy


def shares(unit_ref, parts, joined, axis=1):
    if not joined:
        return [unit_ref.at[i] for i in range(parts)]
    size = unit_ref.shape[1 + axis] // parts
    cuts = [pl.ds(i * size, size) for i in range(parts)]
    return [unit_ref.at[0, cut] if axis == 0 else unit_ref.at[0, :, cut] for cut in cuts]


def place_kernel(experts, parts, plane_ref, routes_ref, tokens_ref, slots_ref, place_ref, near_ref):
    slots, width = slots_ref.shape
    capacity = slots // experts
    tok_rows, top_count = routes_ref.shape
    routes = routes_ref[...]
    home_plane, home_set = lax.rem(routes + 1, parts), lax.div(routes, parts)
    lanes = home_plane * (experts // parts) + home_set
    near_lanes = home_set * parts + lax.rem(home_plane + (parts - plane_ref[0]), parts)
    numbers = lax.broadcasted_iota(jnp.int32, (tok_rows, experts), 1)
    named = [numbers == routes[:, k : k + 1] for k in range(top_count)]
    chosen = sum(n.astype(F32) for n in named)
    earlier = (
        lax.broadcasted_iota(jnp.int32, (tok_rows, tok_rows), 1)
        < lax.broadcasted_iota(jnp.int32, (tok_rows, tok_rows), 0)
    ).astype(F32)
    rank = dot(earlier.astype(BF16), chosen.astype(BF16), (1, 0))
    slot_numbers = lax.broadcasted_iota(jnp.int32, (tok_rows, slots), 1)
    total, near = None, None
    for k in range(top_count):
        own = jnp.sum(jnp.where(named[k], rank, 0.0), axis=1, keepdims=True).astype(jnp.int32)
        mark, near_mark = (
            (slot_numbers == order[:, k : k + 1] * capacity + own).astype(F32)
            for order in (lanes, near_lanes)
        )
        place_ref[k * tok_rows : (k + 1) * tok_rows, :] = mark.astype(BF16)
        total = mark if total is None else total + mark
        near = near_mark if near is None else near + near_mark
    near_ref[...] = near.astype(BF16)
    total = total.astype(BF16)
    for columns in tiles(width):
        slots_ref[:, columns] = dot(total, tokens_ref[:, columns], (0, 0)).astype(BF16)


def spread_kernel(near_ref, rows_ref, _, slots_ref):
    for columns in tiles(rows_ref.shape[1]):
        slots_ref[:, columns] = dot(near_ref[...], rows_ref[:, columns], (0, 0)).astype(BF16)


def hidden_kernel(parts, joined, rows_ref, *refs):
    sources, refs = [rows_ref, *refs[: 2 * parts]], refs[2 * parts :]
    outs, (sems, out_sems), refs = refs[:3], refs[3:5], refs[5:]
    hidden_ref, by_gate_ref, by_up_ref, rows_ref, gate_ref, up_ref = refs
    gate, up = shares(gate_ref, parts, joined), shares(up_ref, parts, joined)
    copies = fetch(sources, [rows_ref, *gate, *up], sems)
    for copy in copies[: 1 + parts]:
        copy.wait()
    for i in range(gate_ref.shape[0]):
        pre_gate = dot(rows_ref[...], gate_ref[i], (1, 0))
        if i == 0:
            for copy in copies[1 + parts :]:
                copy.wait()
        pre_up = dot(rows_ref[...], up_ref[i], (1, 0))
        sig = jax.nn.sigmoid(pre_gate)
        act = pre_gate * sig
        hidden_ref[i] = (act * pre_up).astype(BF16)
        by_gate_ref[i] = pre_up * sig * (1.0 + pre_gate * (1.0 - sig))
        by_up_ref[i] = act
    for copy in fetch([hidden_ref, by_gate_ref, by_up_ref], outs, out_sems):
        copy.wait()


def in_place_kernel(_, after_ref, out_ref):
    pass


def out_kernel(parts, joined, hidden_ref, *refs):
    sources, refs = refs[:parts], refs[parts:]
    out_ref, sems, out_sems, stage_ref, hidden_stage, down_ref = refs
    down = shares(down_ref, parts, joined, 0)
    pieces = tiles(out_ref.shape[1])
    (first,) = fetch([hidden_ref], [hidden_stage], sems)
    copies = [
        fetch(
            [source.at[:, columns] for source in sources],
            [share.at[:, columns] for share in down],
            sems.at[pl.ds(1 + d * parts, parts)],
        )
        for d, columns in enumerate(pieces)
    ]
    first.wait()
    sent = []
    for d, columns in enumerate(pieces):
        for copy in copies[d]:
            copy.wait()
        stage_ref[:, columns] = sum(
            dot(hidden_stage[i], down_ref[i, :, columns], (1, 0)) for i in range(down_ref.shape[0])
        ).astype(BF16)
        sent.append(store(stage_ref.at[:, columns], out_ref.at[:, columns], out_sems.at[d]))
    for copy in sent:
        copy.wait()


def backward_kernel(parts, joined, plane_ref, _, *refs):
    sources, refs = refs[: 2 + 4 * parts], refs[2 + 4 * parts :]
    out_ref, sems, out_sems, back_gate_ref, back_up_ref, stage_ref, rows_ref = refs[:7]
    down_ref, by_gate_ref, by_up_ref, gate_ref, up_ref = refs[7:]
    share = rows_ref.shape[0] // parts
    places = [
        rows_ref.at[pl.ds(pl.multiple_of((plane_ref[0] + parts - i) % parts * share, share), share)]
        for i in range(parts)
    ]
    down, gate, up = (
        shares(down_ref, parts, joined, 0),
        shares(gate_ref, parts, joined),
        shares(up_ref, parts, joined),
    )
    copies = fetch(sources, [*places, *down, by_gate_ref, by_up_ref, *gate, *up], sems)
    for copy in copies[: 2 + 2 * parts]:
        copy.wait()
    for i in range(down_ref.shape[0]):
        back_hidden = dot(rows_ref[...], down_ref[i], (1, 1))
        back_gate_ref[i] = (back_hidden * by_gate_ref[i]).astype(BF16)
        back_up_ref[i] = (back_hidden * by_up_ref[i]).astype(BF16)
    for copy in copies[2 + 2 * parts :]:
        copy.wait()
    sent = []
    for d, columns in enumerate(tiles(out_ref.shape[1])):
        stage_ref[:, columns] = sum(
            dot(back_gate_ref[i], gate_ref[i, columns, :], (1, 1))
            + dot(back_up_ref[i], up_ref[i, columns, :], (1, 1))
            for i in range(down_ref.shape[0])
        ).astype(BF16)
        sent.append(store(stage_ref.at[:, columns], out_ref.at[:, columns], out_sems.at[d]))
    for copy in sent:
        copy.wait()


def mix_kernel(place_ref, gates_ref, cotangent_ref, slots_ref, mixed_ref, gate_grad_ref):
    tok_rows, top_count = gates_ref.shape
    total, grads = None, []
    for k in range(top_count):
        raw = dot(place_ref[k * tok_rows : (k + 1) * tok_rows, :], slots_ref[...], (1, 0))
        grads.append(jnp.sum(raw * cotangent_ref[...].astype(F32), axis=1, keepdims=True))
        term = raw * gates_ref[:, k : k + 1]
        total = term if total is None else total + term
    mixed_ref[...] = total.astype(BF16)
    gate_grad_ref[...] = jnp.concatenate(grads, axis=1)


def sum_kernel(place_ref, gates_ref, slots_ref, out_ref):
    tok_rows, top_count = gates_ref.shape
    total = None
    for k in range(top_count):
        raw = dot(place_ref[k * tok_rows : (k + 1) * tok_rows, :], slots_ref[...], (1, 0))
        term = raw * gates_ref[:, k : k + 1]
        total = term if total is None else total + term
    out_ref[...] = total.astype(BF16)


def call(kernel, outs, flops, scratch=(), far=(), far_out=False, vmem=SMALL_VMEM, aliases=None):
    def run(*args):
        moved = sum(a.size * a.dtype.itemsize for a in (*args, *outs))
        spaces = [
            pltpu.SMEM if a.shape == (1,) else pl.ANY if i in far else pltpu.VMEM
            for i, a in enumerate(args)
        ]
        return pl.pallas_call(
            kernel,
            out_shape=tuple(jax.ShapeDtypeStruct(o.shape, o.dtype) for o in outs),
            in_specs=[pl.BlockSpec(memory_space=space) for space in spaces],
            out_specs=tuple(
                pl.BlockSpec(memory_space=pl.ANY if far_out else pltpu.VMEM) for _ in outs
            ),
            scratch_shapes=scratch,
            input_output_aliases=aliases or {},
            compiler_params=pltpu.CompilerParams(vmem_limit_bytes=vmem),
            cost_estimate=pl.CostEstimate(flops=flops, bytes_accessed=moved, transcendentals=0),
        )(*args)

    return run


def body(tokens, cotangent, routes, gates, w_gate, w_up, w_down):
    tok_rows, width = tokens.shape
    top_count = routes.shape[1]
    parts, experts = lax.axis_size("dp"), lax.axis_size("expert")
    hidden = w_gate.shape[2]
    capacity = max(2, 3 * tok_rows * top_count // (2 * experts))
    slots = experts * capacity
    axes = ("dp", "expert")

    def device(g, j):
        return g * experts + j

    sets = experts // parts

    def home(e, c):
        return device((e + 1) % parts, e // parts * parts + c)

    swap = [(device(g, e), home(e, g)) for g in range(parts) for e in range(experts)]
    planes = [
        [[device(g, parts * q + c) for q in range(sets)] for g in range(parts)] for c in range(parts)
    ]
    everywhere = [[d for plane in planes[c] for d in plane] for c in range(parts)]
    in_plane = [plane for c in range(parts) for plane in planes[c]]

    def swapped(weight):
        return lax.ppermute(weight[0], axes, swap)

    def whole_expert(own):
        held = [own]
        for step in range(1, parts):
            turn = [(j, j // parts * parts + (j + step) % parts) for j in range(experts)]
            held.append(lax.ppermute(own, "expert", turn))
        return held

    def exchange(rows):
        rows = rows.reshape(experts, capacity, width)
        return lax.all_to_all(
            rows, axes, 0, 0, axis_index_groups=everywhere, tiled=True
        ).reshape(slots, width)

    def exchange_late(rows):
        rows = rows.reshape(sets, parts * capacity, width)
        rows = lax.all_to_all(rows, axes, 0, 0, axis_index_groups=in_plane, tiled=True)
        rows = rows.reshape(sets, parts, capacity, width)
        crossed = []
        for i in range(parts):
            share = rows[:, i].reshape(sets * capacity, width)
            if i > 0:
                share = lax.ppermute(share, "dp", [(g, (g + i) % parts) for g in range(parts)])
            crossed.append(share)
        return crossed

    spread_flops = 2 * slots * tok_rows * width
    dot_flops = 2 * slots * width * hidden * parts
    slot_shape = jax.ShapeDtypeStruct((slots, width), BF16)
    place_shape = jax.ShapeDtypeStruct((top_count * tok_rows, slots), BF16)
    joined = hidden % 128 == 0
    units, span = (1, parts * hidden) if joined else (parts, hidden)
    unit_shape = jax.ShapeDtypeStruct((units, slots, span), F32)
    hidden_shape = jax.ShapeDtypeStruct((units, slots, span), BF16)
    token_shape = jax.ShapeDtypeStruct((tok_rows, width), BF16)
    hidden_scratch = pltpu.VMEM((units, slots, span), BF16)
    unit_scratch = pltpu.VMEM((units, slots, span), F32)
    row_scratch = pltpu.VMEM((slots, width), BF16)
    in_scratch = pltpu.VMEM((units, width, span), BF16)
    down_scratch = pltpu.VMEM((units, span, width), BF16)
    pieces = len(tiles(width))

    def sems(number):
        return pltpu.SemaphoreType.DMA((number,))

    gate_own, up_own, down_own = swapped(w_gate), swapped(w_up), swapped(w_down)
    gate_w, up_w = whole_expert(gate_own), whole_expert(up_own)
    plane = lax.axis_index("dp").astype(jnp.int32).reshape(1)
    x_slots, place, near = call(
        functools.partial(place_kernel, experts, parts),
        [slot_shape, place_shape, jax.ShapeDtypeStruct((tok_rows, slots), BF16)],
        spread_flops,
    )(plane, routes, tokens)
    x_rows = exchange(x_slots)
    (dy_slots,) = call(spread_kernel, [slot_shape], 256 * spread_flops, far=(2,))(
        near, cotangent, gate_own
    )
    dy_shares = exchange_late(dy_slots)
    hidden_rows, by_gate, by_up = call(
        functools.partial(hidden_kernel, parts, joined),
        [hidden_shape, unit_shape, unit_shape],
        2 * dot_flops,
        [sems(1 + 2 * parts), sems(3), hidden_scratch, unit_scratch, unit_scratch, row_scratch]
        + [in_scratch] * 2,
        far=range(1 + 2 * parts),
        far_out=True,
        vmem=LARGE_VMEM,
    )(x_rows, *gate_w, *up_w)
    (down_own,) = call(
        in_place_kernel, [down_own], 0, far=range(2), far_out=True, vmem=LARGE_VMEM, aliases={0: 0}
    )(down_own, hidden_rows)
    down_w = whole_expert(down_own)
    (out_rows,) = call(
        functools.partial(out_kernel, parts, joined),
        [slot_shape],
        dot_flops,
        [sems(1 + pieces * parts), sems(pieces), row_scratch, hidden_scratch, down_scratch],
        far=range(1 + parts),
        far_out=True,
    )(hidden_rows, *down_w)
    out_slots = exchange(out_rows)
    (grad_rows,) = call(
        functools.partial(backward_kernel, parts, joined),
        [slot_shape],
        64 * dot_flops,
        [sems(2 + 4 * parts), sems(pieces), hidden_scratch, hidden_scratch]
        + [row_scratch, row_scratch, down_scratch, unit_scratch, unit_scratch]
        + [in_scratch] * 2,
        far=range(1, 4 + 4 * parts),
        far_out=True,
        vmem=LARGE_VMEM,
    )(plane, out_rows, *dy_shares, *down_w, by_gate, by_up, *gate_w, *up_w)
    grad_slots = exchange(grad_rows)
    mixed, gate_grad = call(
        mix_kernel, [token_shape, jax.ShapeDtypeStruct(gates.shape, F32)], 2 * spread_flops
    )(place, gates, cotangent, out_slots)
    (token_grad,) = call(sum_kernel, [token_shape], 2 * spread_flops)(place, gates, grad_slots)
    return (mixed, token_grad, gate_grad)


def solution(mesh):
    rows, weights = P(("dp", "expert"), None), P("expert", None, "dp")
    return jax.shard_map(
        body,
        mesh=mesh,
        in_specs=(rows, rows, rows, rows, weights, weights, P("expert", "dp", None)),
        out_specs=(rows, rows, rows),
        check_vma=False,
    )
```

```python
import functools

import jax
import jax.numpy as jnp
from jax import lax
from jax.experimental import pallas as pl
from jax.experimental.pallas import tpu as pltpu
from jax.sharding import PartitionSpec as P

BF16 = jnp.bfloat16
F32 = jnp.float32
SMALL_VMEM, LARGE_VMEM = 12 << 20, 60 << 20


def dot(a, b, dims):
    return lax.dot_general(a, b, ((dims[:1], dims[1:]), ((), ())), preferred_element_type=F32)


def tiles(width):
    tile = min(512, width)
    return [slice(d, d + tile) for d in range(0, width, tile)]


def fetch(sources, targets, sems):
    copies = [pltpu.make_async_copy(s, t, sems.at[i]) for i, (s, t) in enumerate(zip(sources, targets))]
    for copy in copies:
        copy.start()
    return copies


def store(stage_ref, out_ref, sem):
    copy = pltpu.make_async_copy(stage_ref, out_ref, sem)
    copy.start()
    return copy


def shares(unit_ref, parts, joined, axis=1):
    if not joined:
        return [unit_ref.at[i] for i in range(parts)]
    size = unit_ref.shape[1 + axis] // parts
    cuts = [pl.ds(i * size, size) for i in range(parts)]
    return [unit_ref.at[0, cut] if axis == 0 else unit_ref.at[0, :, cut] for cut in cuts]


def place_kernel(experts, parts, plane_ref, routes_ref, tokens_ref, slots_ref, place_ref, near_ref):
    slots, width = slots_ref.shape
    capacity = slots // experts
    tok_rows, top_count = routes_ref.shape
    routes = routes_ref[...]
    home_plane, home_set = lax.rem(routes + 1, parts), lax.div(routes, parts)
    lanes = home_plane * (experts // parts) + home_set
    near_lanes = home_set * parts + lax.rem(home_plane + (parts - plane_ref[0]), parts)
    numbers = lax.broadcasted_iota(jnp.int32, (tok_rows, experts), 1)
    named = [numbers == routes[:, k : k + 1] for k in range(top_count)]
    chosen = sum(n.astype(F32) for n in named)
    earlier = (
        lax.broadcasted_iota(jnp.int32, (tok_rows, tok_rows), 1)
        < lax.broadcasted_iota(jnp.int32, (tok_rows, tok_rows), 0)
    ).astype(F32)
    rank = dot(earlier.astype(BF16), chosen.astype(BF16), (1, 0))
    slot_numbers = lax.broadcasted_iota(jnp.int32, (tok_rows, slots), 1)
    near = None
    for k in range(top_count):
        own = jnp.sum(jnp.where(named[k], rank, 0.0), axis=1, keepdims=True).astype(jnp.int32)
        mark, near_mark = (
            (slot_numbers == order[:, k : k + 1] * capacity + own).astype(F32)
            for order in (lanes, near_lanes)
        )
        place_ref[k * tok_rows : (k + 1) * tok_rows, :] = mark.astype(BF16)
        near = near_mark if near is None else near + near_mark
    near = near.astype(BF16)
    near_ref[...] = near
    for columns in tiles(width):
        slots_ref[:, columns] = dot(near, tokens_ref[:, columns], (0, 0)).astype(BF16)


def spread_kernel(near_ref, rows_ref, _, slots_ref):
    for columns in tiles(rows_ref.shape[1]):
        slots_ref[:, columns] = dot(near_ref[...], rows_ref[:, columns], (0, 0)).astype(BF16)


def cut_kernel(parts, rows_ref, *refs):
    out_refs, sems = refs[-1 - parts : -1], refs[-1]
    sets = rows_ref.shape[0]
    for copy in fetch(
        [rows_ref.at[q, i] for i in range(parts) for q in range(sets)],
        [out_refs[i].at[q] for i in range(parts) for q in range(sets)],
        sems,
    ):
        copy.wait()


def by_plane(rows_ref, plane_ref, parts):
    size = rows_ref.shape[0] // parts
    starts = [lax.rem(plane_ref[0] + (parts - i), parts) * size for i in range(parts)]
    return [rows_ref.at[pl.ds(pl.multiple_of(start, size), size)] for start in starts]


def hidden_kernel(parts, joined, plane_ref, *refs):
    sources, refs = refs[: 3 * parts], refs[3 * parts :]
    outs, (sems, out_sems), refs = refs[:3], refs[3:5], refs[5:]
    hidden_ref, by_gate_ref, by_up_ref, rows_ref, gate_ref, up_ref = refs
    gate, up = shares(gate_ref, parts, joined), shares(up_ref, parts, joined)
    copies = fetch(sources, [*by_plane(rows_ref, plane_ref, parts), *gate, *up], sems)
    for copy in copies[: 2 * parts]:
        copy.wait()
    for i in range(gate_ref.shape[0]):
        pre_gate = dot(rows_ref[...], gate_ref[i], (1, 0))
        if i == 0:
            for copy in copies[2 * parts :]:
                copy.wait()
        pre_up = dot(rows_ref[...], up_ref[i], (1, 0))
        sig = jax.nn.sigmoid(pre_gate)
        act = pre_gate * sig
        hidden_ref[i] = (act * pre_up).astype(BF16)
        by_gate_ref[i] = pre_up * sig * (1.0 + pre_gate * (1.0 - sig))
        by_up_ref[i] = act
    for copy in fetch([hidden_ref, by_gate_ref, by_up_ref], outs, out_sems):
        copy.wait()


def in_place_kernel(_, after_ref, out_ref):
    pass


def out_kernel(parts, joined, hidden_ref, *refs):
    sources, refs = refs[:parts], refs[parts:]
    out_ref, sems, out_sems, stage_ref, hidden_stage, down_ref = refs
    down = shares(down_ref, parts, joined, 0)
    pieces = tiles(out_ref.shape[1])
    (first,) = fetch([hidden_ref], [hidden_stage], sems)
    copies = [
        fetch(
            [source.at[:, columns] for source in sources],
            [share.at[:, columns] for share in down],
            sems.at[pl.ds(1 + d * parts, parts)],
        )
        for d, columns in enumerate(pieces)
    ]
    first.wait()
    sent = []
    for d, columns in enumerate(pieces):
        for copy in copies[d]:
            copy.wait()
        stage_ref[:, columns] = sum(
            dot(hidden_stage[i], down_ref[i, :, columns], (1, 0)) for i in range(down_ref.shape[0])
        ).astype(BF16)
        sent.append(store(stage_ref.at[:, columns], out_ref.at[:, columns], out_sems.at[d]))
    for copy in sent:
        copy.wait()


def backward_kernel(parts, joined, plane_ref, *refs):
    sources, refs = refs[: 2 + 4 * parts], refs[2 + 4 * parts :]
    out_ref, sems, out_sems, back_gate_ref, back_up_ref, stage_ref, rows_ref = refs[:7]
    down_ref, by_gate_ref, by_up_ref, gate_ref, up_ref = refs[7:]
    down, gate, up = (
        shares(down_ref, parts, joined, 0),
        shares(gate_ref, parts, joined),
        shares(up_ref, parts, joined),
    )
    copies = fetch(sources, [*by_plane(rows_ref, plane_ref, parts), *down, by_gate_ref, by_up_ref, *gate, *up], sems)
    for copy in copies[: 2 + 2 * parts]:
        copy.wait()
    for i in range(down_ref.shape[0]):
        back_hidden = dot(rows_ref[...], down_ref[i], (1, 1))
        back_gate_ref[i] = (back_hidden * by_gate_ref[i]).astype(BF16)
        back_up_ref[i] = (back_hidden * by_up_ref[i]).astype(BF16)
    for copy in copies[2 + 2 * parts :]:
        copy.wait()
    sent = []
    for d, columns in enumerate(tiles(out_ref.shape[1])):
        stage_ref[:, columns] = sum(
            dot(back_gate_ref[i], gate_ref[i, columns, :], (1, 1))
            + dot(back_up_ref[i], up_ref[i, columns, :], (1, 1))
            for i in range(down_ref.shape[0])
        ).astype(BF16)
        sent.append(store(stage_ref.at[:, columns], out_ref.at[:, columns], out_sems.at[d]))
    for copy in sent:
        copy.wait()


def mix_kernel(place_ref, gates_ref, cotangent_ref, slots_ref, mixed_ref, gate_grad_ref):
    tok_rows, top_count = gates_ref.shape
    total, grads = None, []
    for k in range(top_count):
        raw = dot(place_ref[k * tok_rows : (k + 1) * tok_rows, :], slots_ref[...], (1, 0))
        grads.append(jnp.sum(raw * cotangent_ref[...].astype(F32), axis=1, keepdims=True))
        term = raw * gates_ref[:, k : k + 1]
        total = term if total is None else total + term
    mixed_ref[...] = total.astype(BF16)
    gate_grad_ref[...] = jnp.concatenate(grads, axis=1)


def sum_kernel(place_ref, gates_ref, slots_ref, out_ref):
    tok_rows, top_count = gates_ref.shape
    total = None
    for k in range(top_count):
        raw = dot(place_ref[k * tok_rows : (k + 1) * tok_rows, :], slots_ref[...], (1, 0))
        term = raw * gates_ref[:, k : k + 1]
        total = term if total is None else total + term
    out_ref[...] = total.astype(BF16)


def call(kernel, outs, flops, scratch=(), far=(), far_out=False, vmem=SMALL_VMEM, aliases=None):
    def run(*args):
        moved = sum(a.size * a.dtype.itemsize for a in (*args, *outs))
        spaces = [
            pltpu.SMEM if a.shape == (1,) else pl.ANY if i in far else pltpu.VMEM
            for i, a in enumerate(args)
        ]
        return pl.pallas_call(
            kernel,
            out_shape=tuple(jax.ShapeDtypeStruct(o.shape, o.dtype) for o in outs),
            in_specs=[pl.BlockSpec(memory_space=space) for space in spaces],
            out_specs=tuple(
                pl.BlockSpec(memory_space=pl.ANY if far_out else pltpu.VMEM) for _ in outs
            ),
            scratch_shapes=scratch,
            input_output_aliases=aliases or {},
            compiler_params=pltpu.CompilerParams(vmem_limit_bytes=vmem),
            cost_estimate=pl.CostEstimate(flops=flops, bytes_accessed=moved, transcendentals=0),
        )(*args)

    return run


def body(tokens, cotangent, routes, gates, w_gate, w_up, w_down):
    tok_rows, width = tokens.shape
    top_count = routes.shape[1]
    parts, experts = lax.axis_size("dp"), lax.axis_size("expert")
    hidden = w_gate.shape[2]
    capacity = max(2, 3 * tok_rows * top_count // (2 * experts))
    slots = experts * capacity
    axes = ("dp", "expert")

    def device(g, j):
        return g * experts + j

    sets = experts // parts

    def home(e, c):
        return device((e + 1) % parts, e // parts * parts + c)

    swap = [(device(g, e), home(e, g)) for g in range(parts) for e in range(experts)]
    planes = [
        [[device(g, parts * q + c) for q in range(sets)] for g in range(parts)] for c in range(parts)
    ]
    everywhere = [[d for plane in planes[c] for d in plane] for c in range(parts)]
    in_plane = [plane for c in range(parts) for plane in planes[c]]

    def swapped(weight):
        return lax.ppermute(weight[0], axes, swap)

    def whole_expert(own):
        held = [own]
        for step in range(1, parts):
            turn = [(j, j // parts * parts + (j + step) % parts) for j in range(experts)]
            held.append(lax.ppermute(own, "expert", turn))
        return held

    def dispatch(rows, after=()):
        rows = rows.reshape(sets, parts * capacity, width)
        rows = lax.all_to_all(rows, axes, 0, 0, axis_index_groups=in_plane, tiled=True)
        cut = call(
            functools.partial(cut_kernel, parts),
            [jax.ShapeDtypeStruct((sets, capacity, width), BF16)] * parts,
            0,
            [sems(parts * sets)],
            far=range(1 + len(after)),
            far_out=True,
        )(rows.reshape(sets, parts, capacity, width), *after)
        crossed = []
        for i, rows in enumerate(cut):
            rows = rows.reshape(sets * capacity, width)
            if i > 0:
                rows = lax.ppermute(rows, "dp", [(g, (g + i) % parts) for g in range(parts)])
            crossed.append(rows)
        return crossed

    def send_back(rows):
        rows = rows.reshape(experts, capacity, width)
        return lax.all_to_all(
            rows, axes, 0, 0, axis_index_groups=everywhere, tiled=True
        ).reshape(slots, width)

    spread_flops = 2 * slots * tok_rows * width
    dot_flops = 2 * slots * width * hidden * parts
    slot_shape = jax.ShapeDtypeStruct((slots, width), BF16)
    place_shape = jax.ShapeDtypeStruct((top_count * tok_rows, slots), BF16)
    joined = hidden % 128 == 0
    units, span = (1, parts * hidden) if joined else (parts, hidden)
    unit_shape = jax.ShapeDtypeStruct((units, slots, span), F32)
    hidden_shape = jax.ShapeDtypeStruct((units, slots, span), BF16)
    token_shape = jax.ShapeDtypeStruct((tok_rows, width), BF16)
    hidden_scratch = pltpu.VMEM((units, slots, span), BF16)
    unit_scratch = pltpu.VMEM((units, slots, span), F32)
    row_scratch = pltpu.VMEM((slots, width), BF16)
    in_scratch = pltpu.VMEM((units, width, span), BF16)
    down_scratch = pltpu.VMEM((units, span, width), BF16)
    pieces = len(tiles(width))

    def sems(number):
        return pltpu.SemaphoreType.DMA((number,))

    gate_own, up_own, down_own = swapped(w_gate), swapped(w_up), swapped(w_down)
    gate_w, up_w = whole_expert(gate_own), whole_expert(up_own)
    plane = lax.axis_index("dp").astype(jnp.int32).reshape(1)
    x_slots, place, near = call(
        functools.partial(place_kernel, experts, parts),
        [slot_shape, place_shape, jax.ShapeDtypeStruct((tok_rows, slots), BF16)],
        spread_flops,
    )(plane, routes, tokens)
    x_shares = dispatch(x_slots)
    (dy_slots,) = call(spread_kernel, [slot_shape], 256 * spread_flops, far=(2,))(
        near, cotangent, gate_own
    )
    hidden_rows, by_gate, by_up = call(
        functools.partial(hidden_kernel, parts, joined),
        [hidden_shape, unit_shape, unit_shape],
        2 * dot_flops,
        [sems(3 * parts), sems(3), hidden_scratch, unit_scratch, unit_scratch, row_scratch]
        + [in_scratch] * 2,
        far=range(1, 1 + 3 * parts),
        far_out=True,
        vmem=LARGE_VMEM,
    )(plane, *x_shares, *gate_w, *up_w)
    (down_own,) = call(
        in_place_kernel, [down_own], 0, far=range(2), far_out=True, vmem=LARGE_VMEM, aliases={0: 0}
    )(down_own, hidden_rows)
    down_w = whole_expert(down_own)
    (out_rows,) = call(
        functools.partial(out_kernel, parts, joined),
        [slot_shape],
        dot_flops,
        [sems(1 + pieces * parts), sems(pieces), row_scratch, hidden_scratch, down_scratch],
        far=range(1 + parts),
        far_out=True,
    )(hidden_rows, *down_w)
    dy_shares = dispatch(dy_slots, (out_rows,))
    out_slots = send_back(out_rows)
    (grad_rows,) = call(
        functools.partial(backward_kernel, parts, joined),
        [slot_shape],
        64 * dot_flops,
        [sems(2 + 4 * parts), sems(pieces), hidden_scratch, hidden_scratch]
        + [row_scratch, row_scratch, down_scratch, unit_scratch, unit_scratch]
        + [in_scratch] * 2,
        far=range(1, 3 + 4 * parts),
        far_out=True,
        vmem=LARGE_VMEM,
    )(plane, *dy_shares, *down_w, by_gate, by_up, *gate_w, *up_w)
    grad_slots = send_back(grad_rows)
    mixed, gate_grad = call(
        mix_kernel, [token_shape, jax.ShapeDtypeStruct(gates.shape, F32)], 2 * spread_flops
    )(place, gates, cotangent, out_slots)
    (token_grad,) = call(sum_kernel, [token_shape], 2 * spread_flops)(place, gates, grad_slots)
    return (mixed, token_grad, gate_grad)


def solution(mesh):
    rows, weights = P(("dp", "expert"), None), P("expert", None, "dp")
    return jax.shard_map(
        body,
        mesh=mesh,
        in_specs=(rows, rows, rows, rows, weights, weights, P("expert", "dp", None)),
        out_specs=(rows, rows, rows),
        check_vma=False,
    )
```

```python
import functools

import jax
import jax.numpy as jnp
from jax import lax
from jax.experimental import pallas as pl
from jax.experimental.pallas import tpu as pltpu
from jax.sharding import PartitionSpec as P

BF16 = jnp.bfloat16
F32 = jnp.float32
SMALL_VMEM, LARGE_VMEM = 12 << 20, 60 << 20


def dot(a, b, dims):
    return lax.dot_general(a, b, ((dims[:1], dims[1:]), ((), ())), preferred_element_type=F32)


def tiles(width):
    tile = min(512, width)
    return [slice(d, d + tile) for d in range(0, width, tile)]


def fetch(sources, targets, sems):
    copies = [pltpu.make_async_copy(s, t, sems.at[i]) for i, (s, t) in enumerate(zip(sources, targets))]
    for copy in copies:
        copy.start()
    return copies


def store(stage_ref, out_ref, sem):
    copy = pltpu.make_async_copy(stage_ref, out_ref, sem)
    copy.start()
    return copy


def shares(unit_ref, parts, joined, axis=1):
    if not joined:
        return [unit_ref.at[i] for i in range(parts)]
    size = unit_ref.shape[1 + axis] // parts
    cuts = [pl.ds(i * size, size) for i in range(parts)]
    return [unit_ref.at[0, cut] if axis == 0 else unit_ref.at[0, :, cut] for cut in cuts]


def place_kernel(sets, parts, here_ref, *refs):
    route_refs, token_refs, (slots_ref, place_ref, near_ref) = refs[:2], refs[2:4], refs[4:]
    slots, width = slots_ref.shape
    capacity = slots // (2 * sets * parts)
    tok_rows, top_count = route_refs[0].shape
    earlier = (
        lax.broadcasted_iota(jnp.int32, (tok_rows, tok_rows), 1)
        < lax.broadcasted_iota(jnp.int32, (tok_rows, tok_rows), 0)
    ).astype(BF16)
    slot_numbers = lax.broadcasted_iota(jnp.int32, (tok_rows, slots), 1)
    for block, route_ref in enumerate(route_refs):
        routes = route_ref[...]
        home_plane, home_set = lax.rem(routes + 1, parts), lax.div(routes, parts) - here_ref[1]
        inside = (home_set >= 0) & (home_set < sets)
        back = home_plane * sets + home_set
        out = home_set * parts + lax.rem(home_plane + (parts - here_ref[0]), parts)
        numbers = lax.broadcasted_iota(jnp.int32, (tok_rows, 2 * sets * parts), 1)
        named = [numbers == routes[:, k : k + 1] for k in range(top_count)]
        chosen = sum(n.astype(F32) for n in named)
        rank = dot(earlier, chosen.astype(BF16), (1, 0))
        near = None
        for k in range(top_count):
            own = jnp.sum(jnp.where(named[k], rank, 0.0), axis=1, keepdims=True).astype(jnp.int32)
            own = own + block * capacity
            mark, near_mark = (
                (
                    slot_numbers
                    == jnp.where(
                        inside[:, k : k + 1], lane[:, k : k + 1] * (2 * capacity) + own, slots
                    )
                ).astype(F32)
                for lane in (back, out)
            )
            place_ref[block, k] = mark.astype(BF16)
            near = near_mark if near is None else near + near_mark
        near_ref[block] = near.astype(BF16)
    for columns in tiles(width):
        slots_ref[:, columns] = sum(
            dot(near_ref[block], token_refs[block][:, columns], (0, 0)) for block in range(2)
        ).astype(BF16)


def spread_kernel(near_ref, *refs):
    row_refs, slots_ref = refs[:2], refs[-1]
    for columns in tiles(slots_ref.shape[1]):
        slots_ref[:, columns] = sum(
            dot(near_ref[block], row_refs[block][:, columns], (0, 0)) for block in range(2)
        ).astype(BF16)


def cut_kernel(parts, rows_ref, *refs):
    out_refs, sems = refs[-1 - parts : -1], refs[-1]
    sets = rows_ref.shape[0]
    for copy in fetch(
        [rows_ref.at[q, i] for i in range(parts) for q in range(sets)],
        [out_refs[i].at[q] for i in range(parts) for q in range(sets)],
        sems,
    ):
        copy.wait()


def by_plane(rows_ref, plane_ref, parts):
    size = rows_ref.shape[0] // parts
    starts = [lax.rem(plane_ref[0] + (parts - i), parts) * size for i in range(parts)]
    return [rows_ref.at[pl.ds(pl.multiple_of(start, size), size)] for start in starts]


def hidden_kernel(parts, joined, plane_ref, *refs):
    sources, refs = refs[: 3 * parts], refs[3 * parts :]
    outs, (sems, out_sems), refs = refs[:3], refs[3:5], refs[5:]
    hidden_ref, by_gate_ref, by_up_ref, rows_ref, gate_ref, up_ref = refs
    gate, up = shares(gate_ref, parts, joined), shares(up_ref, parts, joined)
    copies = fetch(sources, [*by_plane(rows_ref, plane_ref, parts), *gate, *up], sems)
    for copy in copies[: 2 * parts]:
        copy.wait()
    for i in range(gate_ref.shape[0]):
        pre_gate = dot(rows_ref[...], gate_ref[i], (1, 0))
        if i == 0:
            for copy in copies[2 * parts :]:
                copy.wait()
        pre_up = dot(rows_ref[...], up_ref[i], (1, 0))
        sig = jax.nn.sigmoid(pre_gate)
        act = pre_gate * sig
        hidden_ref[i] = (act * pre_up).astype(BF16)
        by_gate_ref[i] = pre_up * sig * (1.0 + pre_gate * (1.0 - sig))
        by_up_ref[i] = act
    for copy in fetch([hidden_ref, by_gate_ref, by_up_ref], outs, out_sems):
        copy.wait()


def out_kernel(parts, joined, hidden_ref, *refs):
    sources, refs = refs[:parts], refs[parts:]
    out_ref, sems, out_sems, stage_ref, hidden_stage, down_ref = refs
    down = shares(down_ref, parts, joined, 0)
    pieces = tiles(out_ref.shape[1])
    (first,) = fetch([hidden_ref], [hidden_stage], sems)
    copies = [
        fetch(
            [source.at[:, columns] for source in sources],
            [share.at[:, columns] for share in down],
            sems.at[pl.ds(1 + d * parts, parts)],
        )
        for d, columns in enumerate(pieces)
    ]
    first.wait()
    sent = []
    for d, columns in enumerate(pieces):
        for copy in copies[d]:
            copy.wait()
        stage_ref[:, columns] = sum(
            dot(hidden_stage[i], down_ref[i, :, columns], (1, 0)) for i in range(down_ref.shape[0])
        ).astype(BF16)
        sent.append(store(stage_ref.at[:, columns], out_ref.at[:, columns], out_sems.at[d]))
    for copy in sent:
        copy.wait()


def backward_kernel(parts, joined, plane_ref, *refs):
    sources, refs = refs[: 2 + 4 * parts], refs[2 + 4 * parts :]
    out_ref, sems, out_sems, back_gate_ref, back_up_ref, stage_ref, rows_ref = refs[:7]
    down_ref, by_gate_ref, by_up_ref, gate_ref, up_ref = refs[7:]
    down, gate, up = (
        shares(down_ref, parts, joined, 0),
        shares(gate_ref, parts, joined),
        shares(up_ref, parts, joined),
    )
    copies = fetch(sources, [*by_plane(rows_ref, plane_ref, parts), *down, by_gate_ref, by_up_ref, *gate, *up], sems)
    for copy in copies[: 2 + 2 * parts]:
        copy.wait()
    for i in range(down_ref.shape[0]):
        back_hidden = dot(rows_ref[...], down_ref[i], (1, 1))
        back_gate_ref[i] = (back_hidden * by_gate_ref[i]).astype(BF16)
        back_up_ref[i] = (back_hidden * by_up_ref[i]).astype(BF16)
    for copy in copies[2 + 2 * parts :]:
        copy.wait()
    sent = []
    for d, columns in enumerate(tiles(out_ref.shape[1])):
        stage_ref[:, columns] = sum(
            dot(back_gate_ref[i], gate_ref[i, columns, :], (1, 1))
            + dot(back_up_ref[i], up_ref[i, columns, :], (1, 1))
            for i in range(down_ref.shape[0])
        ).astype(BF16)
        sent.append(store(stage_ref.at[:, columns], out_ref.at[:, columns], out_sems.at[d]))
    for copy in sent:
        copy.wait()


def combine_kernel(block, place_ref, gates_ref, slots_ref, *refs):
    cotangent_ref, refs = (refs[0], refs[1:]) if len(refs) == 3 else (None, refs)
    total, grads = None, []
    for k in range(gates_ref.shape[1]):
        raw = dot(place_ref[block, k], slots_ref[...], (1, 0))
        if cotangent_ref is not None:
            grads.append(jnp.sum(raw * cotangent_ref[...].astype(F32), axis=1, keepdims=True))
        term = raw * gates_ref[:, k : k + 1]
        total = term if total is None else total + term
    refs[0][...] = total.astype(refs[0].dtype)
    if grads:
        refs[1][...] = jnp.concatenate(grads, axis=1)


def call(kernel, outs, flops, scratch=(), far=(), far_out=False, vmem=SMALL_VMEM, aliases=None):
    def run(*args):
        moved = sum(a.size * a.dtype.itemsize for a in (*args, *outs))
        spaces = [
            pltpu.SMEM if a.ndim == 1 else pl.ANY if i in far else pltpu.VMEM
            for i, a in enumerate(args)
        ]
        return pl.pallas_call(
            kernel,
            out_shape=tuple(jax.ShapeDtypeStruct(o.shape, o.dtype) for o in outs),
            in_specs=[pl.BlockSpec(memory_space=space) for space in spaces],
            out_specs=tuple(
                pl.BlockSpec(memory_space=pl.ANY if far_out else pltpu.VMEM) for _ in outs
            ),
            scratch_shapes=scratch,
            input_output_aliases=aliases or {},
            compiler_params=pltpu.CompilerParams(vmem_limit_bytes=vmem),
            cost_estimate=pl.CostEstimate(flops=flops, bytes_accessed=moved, transcendentals=0),
        )(*args)

    return run


def body(tokens, cotangent, routes, gates, w_gate, w_up, w_down):
    tok_rows, width = tokens.shape
    top_count = routes.shape[1]
    parts, experts = lax.axis_size("dp"), lax.axis_size("expert")
    hidden = w_gate.shape[2]
    capacity = max(2, 3 * tok_rows * top_count // (2 * experts))
    rows_per_lane = 2 * capacity
    slots = experts // 2 * rows_per_lane
    axes = ("dp", "expert")

    def device(g, j):
        return g * experts + j

    sets = experts // parts // 2

    def home(e, c):
        return device((e + 1) % parts, e // parts * parts + c)

    swap = [(device(g, e), home(e, g)) for g in range(parts) for e in range(experts)]
    across = [(j, (j + experts // 2) % experts) for j in range(experts)]
    planes = [
        [
            [[device(g, parts * (half * sets + q) + c) for q in range(sets)] for g in range(parts)]
            for half in range(2)
        ]
        for c in range(parts)
    ]
    everywhere = [[d for plane in half for d in plane] for c in planes for half in c]
    in_plane = [plane for c in planes for half in c for plane in half]

    def swapped(weight):
        return lax.ppermute(weight[0], axes, swap)

    def whole_expert(own):
        held = [own]
        for step in range(1, parts):
            turn = [(j, j // parts * parts + (j + step) % parts) for j in range(experts)]
            held.append(lax.ppermute(own, "expert", turn))
        return held

    def dispatch(rows, after=()):
        rows = rows.reshape(sets, parts * rows_per_lane, width)
        rows = lax.all_to_all(rows, axes, 0, 0, axis_index_groups=in_plane, tiled=True)
        cut = call(
            functools.partial(cut_kernel, parts),
            [jax.ShapeDtypeStruct((sets, rows_per_lane, width), BF16)] * parts,
            0,
            [sems(parts * sets)],
            far=range(1 + len(after)),
            far_out=True,
        )(rows.reshape(sets, parts, rows_per_lane, width), *after)
        crossed = []
        for i, rows in enumerate(cut):
            rows = rows.reshape(sets * rows_per_lane, width)
            if i > 0:
                rows = lax.ppermute(rows, "dp", [(g, (g + i) % parts) for g in range(parts)])
            crossed.append(rows)
        return crossed

    def send_back(rows):
        rows = rows.reshape(sets * parts, rows_per_lane, width)
        return lax.all_to_all(
            rows, axes, 0, 0, axis_index_groups=everywhere, tiled=True
        ).reshape(slots, width)

    spread_flops = 2 * slots * tok_rows * width
    dot_flops = 2 * slots * width * hidden * parts
    slot_shape = jax.ShapeDtypeStruct((slots, width), BF16)
    place_shape = jax.ShapeDtypeStruct((2, top_count, tok_rows, slots), BF16)
    near_shape = jax.ShapeDtypeStruct((2, tok_rows, slots), BF16)
    joined = hidden % 128 == 0
    units, span = (1, parts * hidden) if joined else (parts, hidden)
    unit_shape = jax.ShapeDtypeStruct((units, slots, span), F32)
    hidden_shape = jax.ShapeDtypeStruct((units, slots, span), BF16)
    sum_shape = jax.ShapeDtypeStruct((tok_rows, width), F32)
    token_shape = jax.ShapeDtypeStruct((tok_rows, width), BF16)
    gate_shape = jax.ShapeDtypeStruct(gates.shape, F32)
    hidden_scratch = pltpu.VMEM((units, slots, span), BF16)
    unit_scratch = pltpu.VMEM((units, slots, span), F32)
    row_scratch = pltpu.VMEM((slots, width), BF16)
    in_scratch = pltpu.VMEM((units, width, span), BF16)
    down_scratch = pltpu.VMEM((units, span, width), BF16)
    pieces = len(tiles(width))

    def sems(number):
        return pltpu.SemaphoreType.DMA((number,))

    def far_side(array):
        return lax.ppermute(array, "expert", across)

    far_routes, far_tokens = far_side(routes), far_side(tokens)
    gate_own, up_own, down_own = swapped(w_gate), swapped(w_up), swapped(w_down)
    far_cotangent, far_gates = far_side(cotangent), far_side(gates)
    gate_w, up_w, down_w = whole_expert(gate_own), whole_expert(up_own), whole_expert(down_own)
    plane = lax.axis_index("dp").astype(jnp.int32).reshape(1)
    first_set = (lax.axis_index("expert") // (experts // 2) * sets).astype(jnp.int32).reshape(1)
    x_slots, place, near = call(
        functools.partial(place_kernel, sets, parts),
        [slot_shape, place_shape, near_shape],
        2 * spread_flops,
    )(jnp.concatenate([plane, first_set]), routes, far_routes, tokens, far_tokens)
    x_shares = dispatch(x_slots)
    (dy_slots,) = call(spread_kernel, [slot_shape], 2 * spread_flops)(
        near, cotangent, far_cotangent
    )
    hidden_rows, by_gate, by_up = call(
        functools.partial(hidden_kernel, parts, joined),
        [hidden_shape, unit_shape, unit_shape],
        2 * dot_flops,
        [sems(3 * parts), sems(3), hidden_scratch, unit_scratch, unit_scratch, row_scratch]
        + [in_scratch] * 2,
        far=range(1, 1 + 3 * parts),
        far_out=True,
        vmem=LARGE_VMEM,
    )(plane, *x_shares, *gate_w, *up_w)
    (out_rows,) = call(
        functools.partial(out_kernel, parts, joined),
        [slot_shape],
        dot_flops,
        [sems(1 + pieces * parts), sems(pieces), row_scratch, hidden_scratch, down_scratch],
        far=range(1 + parts),
        far_out=True,
    )(hidden_rows, *down_w)
    dy_shares = dispatch(dy_slots, (out_rows,))
    out_slots = send_back(out_rows)
    (grad_rows,) = call(
        functools.partial(backward_kernel, parts, joined),
        [slot_shape],
        64 * dot_flops,
        [sems(2 + 4 * parts), sems(pieces), hidden_scratch, hidden_scratch]
        + [row_scratch, row_scratch, down_scratch, unit_scratch, unit_scratch]
        + [in_scratch] * 2,
        far=range(1, 3 + 4 * parts),
        far_out=True,
        vmem=LARGE_VMEM,
    )(plane, *dy_shares, *down_w, by_gate, by_up, *gate_w, *up_w)
    grad_slots = send_back(grad_rows)
    def combine(block, slot_rows, gates, outs, *cotangent):
        return call(functools.partial(combine_kernel, block), outs, 2 * spread_flops)(
            place, gates, slot_rows, *cotangent
        )

    far_sum, far_grad = combine(1, out_slots, far_gates, [token_shape, gate_shape], far_cotangent)
    far_sum, far_grad = far_side(far_sum), far_side(far_grad)
    own_sum, own_grad = combine(0, out_slots, gates, [sum_shape, gate_shape], cotangent)
    mixed = (own_sum + far_sum.astype(F32)).astype(BF16)
    gate_grad = own_grad + far_grad
    (far_sum,) = combine(1, grad_slots, far_gates, [token_shape])
    far_sum = far_side(far_sum)
    (own_sum,) = combine(0, grad_slots, gates, [sum_shape])
    token_grad = (own_sum + far_sum.astype(F32)).astype(BF16)
    return (mixed, token_grad, gate_grad)


def solution(mesh):
    rows, weights = P(("dp", "expert"), None), P("expert", None, "dp")
    return jax.shard_map(
        body,
        mesh=mesh,
        in_specs=(rows, rows, rows, rows, weights, weights, P("expert", "dp", None)),
        out_specs=(rows, rows, rows),
        check_vma=False,
    )
```

```python
import functools

import jax
import jax.numpy as jnp
from jax import lax
from jax.experimental import pallas as pl
from jax.experimental.pallas import tpu as pltpu
from jax.sharding import PartitionSpec as P

BF16 = jnp.bfloat16
F32 = jnp.float32
SMALL_VMEM, LARGE_VMEM = 12 << 20, 60 << 20


def dot(a, b, dims):
    return lax.dot_general(a, b, ((dims[:1], dims[1:]), ((), ())), preferred_element_type=F32)


def tiles(width):
    tile = min(512, width)
    return [slice(d, d + tile) for d in range(0, width, tile)]


def fetch(sources, targets, sems):
    copies = [pltpu.make_async_copy(s, t, sems.at[i]) for i, (s, t) in enumerate(zip(sources, targets))]
    for copy in copies:
        copy.start()
    return copies


def store(stage_ref, out_ref, sem):
    copy = pltpu.make_async_copy(stage_ref, out_ref, sem)
    copy.start()
    return copy


def shares(unit_ref, parts, joined, axis=1):
    if not joined:
        return [unit_ref.at[i] for i in range(parts)]
    size = unit_ref.shape[1 + axis] // parts
    cuts = [pl.ds(i * size, size) for i in range(parts)]
    return [unit_ref.at[0, cut] if axis == 0 else unit_ref.at[0, :, cut] for cut in cuts]


def place_kernel(sets, parts, here_ref, *refs):
    route_refs, token_refs, (slots_ref, place_ref, near_ref) = refs[:2], refs[2:4], refs[4:]
    slots, width = slots_ref.shape
    capacity = slots // (2 * sets * parts)
    tok_rows, top_count = route_refs[0].shape[0], route_refs[0].shape[1] // 2
    earlier = (
        lax.broadcasted_iota(jnp.int32, (tok_rows, tok_rows), 1)
        < lax.broadcasted_iota(jnp.int32, (tok_rows, tok_rows), 0)
    ).astype(BF16)
    slot_numbers = lax.broadcasted_iota(jnp.int32, (tok_rows, slots), 1)
    for block, route_ref in enumerate(route_refs):
        routes = route_ref[:, :top_count].astype(jnp.int32)
        home_plane, home_set = lax.rem(routes + 1, parts), lax.div(routes, parts) - here_ref[1]
        inside = (home_set >= 0) & (home_set < sets)
        back = home_plane * sets + home_set
        out = home_set * parts + lax.rem(home_plane + (parts - here_ref[0]), parts)
        numbers = lax.broadcasted_iota(jnp.int32, (tok_rows, 2 * sets * parts), 1)
        named = [numbers == routes[:, k : k + 1] for k in range(top_count)]
        chosen = sum(n.astype(F32) for n in named)
        rank = dot(earlier, chosen.astype(BF16), (1, 0))
        near = None
        for k in range(top_count):
            own = jnp.sum(jnp.where(named[k], rank, 0.0), axis=1, keepdims=True).astype(jnp.int32)
            own = own + block * capacity
            mark, near_mark = (
                (
                    slot_numbers
                    == jnp.where(
                        inside[:, k : k + 1], lane[:, k : k + 1] * (2 * capacity) + own, slots
                    )
                ).astype(F32)
                for lane in (back, out)
            )
            place_ref[block, k] = mark.astype(BF16)
            near = near_mark if near is None else near + near_mark
        near_ref[block] = near.astype(BF16)
    for columns in tiles(width):
        slots_ref[:, columns] = sum(
            dot(near_ref[block], token_refs[block][:, columns], (0, 0)) for block in range(2)
        ).astype(BF16)


def spread_kernel(near_ref, *refs):
    row_refs, slots_ref = refs[:2], refs[-1]
    for columns in tiles(slots_ref.shape[1]):
        slots_ref[:, columns] = sum(
            dot(near_ref[block], row_refs[block][:, columns], (0, 0)) for block in range(2)
        ).astype(BF16)


def cut_kernel(parts, rows_ref, *refs):
    out_refs, sems = refs[-1 - parts : -1], refs[-1]
    sets = rows_ref.shape[0]
    for copy in fetch(
        [rows_ref.at[q, i] for i in range(parts) for q in range(sets)],
        [out_refs[i].at[q] for i in range(parts) for q in range(sets)],
        sems,
    ):
        copy.wait()


def by_plane(rows_ref, plane_ref, parts):
    size = rows_ref.shape[0] // parts
    starts = [lax.rem(plane_ref[0] + (parts - i), parts) * size for i in range(parts)]
    return [rows_ref.at[pl.ds(pl.multiple_of(start, size), size)] for start in starts]


def hidden_kernel(parts, joined, plane_ref, *refs):
    sources, refs = refs[: 3 * parts], refs[3 * parts :]
    outs, (sems, out_sems), refs = refs[:3], refs[3:5], refs[5:]
    hidden_ref, by_gate_ref, by_up_ref, rows_ref, gate_ref, up_ref = refs
    gate, up = shares(gate_ref, parts, joined), shares(up_ref, parts, joined)
    copies = fetch(sources, [*by_plane(rows_ref, plane_ref, parts), *gate, *up], sems)
    for copy in copies[: 2 * parts]:
        copy.wait()
    for i in range(gate_ref.shape[0]):
        pre_gate = dot(rows_ref[...], gate_ref[i], (1, 0))
        if i == 0:
            for copy in copies[2 * parts :]:
                copy.wait()
        pre_up = dot(rows_ref[...], up_ref[i], (1, 0))
        sig = jax.nn.sigmoid(pre_gate)
        act = pre_gate * sig
        hidden_ref[i] = (act * pre_up).astype(BF16)
        by_gate_ref[i] = pre_up * sig * (1.0 + pre_gate * (1.0 - sig))
        by_up_ref[i] = act
    for copy in fetch([hidden_ref, by_gate_ref, by_up_ref], outs, out_sems):
        copy.wait()


def out_kernel(parts, joined, hidden_ref, *refs):
    sources, refs = refs[:parts], refs[parts:]
    out_ref, sems, out_sems, stage_ref, hidden_stage, down_ref = refs
    down = shares(down_ref, parts, joined, 0)
    pieces = tiles(out_ref.shape[1])
    (first,) = fetch([hidden_ref], [hidden_stage], sems)
    copies = [
        fetch(
            [source.at[:, columns] for source in sources],
            [share.at[:, columns] for share in down],
            sems.at[pl.ds(1 + d * parts, parts)],
        )
        for d, columns in enumerate(pieces)
    ]
    first.wait()
    sent = []
    for d, columns in enumerate(pieces):
        for copy in copies[d]:
            copy.wait()
        stage_ref[:, columns] = sum(
            dot(hidden_stage[i], down_ref[i, :, columns], (1, 0)) for i in range(down_ref.shape[0])
        ).astype(BF16)
        sent.append(store(stage_ref.at[:, columns], out_ref.at[:, columns], out_sems.at[d]))
    for copy in sent:
        copy.wait()


def backward_kernel(parts, joined, plane_ref, _, *refs):
    sources, refs = refs[: 2 + 4 * parts], refs[2 + 4 * parts :]
    out_ref, sems, out_sems, back_gate_ref, back_up_ref, stage_ref, rows_ref = refs[:7]
    down_ref, by_gate_ref, by_up_ref, gate_ref, up_ref = refs[7:]
    down, gate, up = (
        shares(down_ref, parts, joined, 0),
        shares(gate_ref, parts, joined),
        shares(up_ref, parts, joined),
    )
    copies = fetch(sources, [*by_plane(rows_ref, plane_ref, parts), *down, by_gate_ref, by_up_ref, *gate, *up], sems)
    for copy in copies[: 2 + 2 * parts]:
        copy.wait()
    for i in range(down_ref.shape[0]):
        back_hidden = dot(rows_ref[...], down_ref[i], (1, 1))
        back_gate_ref[i] = (back_hidden * by_gate_ref[i]).astype(BF16)
        back_up_ref[i] = (back_hidden * by_up_ref[i]).astype(BF16)
    for copy in copies[2 + 2 * parts :]:
        copy.wait()
    sent = []
    for d, columns in enumerate(tiles(out_ref.shape[1])):
        stage_ref[:, columns] = sum(
            dot(back_gate_ref[i], gate_ref[i, columns, :], (1, 1))
            + dot(back_up_ref[i], up_ref[i, columns, :], (1, 1))
            for i in range(down_ref.shape[0])
        ).astype(BF16)
        sent.append(store(stage_ref.at[:, columns], out_ref.at[:, columns], out_sems.at[d]))
    for copy in sent:
        copy.wait()


def combine_kernel(block, place_ref, gates_ref, slots_ref, *refs):
    cotangent_ref, refs = (refs[0], refs[1:]) if len(refs) == 3 else (None, refs)
    total, grads = None, []
    top_count = gates_ref.shape[1] // 2
    for k in range(top_count):
        raw = dot(place_ref[block, k], slots_ref[...], (1, 0))
        if cotangent_ref is not None:
            grads.append(jnp.sum(raw * cotangent_ref[...].astype(F32), axis=1, keepdims=True))
        term = raw * gates_ref[:, top_count + k : top_count + k + 1]
        total = term if total is None else total + term
    refs[0][...] = total.astype(refs[0].dtype)
    if grads:
        refs[1][...] = jnp.concatenate(grads, axis=1)


def finish_kernel(own_ref, far_ref, own_grad_ref, far_grad_ref, _, sum_ref, grad_ref):
    sum_ref[...] = (own_ref[...] + far_ref[...].astype(F32)).astype(BF16)
    grad_ref[...] = own_grad_ref[...] + far_grad_ref[...]


def call(kernel, outs, flops, scratch=(), far=(), far_out=False, vmem=SMALL_VMEM, aliases=None):
    def run(*args):
        moved = sum(a.size * a.dtype.itemsize for a in (*args, *outs))
        spaces = [
            pltpu.SMEM if a.ndim == 1 else pl.ANY if i in far else pltpu.VMEM
            for i, a in enumerate(args)
        ]
        return pl.pallas_call(
            kernel,
            out_shape=tuple(jax.ShapeDtypeStruct(o.shape, o.dtype) for o in outs),
            in_specs=[pl.BlockSpec(memory_space=space) for space in spaces],
            out_specs=tuple(
                pl.BlockSpec(memory_space=pl.ANY if far_out else pltpu.VMEM) for _ in outs
            ),
            scratch_shapes=scratch,
            input_output_aliases=aliases or {},
            compiler_params=pltpu.CompilerParams(vmem_limit_bytes=vmem),
            cost_estimate=pl.CostEstimate(flops=flops, bytes_accessed=moved, transcendentals=0),
        )(*args)

    return run


def body(tokens, cotangent, routes, gates, w_gate, w_up, w_down):
    tok_rows, width = tokens.shape
    top_count = routes.shape[1]
    parts, experts = lax.axis_size("dp"), lax.axis_size("expert")
    hidden = w_gate.shape[2]
    capacity = max(2, 3 * tok_rows * top_count // (2 * experts))
    rows_per_lane = 2 * capacity
    slots = experts // 2 * rows_per_lane
    axes = ("dp", "expert")

    def device(g, j):
        return g * experts + j

    sets = experts // parts // 2

    def home(e, c):
        return device((e + 1) % parts, e // parts * parts + c)

    swap = [(device(g, e), home(e, g)) for g in range(parts) for e in range(experts)]
    across = [(j, (j + experts // 2) % experts) for j in range(experts)]
    planes = [
        [
            [[device(g, parts * (half * sets + q) + c) for q in range(sets)] for g in range(parts)]
            for half in range(2)
        ]
        for c in range(parts)
    ]
    everywhere = [[d for plane in half for d in plane] for c in planes for half in c]
    in_plane = [plane for c in planes for half in c for plane in half]

    def swapped(weight):
        return lax.ppermute(weight[0], axes, swap)

    def whole_expert(own):
        held = [own]
        for step in range(1, parts):
            turn = [(j, j // parts * parts + (j + step) % parts) for j in range(experts)]
            held.append(lax.ppermute(own, "expert", turn))
        return held

    def dispatch(rows):
        rows = rows.reshape(sets, parts * rows_per_lane, width)
        rows = lax.all_to_all(rows, axes, 0, 0, axis_index_groups=in_plane, tiled=True)
        cut = call(
            functools.partial(cut_kernel, parts),
            [jax.ShapeDtypeStruct((sets, rows_per_lane, width), BF16)] * parts,
            0,
            [sems(parts * sets)],
            far=(0,),
            far_out=True,
        )(rows.reshape(sets, parts, rows_per_lane, width))
        crossed = []
        for i, rows in enumerate(cut):
            rows = rows.reshape(sets * rows_per_lane, width)
            if i > 0:
                rows = lax.ppermute(rows, "dp", [(g, (g + i) % parts) for g in range(parts)])
            crossed.append(rows)
        return crossed

    def send_back(rows):
        rows = rows.reshape(sets * parts, rows_per_lane, width)
        return lax.all_to_all(
            rows, axes, 0, 0, axis_index_groups=everywhere, tiled=True
        ).reshape(slots, width)

    spread_flops = 2 * slots * tok_rows * width
    dot_flops = 2 * slots * width * hidden * parts
    slot_shape = jax.ShapeDtypeStruct((slots, width), BF16)
    place_shape = jax.ShapeDtypeStruct((2, top_count, tok_rows, slots), BF16)
    near_shape = jax.ShapeDtypeStruct((2, tok_rows, slots), BF16)
    joined = hidden % 128 == 0
    units, span = (1, parts * hidden) if joined else (parts, hidden)
    unit_shape = jax.ShapeDtypeStruct((units, slots, span), F32)
    hidden_shape = jax.ShapeDtypeStruct((units, slots, span), BF16)
    sum_shape = jax.ShapeDtypeStruct((tok_rows, width), F32)
    token_shape = jax.ShapeDtypeStruct((tok_rows, width), BF16)
    gate_shape = jax.ShapeDtypeStruct(gates.shape, F32)
    hidden_scratch = pltpu.VMEM((units, slots, span), BF16)
    unit_scratch = pltpu.VMEM((units, slots, span), F32)
    row_scratch = pltpu.VMEM((slots, width), BF16)
    in_scratch = pltpu.VMEM((units, width, span), BF16)
    down_scratch = pltpu.VMEM((units, span, width), BF16)
    pieces = len(tiles(width))

    def sems(number):
        return pltpu.SemaphoreType.DMA((number,))

    def far_side(array):
        return lax.ppermute(array, "expert", across)

    choices = jnp.concatenate([routes.astype(F32), gates], axis=1)
    far_choices, far_tokens = far_side(choices), far_side(tokens)
    gate_own, up_own, down_own = swapped(w_gate), swapped(w_up), swapped(w_down)
    far_cotangent = far_side(cotangent)
    gate_w, up_w, down_w = whole_expert(gate_own), whole_expert(up_own), whole_expert(down_own)
    plane = lax.axis_index("dp").astype(jnp.int32).reshape(1)
    first_set = (lax.axis_index("expert") // (experts // 2) * sets).astype(jnp.int32).reshape(1)
    x_slots, place, near = call(
        functools.partial(place_kernel, sets, parts),
        [slot_shape, place_shape, near_shape],
        2 * spread_flops,
    )(jnp.concatenate([plane, first_set]), choices, far_choices, tokens, far_tokens)
    x_shares = dispatch(x_slots)
    (dy_slots,) = call(spread_kernel, [slot_shape], 256 * spread_flops, far=(3, 4))(
        near, cotangent, far_cotangent, gate_own, up_own
    )
    hidden_rows, by_gate, by_up = call(
        functools.partial(hidden_kernel, parts, joined),
        [hidden_shape, unit_shape, unit_shape],
        2 * dot_flops,
        [sems(3 * parts), sems(3), hidden_scratch, unit_scratch, unit_scratch, row_scratch]
        + [in_scratch] * 2,
        far=range(1, 1 + 3 * parts),
        far_out=True,
        vmem=LARGE_VMEM,
    )(plane, *x_shares, *gate_w, *up_w)
    (out_rows,) = call(
        functools.partial(out_kernel, parts, joined),
        [slot_shape],
        dot_flops,
        [sems(1 + pieces * parts), sems(pieces), row_scratch, hidden_scratch, down_scratch],
        far=range(1 + parts),
        far_out=True,
    )(hidden_rows, *down_w)
    dy_shares = dispatch(dy_slots)
    out_slots = send_back(out_rows)
    (grad_rows,) = call(
        functools.partial(backward_kernel, parts, joined),
        [slot_shape],
        64 * dot_flops,
        [sems(2 + 4 * parts), sems(pieces), hidden_scratch, hidden_scratch]
        + [row_scratch, row_scratch, down_scratch, unit_scratch, unit_scratch]
        + [in_scratch] * 2,
        far=range(1, 4 + 4 * parts),
        far_out=True,
        vmem=LARGE_VMEM,
    )(plane, out_rows, *dy_shares, *down_w, by_gate, by_up, *gate_w, *up_w)
    grad_slots = send_back(grad_rows)
    def combine(block, slot_rows, gates, outs, *cotangent):
        return call(functools.partial(combine_kernel, block), outs, 2 * spread_flops)(
            place, gates, slot_rows, *cotangent
        )

    far_out, far_grad = combine(
        1, out_slots, far_choices, [token_shape, gate_shape], far_cotangent
    )
    far_out, far_grad = far_side(far_out), far_side(far_grad)
    own_out, own_grad = combine(0, out_slots, choices, [sum_shape, gate_shape], cotangent)
    (far_sum,) = combine(1, grad_slots, far_choices, [token_shape])
    mixed, gate_grad = call(finish_kernel, [token_shape, gate_shape], 0, far=(4,))(
        own_out, far_out, own_grad, far_grad, far_sum
    )
    far_sum = far_side(far_sum)
    (own_sum,) = combine(0, grad_slots, choices, [sum_shape])
    token_grad = (own_sum + far_sum.astype(F32)).astype(BF16)
    return (mixed, token_grad, gate_grad)


def solution(mesh):
    rows, weights = P(("dp", "expert"), None), P("expert", None, "dp")
    return jax.shard_map(
        body,
        mesh=mesh,
        in_specs=(rows, rows, rows, rows, weights, weights, P("expert", "dp", None)),
        out_specs=(rows, rows, rows),
        check_vma=False,
    )
```

```python
import functools

import jax
import jax.numpy as jnp
from jax import lax
from jax.experimental import pallas as pl
from jax.experimental.pallas import tpu as pltpu
from jax.sharding import PartitionSpec as P

BF16 = jnp.bfloat16
F32 = jnp.float32
SMALL_VMEM, LARGE_VMEM = 12 << 20, 60 << 20


def dot(a, b, dims):
    return lax.dot_general(a, b, ((dims[:1], dims[1:]), ((), ())), preferred_element_type=F32)


def tiles(width):
    tile = min(512, width)
    return [slice(d, d + tile) for d in range(0, width, tile)]


def fetch(sources, targets, sems):
    copies = [pltpu.make_async_copy(s, t, sems.at[i]) for i, (s, t) in enumerate(zip(sources, targets))]
    for copy in copies:
        copy.start()
    return copies


def store(stage_ref, out_ref, sem):
    copy = pltpu.make_async_copy(stage_ref, out_ref, sem)
    copy.start()
    return copy


def shares(unit_ref, parts, joined, axis=1):
    if not joined:
        return [unit_ref.at[i] for i in range(parts)]
    size = unit_ref.shape[1 + axis] // parts
    cuts = [pl.ds(i * size, size) for i in range(parts)]
    return [unit_ref.at[0, cut] if axis == 0 else unit_ref.at[0, :, cut] for cut in cuts]


def place_kernel(experts, parts, plane_ref, routes_ref, tokens_ref, slots_ref, place_ref, near_ref):
    slots, width = slots_ref.shape
    capacity = slots // experts
    tok_rows, top_count = routes_ref.shape
    routes = routes_ref[...]
    home_plane, home_set = lax.rem(routes + 1, parts), lax.div(routes, parts)
    lanes = home_plane * (experts // parts) + home_set
    near_lanes = home_set * parts + lax.rem(home_plane + (parts - plane_ref[0]), parts)
    numbers = lax.broadcasted_iota(jnp.int32, (tok_rows, experts), 1)
    named = [numbers == routes[:, k : k + 1] for k in range(top_count)]
    chosen = sum(n.astype(F32) for n in named)
    earlier = (
        lax.broadcasted_iota(jnp.int32, (tok_rows, tok_rows), 1)
        < lax.broadcasted_iota(jnp.int32, (tok_rows, tok_rows), 0)
    ).astype(F32)
    rank = dot(earlier.astype(BF16), chosen.astype(BF16), (1, 0))
    slot_numbers = lax.broadcasted_iota(jnp.int32, (tok_rows, slots), 1)
    near = None
    for k in range(top_count):
        own = jnp.sum(jnp.where(named[k], rank, 0.0), axis=1, keepdims=True).astype(jnp.int32)
        mark, near_mark = (
            (slot_numbers == order[:, k : k + 1] * capacity + own).astype(F32)
            for order in (lanes, near_lanes)
        )
        place_ref[k * tok_rows : (k + 1) * tok_rows, :] = mark.astype(BF16)
        near = near_mark if near is None else near + near_mark
    near = near.astype(BF16)
    near_ref[...] = near
    for columns in tiles(width):
        slots_ref[:, columns] = dot(near, tokens_ref[:, columns], (0, 0)).astype(BF16)


def spread_kernel(near_ref, rows_ref, _, slots_ref):
    for columns in tiles(rows_ref.shape[1]):
        slots_ref[:, columns] = dot(near_ref[...], rows_ref[:, columns], (0, 0)).astype(BF16)


def cut_kernel(parts, rows_ref, *refs):
    out_refs, sems = refs[-1 - parts : -1], refs[-1]
    sets = rows_ref.shape[0]
    for copy in fetch(
        [rows_ref.at[q, i] for i in range(parts) for q in range(sets)],
        [out_refs[i].at[q] for i in range(parts) for q in range(sets)],
        sems,
    ):
        copy.wait()


def by_plane(rows_ref, plane_ref, parts):
    size = rows_ref.shape[0] // parts
    starts = [lax.rem(plane_ref[0] + (parts - i), parts) * size for i in range(parts)]
    return [rows_ref.at[pl.ds(pl.multiple_of(start, size), size)] for start in starts]


def chunks(span):
    size = 256 if span % 256 == 0 else span
    return [pl.ds(start, size) for start in range(0, span, size)]


def forward_kernel(parts, joined, plane_ref, *refs):
    sources, outs, refs = refs[: 4 * parts], refs[4 * parts : 4 * parts + 3], refs[4 * parts + 3 :]
    sems, out_sems, rows_ref, gate_ref, up_ref, down_ref = refs[:6]
    stage_ref, hidden_ref, by_gate_ref, by_up_ref = refs[6:]
    units, span = gate_ref.shape[0], gate_ref.shape[2]
    targets = [
        *by_plane(rows_ref, plane_ref, parts),
        *shares(gate_ref, parts, joined),
        *shares(up_ref, parts, joined),
        *shares(down_ref, parts, joined, 0),
    ]
    copies = fetch(sources, targets, sems)
    for copy in copies[: 3 * parts]:
        copy.wait()
    for i in range(units):
        for cut in chunks(span):
            pre_gate = dot(rows_ref[...], gate_ref[i, :, cut], (1, 0))
            pre_up = dot(rows_ref[...], up_ref[i, :, cut], (1, 0))
            sig = 0.5 + 0.5 * jnp.tanh(0.5 * pre_gate)
            act = pre_gate * sig
            hidden_ref[i, :, cut] = (act * pre_up).astype(BF16)
            by_gate_ref[i, :, cut] = pre_up * (sig + act * (1.0 - sig))
            by_up_ref[i, :, cut] = act
    sent = fetch([by_gate_ref, by_up_ref], outs[1:], out_sems)
    for copy in copies[3 * parts :]:
        copy.wait()
    for d, columns in enumerate(tiles(stage_ref.shape[1])):
        stage_ref[:, columns] = sum(
            dot(hidden_ref[i], down_ref[i, :, columns], (1, 0)) for i in range(units)
        ).astype(BF16)
        sent.append(store(stage_ref.at[:, columns], outs[0].at[:, columns], out_sems.at[2 + d]))
    for copy in sent:
        copy.wait()


def backward_kernel(parts, joined, plane_ref, *refs):
    sources, refs = refs[: 2 + 4 * parts], refs[2 + 4 * parts :]
    out_ref, sems, out_sems, rows_ref, down_ref, by_gate_ref, by_up_ref, gate_ref, up_ref = refs[:9]
    stage_ref, back_gate_ref, back_up_ref = refs[9:]
    units, span = down_ref.shape[:2]
    targets = [
        *by_plane(rows_ref, plane_ref, parts),
        *shares(down_ref, parts, joined, 0),
        by_gate_ref,
        by_up_ref,
        *shares(gate_ref, parts, joined),
        *shares(up_ref, parts, joined),
    ]
    copies = fetch(sources, targets, sems)
    for copy in copies[: 2 + 2 * parts]:
        copy.wait()
    for i in range(units):
        for cut in chunks(span):
            back_hidden = dot(rows_ref[...], down_ref[i, cut, :], (1, 1))
            back_gate_ref[i, :, cut] = (back_hidden * by_gate_ref[i, :, cut]).astype(BF16)
            back_up_ref[i, :, cut] = (back_hidden * by_up_ref[i, :, cut]).astype(BF16)
    for copy in copies[2 + 2 * parts :]:
        copy.wait()
    sent = []
    for d, columns in enumerate(tiles(stage_ref.shape[1])):
        stage_ref[:, columns] = sum(
            dot(back_gate_ref[i], gate_ref[i, columns, :], (1, 1))
            + dot(back_up_ref[i], up_ref[i, columns, :], (1, 1))
            for i in range(units)
        ).astype(BF16)
        sent.append(store(stage_ref.at[:, columns], out_ref.at[:, columns], out_sems.at[d]))
    for copy in sent:
        copy.wait()


def mix_kernel(place_ref, gates_ref, cotangent_ref, slots_ref, mixed_ref, gate_grad_ref):
    tok_rows, top_count = gates_ref.shape
    total, grads = None, []
    for k in range(top_count):
        raw = dot(place_ref[k * tok_rows : (k + 1) * tok_rows, :], slots_ref[...], (1, 0))
        grads.append(jnp.sum(raw * cotangent_ref[...].astype(F32), axis=1, keepdims=True))
        term = raw * gates_ref[:, k : k + 1]
        total = term if total is None else total + term
    mixed_ref[...] = total.astype(BF16)
    gate_grad_ref[...] = jnp.concatenate(grads, axis=1)


def sum_kernel(place_ref, gates_ref, slots_ref, out_ref):
    tok_rows, top_count = gates_ref.shape
    total = None
    for k in range(top_count):
        raw = dot(place_ref[k * tok_rows : (k + 1) * tok_rows, :], slots_ref[...], (1, 0))
        term = raw * gates_ref[:, k : k + 1]
        total = term if total is None else total + term
    out_ref[...] = total.astype(BF16)


def call(kernel, outs, flops, scratch=(), far=(), far_out=False, vmem=SMALL_VMEM):
    def run(*args):
        moved = sum(a.size * a.dtype.itemsize for a in (*args, *outs))
        spaces = [
            pltpu.SMEM if a.shape == (1,) else pl.ANY if i in far else pltpu.VMEM
            for i, a in enumerate(args)
        ]
        return pl.pallas_call(
            kernel,
            out_shape=tuple(jax.ShapeDtypeStruct(o.shape, o.dtype) for o in outs),
            in_specs=[pl.BlockSpec(memory_space=space) for space in spaces],
            out_specs=tuple(
                pl.BlockSpec(memory_space=pl.ANY if far_out else pltpu.VMEM) for _ in outs
            ),
            scratch_shapes=scratch,
            compiler_params=pltpu.CompilerParams(vmem_limit_bytes=vmem),
            cost_estimate=pl.CostEstimate(flops=flops, bytes_accessed=moved, transcendentals=0),
        )(*args)

    return run


def body(tokens, cotangent, routes, gates, w_gate, w_up, w_down):
    tok_rows, width = tokens.shape
    top_count = routes.shape[1]
    parts, experts = lax.axis_size("dp"), lax.axis_size("expert")
    hidden = w_gate.shape[2]
    capacity = max(2, 3 * tok_rows * top_count // (2 * experts))
    slots = experts * capacity
    axes = ("dp", "expert")

    def device(g, j):
        return g * experts + j

    sets = experts // parts

    def home(e, c):
        return device((e + 1) % parts, e // parts * parts + c)

    swap = [(device(g, e), home(e, g)) for g in range(parts) for e in range(experts)]
    planes = [
        [[device(g, parts * q + c) for q in range(sets)] for g in range(parts)] for c in range(parts)
    ]
    everywhere = [[d for plane in planes[c] for d in plane] for c in range(parts)]
    in_plane = [plane for c in range(parts) for plane in planes[c]]

    def swapped(weight):
        return lax.ppermute(weight[0], axes, swap)

    def whole_expert(own):
        held = [own]
        for step in range(1, parts):
            turn = [(j, j // parts * parts + (j + step) % parts) for j in range(experts)]
            held.append(lax.ppermute(own, "expert", turn))
        return held

    def dispatch(rows, after=()):
        rows = rows.reshape(sets, parts * capacity, width)
        rows = lax.all_to_all(rows, axes, 0, 0, axis_index_groups=in_plane, tiled=True)
        cut = call(
            functools.partial(cut_kernel, parts),
            [jax.ShapeDtypeStruct((sets, capacity, width), BF16)] * parts,
            0,
            [sems(parts * sets)],
            far=range(1 + len(after)),
            far_out=True,
        )(rows.reshape(sets, parts, capacity, width), *after)
        crossed = []
        for i, rows in enumerate(cut):
            rows = rows.reshape(sets * capacity, width)
            if i > 0:
                rows = lax.ppermute(rows, "dp", [(g, (g + i) % parts) for g in range(parts)])
            crossed.append(rows)
        return crossed

    def send_back(rows):
        rows = rows.reshape(experts, capacity, width)
        return lax.all_to_all(
            rows, axes, 0, 0, axis_index_groups=everywhere, tiled=True
        ).reshape(slots, width)

    spread_flops = 2 * slots * tok_rows * width
    dot_flops = 2 * slots * width * hidden * parts
    slot_shape = jax.ShapeDtypeStruct((slots, width), BF16)
    place_shape = jax.ShapeDtypeStruct((top_count * tok_rows, slots), BF16)
    joined = hidden % 128 == 0
    units, span = (1, parts * hidden) if joined else (parts, hidden)
    unit_shape = jax.ShapeDtypeStruct((units, slots, span), F32)
    token_shape = jax.ShapeDtypeStruct((tok_rows, width), BF16)
    hidden_scratch = pltpu.VMEM((units, slots, span), BF16)
    unit_scratch = pltpu.VMEM((units, slots, span), F32)
    row_scratch = pltpu.VMEM((slots, width), BF16)
    in_scratch = pltpu.VMEM((units, width, span), BF16)
    down_scratch = pltpu.VMEM((units, span, width), BF16)
    pieces = len(tiles(width))

    def sems(number):
        return pltpu.SemaphoreType.DMA((number,))

    gate_own, up_own, down_own = swapped(w_gate), swapped(w_up), swapped(w_down)
    gate_w, up_w, down_w = whole_expert(gate_own), whole_expert(up_own), whole_expert(down_own)
    plane = lax.axis_index("dp").astype(jnp.int32).reshape(1)
    x_slots, place, near = call(
        functools.partial(place_kernel, experts, parts),
        [slot_shape, place_shape, jax.ShapeDtypeStruct((tok_rows, slots), BF16)],
        spread_flops,
    )(plane, routes, tokens)
    x_shares = dispatch(x_slots)
    (dy_slots,) = call(spread_kernel, [slot_shape], 256 * spread_flops, far=(2,))(
        near, cotangent, gate_own
    )
    out_rows, by_gate, by_up = call(
        functools.partial(forward_kernel, parts, joined),
        [slot_shape, unit_shape, unit_shape],
        3 * dot_flops,
        [sems(4 * parts), sems(2 + pieces), row_scratch, in_scratch, in_scratch, down_scratch]
        + [row_scratch, hidden_scratch, unit_scratch, unit_scratch],
        far=range(1, 1 + 4 * parts),
        far_out=True,
        vmem=LARGE_VMEM,
    )(plane, *x_shares, *gate_w, *up_w, *down_w)
    dy_shares = dispatch(dy_slots, (out_rows,))
    out_slots = send_back(out_rows)
    (grad_rows,) = call(
        functools.partial(backward_kernel, parts, joined),
        [slot_shape],
        3 * dot_flops,
        [sems(2 + 4 * parts), sems(pieces), row_scratch, down_scratch, unit_scratch, unit_scratch]
        + [in_scratch, in_scratch, row_scratch, hidden_scratch, hidden_scratch],
        far=range(1, 3 + 4 * parts),
        far_out=True,
        vmem=LARGE_VMEM,
    )(plane, *dy_shares, *down_w, by_gate, by_up, *gate_w, *up_w)
    grad_slots = send_back(grad_rows)
    mixed, gate_grad = call(
        mix_kernel, [token_shape, jax.ShapeDtypeStruct(gates.shape, F32)], 2 * spread_flops
    )(place, gates, cotangent, out_slots)
    (token_grad,) = call(sum_kernel, [token_shape], 2 * spread_flops)(place, gates, grad_slots)
    return (mixed, token_grad, gate_grad)


def solution(mesh):
    rows, weights = P(("dp", "expert"), None), P("expert", None, "dp")
    return jax.shard_map(
        body,
        mesh=mesh,
        in_specs=(rows, rows, rows, rows, weights, weights, P("expert", "dp", None)),
        out_specs=(rows, rows, rows),
        check_vma=False,
    )
```

```python
import functools

import jax
import jax.numpy as jnp
from jax import lax
from jax.experimental import pallas as pl
from jax.experimental.pallas import tpu as pltpu
from jax.sharding import PartitionSpec as P

BF16 = jnp.bfloat16
F32 = jnp.float32
SMALL_VMEM, LARGE_VMEM = 12 << 20, 62_300_000


def dot(a, b, dims):
    return lax.dot_general(a, b, ((dims[:1], dims[1:]), ((), ())), preferred_element_type=F32)


def tiles(width):
    tile = min(512, width)
    return [slice(d, d + tile) for d in range(0, width, tile)]


def fetch(sources, targets, sems):
    copies = [pltpu.make_async_copy(s, t, sems.at[i]) for i, (s, t) in enumerate(zip(sources, targets))]
    for copy in copies:
        copy.start()
    return copies


def store(stage_ref, out_ref, sem):
    copy = pltpu.make_async_copy(stage_ref, out_ref, sem)
    copy.start()
    return copy


def shares(unit_ref, parts, joined, axis=1):
    if not joined:
        return [unit_ref.at[i] for i in range(parts)]
    size = unit_ref.shape[1 + axis] // parts
    cuts = [pl.ds(i * size, size) for i in range(parts)]
    return [unit_ref.at[0, cut] if axis == 0 else unit_ref.at[0, :, cut] for cut in cuts]


def place_kernel(experts, parts, plane_ref, routes_ref, tokens_ref, slots_ref, near_ref, *refs):
    place_ref, sems, out_sems, rows_ref, stage_ref = refs
    slots, width = slots_ref.shape
    capacity = slots // experts
    tok_rows, top_count = routes_ref.shape
    (copy,) = fetch([tokens_ref], [rows_ref], sems)
    routes = routes_ref[...]
    home_plane, home_set = lax.rem(routes + 1, parts), lax.div(routes, parts)
    lanes = home_plane * (experts // parts) + home_set
    near_lanes = home_set * parts + lax.rem(home_plane + (parts - plane_ref[0]), parts)
    numbers = lax.broadcasted_iota(jnp.int32, (tok_rows, experts), 1)
    named = [numbers == routes[:, k : k + 1] for k in range(top_count)]
    chosen = sum(n.astype(F32) for n in named)
    earlier = (
        lax.broadcasted_iota(jnp.int32, (tok_rows, tok_rows), 1)
        < lax.broadcasted_iota(jnp.int32, (tok_rows, tok_rows), 0)
    ).astype(F32)
    rank = dot(earlier.astype(BF16), chosen.astype(BF16), (1, 0))
    slot_numbers = lax.broadcasted_iota(jnp.int32, (tok_rows, slots), 1)
    near = None
    for k in range(top_count):
        own = jnp.sum(jnp.where(named[k], rank, 0.0), axis=1, keepdims=True).astype(jnp.int32)
        mark, near_mark = (
            (slot_numbers == order[:, k : k + 1] * capacity + own).astype(F32)
            for order in (lanes, near_lanes)
        )
        place_ref[k * tok_rows : (k + 1) * tok_rows, :] = mark.astype(BF16)
        near = near_mark if near is None else near + near_mark
    near_ref[...] = near.astype(BF16)
    copy.wait()
    spread(near_ref, rows_ref, stage_ref, slots_ref, out_sems)


def spread(near_ref, rows_ref, stage_ref, slots_ref, sems):
    sent = []
    for d, columns in enumerate(tiles(rows_ref.shape[1])):
        stage_ref[:, columns] = dot(near_ref[...], rows_ref[:, columns], (0, 0)).astype(BF16)
        sent.append(store(stage_ref.at[:, columns], slots_ref.at[:, columns], sems.at[d]))
    for copy in sent:
        copy.wait()


def spread_kernel(near_ref, rows_ref, _, slots_ref, out_sems, stage_ref):
    spread(near_ref, rows_ref, stage_ref, slots_ref, out_sems)


def cut_kernel(numbers, rows_ref, *refs):
    out_refs, sems = refs[-1 - len(numbers) : -1], refs[-1]
    sets = rows_ref.shape[0]
    for copy in fetch(
        [rows_ref.at[q, i] for i in numbers for q in range(sets)],
        [out_ref.at[q] for out_ref in out_refs for q in range(sets)],
        sems,
    ):
        copy.wait()


def by_plane(rows_ref, plane_ref, parts):
    size = rows_ref.shape[0] // parts
    starts = [lax.rem(plane_ref[0] + (parts - i), parts) * size for i in range(parts)]
    return [rows_ref.at[pl.ds(pl.multiple_of(start, size), size)] for start in starts]


def chunks(span):
    size = 256 if span % 256 == 0 else span
    return [pl.ds(start, size) for start in range(0, span, size)]


def forward_kernel(parts, joined, plane_ref, *refs):
    sources, outs, refs = refs[: 4 * parts], refs[4 * parts : 4 * parts + 3], refs[4 * parts + 3 :]
    sems, out_sems, rows_ref, gate_ref, up_ref, down_ref = refs[:6]
    stage_ref, hidden_ref, by_gate_ref, by_up_ref = refs[6:]
    units, span = gate_ref.shape[0], gate_ref.shape[2]
    targets = [
        *by_plane(rows_ref, plane_ref, parts),
        *shares(gate_ref, parts, joined),
        *shares(up_ref, parts, joined),
        *shares(down_ref, parts, joined, 0),
    ]
    copies = fetch(sources, targets, sems)
    for copy in copies[: 3 * parts]:
        copy.wait()
    for i in range(units):
        for cut in chunks(span):
            pre_gate = dot(rows_ref[...], gate_ref[i, :, cut], (1, 0))
            pre_up = dot(rows_ref[...], up_ref[i, :, cut], (1, 0))
            sig = 0.5 + 0.5 * jnp.tanh(0.5 * pre_gate)
            act = pre_gate * sig
            hidden_ref[i, :, cut] = (act * pre_up).astype(BF16)
            by_gate_ref[i, :, cut] = pre_up * (sig + act * (1.0 - sig))
            by_up_ref[i, :, cut] = act
    sent = fetch([by_gate_ref, by_up_ref], outs[1:], out_sems)
    for copy in copies[3 * parts :]:
        copy.wait()
    for d, columns in enumerate(tiles(stage_ref.shape[1])):
        stage_ref[:, columns] = sum(
            dot(hidden_ref[i], down_ref[i, :, columns], (1, 0)) for i in range(units)
        ).astype(BF16)
        sent.append(store(stage_ref.at[:, columns], outs[0].at[:, columns], out_sems.at[2 + d]))
    for copy in sent:
        copy.wait()


def backward_kernel(parts, joined, plane_ref, *refs):
    sources, refs = refs[: 2 + 4 * parts], refs[2 + 4 * parts :]
    out_ref, sems, out_sems, rows_ref, down_ref, by_gate_ref, by_up_ref, gate_ref, up_ref = refs[:9]
    stage_ref, back_gate_ref, back_up_ref = refs[9:]
    units, span = down_ref.shape[:2]
    targets = [
        *by_plane(rows_ref, plane_ref, parts),
        *shares(down_ref, parts, joined, 0),
        by_gate_ref,
        by_up_ref,
        *shares(gate_ref, parts, joined),
        *shares(up_ref, parts, joined),
    ]
    copies = fetch(sources, targets, sems)
    for copy in copies[: 2 + 2 * parts]:
        copy.wait()
    for i in range(units):
        for cut in chunks(span):
            back_hidden = dot(rows_ref[...], down_ref[i, cut, :], (1, 1))
            back_gate_ref[i, :, cut] = (back_hidden * by_gate_ref[i, :, cut]).astype(BF16)
            back_up_ref[i, :, cut] = (back_hidden * by_up_ref[i, :, cut]).astype(BF16)
    for copy in copies[2 + 2 * parts :]:
        copy.wait()
    sent = []
    for d, columns in enumerate(tiles(stage_ref.shape[1])):
        stage_ref[:, columns] = sum(
            dot(back_gate_ref[i], gate_ref[i, columns, :], (1, 1))
            + dot(back_up_ref[i], up_ref[i, columns, :], (1, 1))
            for i in range(units)
        ).astype(BF16)
        sent.append(store(stage_ref.at[:, columns], out_ref.at[:, columns], out_sems.at[d]))
    for copy in sent:
        copy.wait()


def mix_kernel(place_ref, gates_ref, cotangent_ref, slots_ref, mixed_ref, gate_grad_ref):
    tok_rows, top_count = gates_ref.shape
    total, grads = None, []
    for k in range(top_count):
        raw = dot(place_ref[k * tok_rows : (k + 1) * tok_rows, :], slots_ref[...], (1, 0))
        grads.append(jnp.sum(raw * cotangent_ref[...].astype(F32), axis=1, keepdims=True))
        term = raw * gates_ref[:, k : k + 1]
        total = term if total is None else total + term
    mixed_ref[...] = total.astype(BF16)
    gate_grad_ref[...] = jnp.concatenate(grads, axis=1)


def sum_kernel(place_ref, gates_ref, slots_ref, out_ref):
    tok_rows, top_count = gates_ref.shape
    total = None
    for k in range(top_count):
        raw = dot(place_ref[k * tok_rows : (k + 1) * tok_rows, :], slots_ref[...], (1, 0))
        term = raw * gates_ref[:, k : k + 1]
        total = term if total is None else total + term
    out_ref[...] = total.astype(BF16)


def call(kernel, outs, flops, scratch=(), far=(), pinned=(), out_spaces=None, vmem=SMALL_VMEM):
    def run(*args):
        moved = sum(a.size * a.dtype.itemsize for a in (*args, *outs))
        spaces = [
            pltpu.SMEM
            if a.shape == (1,)
            else pl.ANY
            if i in far
            else pltpu.HBM
            if i in pinned
            else pltpu.VMEM
            for i, a in enumerate(args)
        ]
        return pl.pallas_call(
            kernel,
            out_shape=tuple(outs),
            in_specs=[pl.BlockSpec(memory_space=space) for space in spaces],
            out_specs=tuple(
                pl.BlockSpec(memory_space=space)
                for space in out_spaces or [pltpu.VMEM] * len(outs)
            ),
            scratch_shapes=scratch,
            compiler_params=pltpu.CompilerParams(vmem_limit_bytes=vmem),
            cost_estimate=pl.CostEstimate(flops=flops, bytes_accessed=moved, transcendentals=0),
        )(*args)

    return run


def body(tokens, cotangent, routes, gates, w_gate, w_up, w_down):
    tok_rows, width = tokens.shape
    top_count = routes.shape[1]
    parts, experts = lax.axis_size("dp"), lax.axis_size("expert")
    hidden = w_gate.shape[2]
    capacity = max(2, 3 * tok_rows * top_count // (2 * experts))
    slots = experts * capacity
    axes = ("dp", "expert")

    def device(g, j):
        return g * experts + j

    sets = experts // parts

    def home(e, c):
        return device((e + 1) % parts, e // parts * parts + c)

    swap = [(device(g, e), home(e, g)) for g in range(parts) for e in range(experts)]
    planes = [
        [[device(g, parts * q + c) for q in range(sets)] for g in range(parts)] for c in range(parts)
    ]
    everywhere = [[d for plane in planes[c] for d in plane] for c in range(parts)]
    in_plane = [plane for c in range(parts) for plane in planes[c]]

    def swapped(weight):
        return lax.ppermute(weight[0], axes, swap)

    def whole_expert(own):
        held = [own]
        for step in range(1, parts):
            turn = [(j, j // parts * parts + (j + step) % parts) for j in range(experts)]
            held.append(lax.ppermute(own, "expert", turn))
        return held

    def dispatch(rows, after=()):
        rows = rows.reshape(sets, parts * capacity, width)
        rows = lax.all_to_all(rows, axes, 0, 0, axis_index_groups=in_plane, tiled=True)
        rows = rows.reshape(sets, parts, capacity, width)

        def cut(numbers, space):
            return call(
                functools.partial(cut_kernel, numbers),
                [jax.ShapeDtypeStruct((sets, capacity, width), BF16)] * len(numbers),
                0,
                [sems(len(numbers) * sets)],
                far=(0,),
                pinned=range(1, 1 + len(after)),
                out_spaces=[space] * len(numbers),
            )(rows, *after)

        leaving = cut(range(1, parts), pl.ANY)
        cuts = [*cut(range(1), pltpu.HBM), *leaving]
        crossed = []
        for i, rows in enumerate(cuts):
            rows = rows.reshape(sets * capacity, width)
            if i > 0:
                rows = lax.ppermute(rows, "dp", [(g, (g + i) % parts) for g in range(parts)])
            crossed.append(rows)
        return crossed

    def send_back(rows):
        rows = rows.reshape(experts, capacity, width)
        return lax.all_to_all(
            rows, axes, 0, 0, axis_index_groups=everywhere, tiled=True
        ).reshape(slots, width)

    spread_flops = 2 * slots * tok_rows * width
    dot_flops = 2 * slots * width * hidden * parts
    slot_shape = jax.ShapeDtypeStruct((slots, width), BF16)
    place_shape = jax.ShapeDtypeStruct((top_count * tok_rows, slots), BF16)
    joined = hidden % 128 == 0
    units, span = (1, parts * hidden) if joined else (parts, hidden)
    unit_shape = jax.ShapeDtypeStruct((units, slots, span), F32)
    token_shape = jax.ShapeDtypeStruct((tok_rows, width), BF16)
    hidden_scratch = pltpu.VMEM((units, slots, span), BF16)
    unit_scratch = pltpu.VMEM((units, slots, span), F32)
    row_scratch = pltpu.VMEM((slots, width), BF16)
    in_scratch = pltpu.VMEM((units, width, span), BF16)
    down_scratch = pltpu.VMEM((units, span, width), BF16)
    pieces = len(tiles(width))

    def sems(number):
        return pltpu.SemaphoreType.DMA((number,))

    gate_own, up_own, down_own = swapped(w_gate), swapped(w_up), swapped(w_down)
    gate_w, up_w, down_w = whole_expert(gate_own), whole_expert(up_own), whole_expert(down_own)
    plane = lax.axis_index("dp").astype(jnp.int32).reshape(1)
    x_slots, near, place = call(
        functools.partial(place_kernel, experts, parts),
        [slot_shape, jax.ShapeDtypeStruct((tok_rows, slots), BF16), place_shape],
        spread_flops,
        [sems(1), sems(pieces), pltpu.VMEM((tok_rows, width), BF16), row_scratch],
        pinned=(2,),
        out_spaces=[pltpu.HBM, pltpu.VMEM, pltpu.VMEM],
    )(plane, routes, tokens)
    x_shares = dispatch(x_slots)
    (dy_slots,) = call(
        spread_kernel,
        [slot_shape],
        256 * spread_flops,
        [sems(pieces), row_scratch],
        pinned=(2,),
        out_spaces=[pltpu.HBM],
    )(near, cotangent, gate_own)
    out_rows, by_gate, by_up = call(
        functools.partial(forward_kernel, parts, joined),
        [slot_shape, unit_shape, unit_shape],
        3 * dot_flops,
        [sems(4 * parts), sems(2 + pieces), row_scratch, in_scratch, in_scratch, down_scratch]
        + [row_scratch, hidden_scratch, unit_scratch, unit_scratch],
        far=range(1, 1 + 4 * parts),
        out_spaces=[pltpu.HBM] * 3,
        vmem=LARGE_VMEM,
    )(plane, *x_shares, *gate_w, *up_w, *down_w)
    dy_shares = dispatch(dy_slots, (out_rows,))
    out_slots = send_back(out_rows)
    (grad_rows,) = call(
        functools.partial(backward_kernel, parts, joined),
        [slot_shape],
        64 * dot_flops,
        [sems(2 + 4 * parts), sems(pieces), row_scratch, down_scratch, unit_scratch, unit_scratch]
        + [in_scratch, in_scratch, row_scratch, hidden_scratch, hidden_scratch],
        far=range(1, 3 + 4 * parts),
        out_spaces=[pltpu.HBM],
        vmem=LARGE_VMEM,
    )(plane, *dy_shares, *down_w, by_gate, by_up, *gate_w, *up_w)
    grad_slots = send_back(grad_rows)
    mixed, gate_grad = call(
        mix_kernel, [token_shape, jax.ShapeDtypeStruct(gates.shape, F32)], 2 * spread_flops
    )(place, gates, cotangent, out_slots)
    (token_grad,) = call(sum_kernel, [token_shape], 2 * spread_flops)(place, gates, grad_slots)
    return (mixed, token_grad, gate_grad)


def solution(mesh):
    rows, weights = P(("dp", "expert"), None), P("expert", None, "dp")
    return jax.shard_map(
        body,
        mesh=mesh,
        in_specs=(rows, rows, rows, rows, weights, weights, P("expert", "dp", None)),
        out_specs=(rows, rows, rows),
        check_vma=False,
    )
```

```python
import functools
import itertools

import jax
import jax.numpy as jnp
from jax import lax
from jax.experimental import pallas as pl
from jax.experimental.pallas import tpu as pltpu
from jax.sharding import PartitionSpec as P

BF16 = jnp.bfloat16
F32 = jnp.float32
SMALL_VMEM, LARGE_VMEM = 12 << 20, 62_300_000


def dot(a, b, dims):
    return lax.dot_general(a, b, ((dims[:1], dims[1:]), ((), ())), preferred_element_type=F32)


def tiles(width):
    tile = min(512, width)
    return [slice(d, d + tile) for d in range(0, width, tile)]


def fetch(sources, targets, sems):
    copies = [pltpu.make_async_copy(s, t, sems.at[i]) for i, (s, t) in enumerate(zip(sources, targets))]
    for copy in copies:
        copy.start()
    return copies


def store(stage_ref, out_ref, sem):
    copy = pltpu.make_async_copy(stage_ref, out_ref, sem)
    copy.start()
    return copy


def shares(unit_ref, parts, joined, axis=1):
    if not joined:
        return [unit_ref.at[i] for i in range(parts)]
    size = unit_ref.shape[1 + axis] // parts
    cuts = [pl.ds(i * size, size) for i in range(parts)]
    return [unit_ref.at[0, cut] if axis == 0 else unit_ref.at[0, :, cut] for cut in cuts]


def place_kernel(experts, parts, plane_ref, spot_ref, routes_ref, tokens_ref, slots_ref, near_ref, *refs):
    place_ref, turned_ref, sems, out_sems, rows_ref, stage_ref = refs
    slots, width = slots_ref.shape
    capacity = slots // experts
    tok_rows, top_count = routes_ref.shape
    (copy,) = fetch([tokens_ref], [rows_ref], sems)
    routes = routes_ref[...]
    home_plane, home_set = lax.rem(routes + 1, parts), lax.div(routes, parts)
    lanes = home_plane * (experts // parts) + home_set
    near_lanes = home_set * parts + lax.rem(home_plane + (parts - plane_ref[0]), parts)
    numbers = lax.broadcasted_iota(jnp.int32, (tok_rows, experts), 1)
    named = [numbers == routes[:, k : k + 1] for k in range(top_count)]
    chosen = sum(n.astype(F32) for n in named)
    earlier = (
        lax.broadcasted_iota(jnp.int32, (tok_rows, tok_rows), 1)
        < lax.broadcasted_iota(jnp.int32, (tok_rows, tok_rows), 0)
    ).astype(F32)
    rank = dot(earlier.astype(BF16), chosen.astype(BF16), (1, 0))
    slot_numbers = lax.broadcasted_iota(jnp.int32, (tok_rows, slots), 1)
    near = None
    for k in range(top_count):
        own = jnp.sum(jnp.where(named[k], rank, 0.0), axis=1, keepdims=True).astype(jnp.int32)
        mark, turned_mark, near_mark = (
            (slot_numbers == order[:, k : k + 1] * capacity + own).astype(F32)
            for order in (lanes, lanes ^ spot_ref[0], near_lanes)
        )
        turned_ref[k * tok_rows : (k + 1) * tok_rows, :] = turned_mark.astype(BF16)
        place_ref[k * tok_rows : (k + 1) * tok_rows, :] = mark.astype(BF16)
        near = near_mark if near is None else near + near_mark
    near_ref[...] = near.astype(BF16)
    copy.wait()
    spread(near_ref, rows_ref, stage_ref, slots_ref, out_sems)


def spread(near_ref, rows_ref, stage_ref, slots_ref, sems):
    sent = []
    for d, columns in enumerate(tiles(rows_ref.shape[1])):
        stage_ref[:, columns] = dot(near_ref[...], rows_ref[:, columns], (0, 0)).astype(BF16)
        sent.append(store(stage_ref.at[:, columns], slots_ref.at[:, columns], sems.at[d]))
    for copy in sent:
        copy.wait()


def spread_kernel(near_ref, rows_ref, _, slots_ref, out_sems, stage_ref):
    spread(near_ref, rows_ref, stage_ref, slots_ref, out_sems)


def cut_kernel(numbers, rows_ref, *refs):
    out_refs, sems = refs[-1 - len(numbers) : -1], refs[-1]
    sets = rows_ref.shape[0]
    for copy in fetch(
        [rows_ref.at[q, i] for i in numbers for q in range(sets)],
        [out_ref.at[q] for out_ref in out_refs for q in range(sets)],
        sems,
    ):
        copy.wait()


def by_plane(rows_ref, plane_ref, parts):
    size = rows_ref.shape[0] // parts
    starts = [lax.rem(plane_ref[0] + (parts - i), parts) * size for i in range(parts)]
    return [rows_ref.at[pl.ds(pl.multiple_of(start, size), size)] for start in starts]


def chunks(span):
    size = 256 if span % 256 == 0 else span
    return [pl.ds(start, size) for start in range(0, span, size)]


def forward_kernel(parts, joined, plane_ref, *refs):
    sources, outs, refs = refs[: 4 * parts], refs[4 * parts : 4 * parts + 3], refs[4 * parts + 3 :]
    sems, out_sems, rows_ref, gate_ref, up_ref, down_ref = refs[:6]
    stage_ref, hidden_ref, by_gate_ref, by_up_ref = refs[6:]
    units, span = gate_ref.shape[0], gate_ref.shape[2]
    targets = [
        *by_plane(rows_ref, plane_ref, parts),
        *shares(gate_ref, parts, joined),
        *shares(up_ref, parts, joined),
        *shares(down_ref, parts, joined, 0),
    ]
    copies = fetch(sources, targets, sems)
    for copy in copies[: 3 * parts]:
        copy.wait()
    for i in range(units):
        for cut in chunks(span):
            pre_gate = dot(rows_ref[...], gate_ref[i, :, cut], (1, 0))
            pre_up = dot(rows_ref[...], up_ref[i, :, cut], (1, 0))
            sig = 0.5 + 0.5 * jnp.tanh(0.5 * pre_gate)
            act = pre_gate * sig
            hidden_ref[i, :, cut] = (act * pre_up).astype(BF16)
            by_gate_ref[i, :, cut] = pre_up * (sig + act * (1.0 - sig))
            by_up_ref[i, :, cut] = act
    sent = fetch([by_gate_ref, by_up_ref], outs[1:], out_sems)
    for copy in copies[3 * parts :]:
        copy.wait()
    for d, columns in enumerate(tiles(stage_ref.shape[1])):
        stage_ref[:, columns] = sum(
            dot(hidden_ref[i], down_ref[i, :, columns], (1, 0)) for i in range(units)
        ).astype(BF16)
        sent.append(store(stage_ref.at[:, columns], outs[0].at[:, columns], out_sems.at[2 + d]))
    for copy in sent:
        copy.wait()


def backward_kernel(parts, joined, lanes, plane_ref, spot_ref, *refs):
    sources, refs = refs[: 2 + 4 * parts], refs[2 + 4 * parts :]
    out_refs, refs = refs[: max(lanes, 1)], refs[max(lanes, 1) :]
    sems, out_sems, rows_ref, down_ref, by_gate_ref, by_up_ref, gate_ref, up_ref = refs[:8]
    stage_ref, back_gate_ref, back_up_ref = refs[8:]
    units, span = down_ref.shape[:2]
    targets = [
        *by_plane(rows_ref, plane_ref, parts),
        *shares(down_ref, parts, joined, 0),
        by_gate_ref,
        by_up_ref,
        *shares(gate_ref, parts, joined),
        *shares(up_ref, parts, joined),
    ]
    copies = fetch(sources, targets, sems)
    for copy in copies[: 2 + 2 * parts]:
        copy.wait()
    for i in range(units):
        for cut in chunks(span):
            back_hidden = dot(rows_ref[...], down_ref[i, cut, :], (1, 1))
            back_gate_ref[i, :, cut] = (back_hidden * by_gate_ref[i, :, cut]).astype(BF16)
            back_up_ref[i, :, cut] = (back_hidden * by_up_ref[i, :, cut]).astype(BF16)
    for copy in copies[2 + 2 * parts :]:
        copy.wait()
    sent = []
    for d, columns in enumerate(tiles(stage_ref.shape[-1])):
        rows = sum(
            dot(back_gate_ref[i], gate_ref[i, columns, :], (1, 1))
            + dot(back_up_ref[i], up_ref[i, columns, :], (1, 1))
            for i in range(units)
        )
        if lanes:
            rows = rows.reshape(lanes, rows.shape[0] // lanes, rows.shape[1])
            stage_ref[:, :, columns] = rows.astype(BF16)
        else:
            stage_ref[:, columns] = rows.astype(BF16)
            sent.append(store(stage_ref.at[:, columns], out_refs[0].at[:, columns], out_sems.at[d]))
    if lanes:
        sent = fetch([stage_ref.at[spot_ref[0] ^ b] for b in range(lanes)], out_refs, out_sems)
    for copy in sent:
        copy.wait()


def mix_kernel(place_ref, gates_ref, cotangent_ref, slots_ref, mixed_ref, gate_grad_ref):
    tok_rows, top_count = gates_ref.shape
    total, grads = None, []
    for k in range(top_count):
        raw = dot(place_ref[k * tok_rows : (k + 1) * tok_rows, :], slots_ref[...], (1, 0))
        grads.append(jnp.sum(raw * cotangent_ref[...].astype(F32), axis=1, keepdims=True))
        term = raw * gates_ref[:, k : k + 1]
        total = term if total is None else total + term
    mixed_ref[...] = total.astype(BF16)
    gate_grad_ref[...] = jnp.concatenate(grads, axis=1)


def sum_kernel(place_ref, gates_ref, *refs):
    lane_refs, out_ref, rows_ref = refs[:-2], refs[-2], refs[-1]
    if len(lane_refs) > 1:
        for b in range(0, len(lane_refs), 2):
            pair = jnp.concatenate([ref[...].astype(F32) for ref in lane_refs[b : b + 2]], axis=0)
            size = pair.shape[0]
            rows_ref[b // 2 * size : (b // 2 + 1) * size, :] = pair.astype(BF16)
    else:
        rows_ref = lane_refs[0]
    tok_rows, top_count = gates_ref.shape
    total = None
    for k in range(top_count):
        raw = dot(place_ref[k * tok_rows : (k + 1) * tok_rows, :], rows_ref[...], (1, 0))
        term = raw * gates_ref[:, k : k + 1]
        total = term if total is None else total + term
    out_ref[...] = total.astype(BF16)


def call(kernel, outs, flops, scratch=(), far=(), pinned=(), out_spaces=None, vmem=SMALL_VMEM):
    def run(*args):
        moved = sum(a.size * a.dtype.itemsize for a in (*args, *outs))
        spaces = [
            pltpu.SMEM
            if a.shape == (1,)
            else pl.ANY
            if i in far
            else pltpu.HBM
            if i in pinned
            else pltpu.VMEM
            for i, a in enumerate(args)
        ]
        return pl.pallas_call(
            kernel,
            out_shape=tuple(outs),
            in_specs=[pl.BlockSpec(memory_space=space) for space in spaces],
            out_specs=tuple(
                pl.BlockSpec(memory_space=space)
                for space in out_spaces or [pltpu.VMEM] * len(outs)
            ),
            scratch_shapes=scratch,
            compiler_params=pltpu.CompilerParams(vmem_limit_bytes=vmem),
            cost_estimate=pl.CostEstimate(flops=flops, bytes_accessed=moved, transcendentals=0),
        )(*args)

    return run


def body(tokens, cotangent, routes, gates, w_gate, w_up, w_down):
    tok_rows, width = tokens.shape
    top_count = routes.shape[1]
    parts, experts = lax.axis_size("dp"), lax.axis_size("expert")
    hidden = w_gate.shape[2]
    capacity = max(2, 3 * tok_rows * top_count // (2 * experts))
    slots = experts * capacity
    axes = ("dp", "expert")

    def device(g, j):
        return g * experts + j

    sets = experts // parts

    def home(e, c):
        return device((e + 1) % parts, e // parts * parts + c)

    swap = [(device(g, e), home(e, g)) for g in range(parts) for e in range(experts)]
    planes = [
        [[device(g, parts * q + c) for q in range(sets)] for g in range(parts)] for c in range(parts)
    ]
    everywhere = [[d for plane in planes[c] for d in plane] for c in range(parts)]
    in_plane = [plane for c in range(parts) for plane in planes[c]]

    def swapped(weight):
        return lax.ppermute(weight[0], axes, swap)

    def whole_expert(own):
        held = [own]
        for step in range(1, parts):
            turn = [(j, j // parts * parts + (j + step) % parts) for j in range(experts)]
            held.append(lax.ppermute(own, "expert", turn))
        return held

    def dispatch(rows, after=()):
        rows = rows.reshape(sets, parts * capacity, width)
        rows = lax.all_to_all(rows, axes, 0, 0, axis_index_groups=in_plane, tiled=True)
        rows = rows.reshape(sets, parts, capacity, width)

        def cut(numbers, space):
            return call(
                functools.partial(cut_kernel, numbers),
                [jax.ShapeDtypeStruct((sets, capacity, width), BF16)] * len(numbers),
                0,
                [sems(len(numbers) * sets)],
                far=(0,),
                pinned=range(1, 1 + len(after)),
                out_spaces=[space] * len(numbers),
            )(rows, *after)

        leaving = cut(range(1, parts), pl.ANY)
        cuts = [*cut(range(1), pltpu.HBM), *leaving]
        crossed = []
        for i, rows in enumerate(cuts):
            rows = rows.reshape(sets * capacity, width)
            if i > 0:
                rows = lax.ppermute(rows, "dp", [(g, (g + i) % parts) for g in range(parts)])
            crossed.append(rows)
        return crossed

    def send_back(rows):
        rows = rows.reshape(experts, capacity, width)
        return lax.all_to_all(
            rows, axes, 0, 0, axis_index_groups=everywhere, tiled=True
        ).reshape(slots, width)

    def send_lanes_back(lane_rows):
        passing = [b for b in range(1, experts) if b & (sets // 2)]
        others = [b for b in range(1, experts) if not b & (sets // 2)]
        received = {0: lane_rows[0]}
        for pair in itertools.zip_longest(passing, others):
            for b in pair:
                if b is not None:
                    pairs = [(group[k], group[k ^ b]) for group in everywhere for k in range(experts)]
                    received[b] = lax.ppermute(lane_rows[b], axes, pairs)
        return [received[b] for b in range(experts)]

    spread_flops = 2 * slots * tok_rows * width
    dot_flops = 2 * slots * width * hidden * parts
    slot_shape = jax.ShapeDtypeStruct((slots, width), BF16)
    place_shape = jax.ShapeDtypeStruct((top_count * tok_rows, slots), BF16)
    joined = hidden % 128 == 0
    units, span = (1, parts * hidden) if joined else (parts, hidden)
    unit_shape = jax.ShapeDtypeStruct((units, slots, span), F32)
    token_shape = jax.ShapeDtypeStruct((tok_rows, width), BF16)
    hidden_scratch = pltpu.VMEM((units, slots, span), BF16)
    unit_scratch = pltpu.VMEM((units, slots, span), F32)
    row_scratch = pltpu.VMEM((slots, width), BF16)
    in_scratch = pltpu.VMEM((units, width, span), BF16)
    down_scratch = pltpu.VMEM((units, span, width), BF16)
    pieces = len(tiles(width))

    def sems(number):
        return pltpu.SemaphoreType.DMA((number,))

    gate_own, up_own, down_own = swapped(w_gate), swapped(w_up), swapped(w_down)
    gate_w, up_w, down_w = whole_expert(gate_own), whole_expert(up_own), whole_expert(down_own)
    plane = lax.axis_index("dp").astype(jnp.int32).reshape(1)
    spot = plane * sets + (lax.axis_index("expert") // parts).astype(jnp.int32)
    by_lane = capacity % 8 == 0 and experts & (experts - 1) == 0
    x_slots, near, place, turned = call(
        functools.partial(place_kernel, experts, parts),
        [slot_shape, jax.ShapeDtypeStruct((tok_rows, slots), BF16), place_shape, place_shape],
        spread_flops,
        [sems(1), sems(pieces), pltpu.VMEM((tok_rows, width), BF16), row_scratch],
        pinned=(3,),
        out_spaces=[pltpu.HBM, pltpu.VMEM, pltpu.VMEM, pltpu.VMEM],
    )(plane, spot, routes, tokens)
    x_shares = dispatch(x_slots)
    (dy_slots,) = call(
        spread_kernel,
        [slot_shape],
        256 * spread_flops,
        [sems(pieces), row_scratch],
        pinned=(2,),
        out_spaces=[pltpu.HBM],
    )(near, cotangent, gate_own)
    out_rows, by_gate, by_up = call(
        functools.partial(forward_kernel, parts, joined),
        [slot_shape, unit_shape, unit_shape],
        3 * dot_flops,
        [sems(4 * parts), sems(2 + pieces), row_scratch, in_scratch, in_scratch, down_scratch]
        + [row_scratch, hidden_scratch, unit_scratch, unit_scratch],
        far=range(1, 1 + 4 * parts),
        out_spaces=[pltpu.HBM] * 3,
        vmem=LARGE_VMEM,
    )(plane, *x_shares, *gate_w, *up_w, *down_w)
    dy_shares = dispatch(dy_slots, (out_rows,))
    out_slots = send_back(out_rows)
    lane_shape = jax.ShapeDtypeStruct((capacity, width), BF16)
    grad_stage = pltpu.VMEM((experts, capacity, width), BF16) if by_lane else row_scratch
    grad_rows = call(
        functools.partial(backward_kernel, parts, joined, experts if by_lane else 0),
        [lane_shape] * experts if by_lane else [slot_shape],
        64 * dot_flops,
        [sems(2 + 4 * parts), sems(experts if by_lane else pieces), row_scratch, down_scratch]
        + [unit_scratch, unit_scratch, in_scratch, in_scratch]
        + [grad_stage, hidden_scratch, hidden_scratch],
        far=range(2, 4 + 4 * parts),
        out_spaces=[pltpu.HBM] * (experts if by_lane else 1),
        vmem=LARGE_VMEM,
    )(plane, spot, *dy_shares, *down_w, by_gate, by_up, *gate_w, *up_w)
    grad_slots = send_lanes_back(grad_rows) if by_lane else [send_back(grad_rows[0])]
    mixed, gate_grad = call(
        mix_kernel, [token_shape, jax.ShapeDtypeStruct(gates.shape, F32)], 2 * spread_flops
    )(place, gates, cotangent, out_slots)
    (token_grad,) = call(sum_kernel, [token_shape], 2 * spread_flops, [row_scratch])(
        turned if by_lane else place, gates, *grad_slots
    )
    return (mixed, token_grad, gate_grad)


def solution(mesh):
    rows, weights = P(("dp", "expert"), None), P("expert", None, "dp")
    return jax.shard_map(
        body,
        mesh=mesh,
        in_specs=(rows, rows, rows, rows, weights, weights, P("expert", "dp", None)),
        out_specs=(rows, rows, rows),
        check_vma=False,
    )
```

```python
import functools

import jax
import jax.numpy as jnp
from jax import lax
from jax.experimental import pallas as pl
from jax.experimental.pallas import tpu as pltpu
from jax.sharding import PartitionSpec as P

BF16 = jnp.bfloat16
F32 = jnp.float32
SMALL_VMEM, LARGE_VMEM = 12 << 20, 62_300_000


def dot(a, b, dims):
    return lax.dot_general(a, b, ((dims[:1], dims[1:]), ((), ())), preferred_element_type=F32)


def tiles(width):
    tile = min(512, width)
    return [slice(d, d + tile) for d in range(0, width, tile)]


def fetch(sources, targets, sems):
    copies = [pltpu.make_async_copy(s, t, sems.at[i]) for i, (s, t) in enumerate(zip(sources, targets))]
    for copy in copies:
        copy.start()
    return copies


def store(stage_ref, out_ref, sem):
    copy = pltpu.make_async_copy(stage_ref, out_ref, sem)
    copy.start()
    return copy


def shares(unit_ref, parts, joined, axis=1):
    if not joined:
        return [unit_ref.at[i] for i in range(parts)]
    size = unit_ref.shape[1 + axis] // parts
    cuts = [pl.ds(i * size, size) for i in range(parts)]
    return [unit_ref.at[0, cut] if axis == 0 else unit_ref.at[0, :, cut] for cut in cuts]


def ranks(routes, experts):
    tok_rows, top_count = routes.shape
    numbers = lax.broadcasted_iota(jnp.int32, (tok_rows, experts), 1)
    named = [numbers == routes[:, k : k + 1] for k in range(top_count)]
    chosen = sum(n.astype(F32) for n in named)
    earlier = (
        lax.broadcasted_iota(jnp.int32, (tok_rows, tok_rows), 1)
        < lax.broadcasted_iota(jnp.int32, (tok_rows, tok_rows), 0)
    ).astype(F32)
    rank = dot(earlier.astype(BF16), chosen.astype(BF16), (1, 0))
    return jnp.concatenate(
        [jnp.sum(jnp.where(n, rank, 0.0), axis=1, keepdims=True) for n in named], axis=1
    ).astype(jnp.int32)


def lanes_of(routes, experts, parts, plane, half):
    sets = experts // parts
    home_plane, home_set = lax.rem(routes + 1, parts), lax.div(routes, parts)
    local = home_set - half * (sets // 2)
    inside = (local >= 0) & (local < sets // 2)
    return home_plane * sets + home_set, local, lax.rem(home_plane + (parts - plane), parts), inside


def marks(slot, count):
    tok_rows, top_count = slot.shape
    numbers = lax.broadcasted_iota(jnp.int32, (tok_rows, count), 1)
    return [(numbers == slot[:, k : k + 1]).astype(F32) for k in range(top_count)]


def place_kernel(experts, parts, plane_ref, half_ref, routes_ref, tokens_ref, cotangent_ref, *refs):
    slots_ref, place_ref, sems, out_sems, rows_ref, near_ref, stage_ref = refs
    slots = slots_ref.shape[0]
    capacity = slots // experts
    tok_rows = routes_ref.shape[0]
    copies = fetch(
        [tokens_ref, cotangent_ref],
        [rows_ref.at[pl.ds(0, tok_rows)], rows_ref.at[pl.ds(tok_rows, tok_rows)]],
        sems,
    )
    routes = routes_ref[...]
    rank = ranks(routes, experts)
    back, local, ahead, inside = lanes_of(routes, experts, parts, plane_ref[0], half_ref[0])
    for k, mark in enumerate(marks(back * capacity + rank, slots)):
        place_ref[k * tok_rows : (k + 1) * tok_rows, :] = mark.astype(BF16)
    for i in range(2):
        slot = ((local * 2 + i) * parts + ahead) * capacity + rank
        near = sum(marks(jnp.where(inside, slot, -1), slots))
        near_ref[i * tok_rows : (i + 1) * tok_rows, :] = near.astype(BF16)
    for copy in copies:
        copy.wait()
    spread(near_ref, rows_ref, stage_ref, slots_ref, out_sems)


def far_kernel(experts, parts, plane_ref, half_ref, routes_ref, rows_ref, _, *refs):
    slots_ref, near_ref, out_sems, stage_ref = refs
    slots = slots_ref.shape[0]
    routes = routes_ref[...]
    _, local, ahead, inside = lanes_of(routes, experts, parts, plane_ref[0], half_ref[0])
    slot = (local * parts + ahead) * (2 * slots // experts) + ranks(routes, experts)
    near_ref[...] = sum(marks(jnp.where(inside, slot, -1), slots)).astype(BF16)
    spread(near_ref, rows_ref, stage_ref, slots_ref, out_sems)


def spread(near_ref, rows_ref, stage_ref, slots_ref, sems):
    sent = []
    for d, columns in enumerate(tiles(rows_ref.shape[1])):
        stage_ref[:, columns] = dot(near_ref[...], rows_ref[:, columns], (0, 0)).astype(BF16)
        sent.append(store(stage_ref.at[:, columns], slots_ref.at[:, columns], sems.at[d]))
    for copy in sent:
        copy.wait()


def spread_kernel(near_ref, rows_ref, *refs):
    slots_ref, out_sems, stage_ref = refs[-3:]
    spread(near_ref, rows_ref, stage_ref, slots_ref, out_sems)


def cut_kernel(array, numbers, half_ref, own_ref, far_ref, *refs):
    out_refs, sems = refs[-1 - len(numbers) : -1], refs[-1]
    sets = range(own_ref.shape[0])
    sources = [own_ref.at[q, array, i] for i in numbers for q in sets]
    targets = [out_ref.at[half_ref[0], q] for out_ref in out_refs for q in sets]
    sources += [far_ref.at[q, i] for i in numbers for q in sets]
    targets += [out_ref.at[1 - half_ref[0], q] for out_ref in out_refs for q in sets]
    for copy in fetch(sources, targets, sems):
        copy.wait()


def by_plane(rows_ref, plane_ref, parts):
    size = rows_ref.shape[0] // parts
    starts = [lax.rem(plane_ref[0] + (parts - i), parts) * size for i in range(parts)]
    return [rows_ref.at[pl.ds(pl.multiple_of(start, size), size)] for start in starts]


def chunks(span):
    size = 256 if span % 256 == 0 else span
    return [pl.ds(start, size) for start in range(0, span, size)]


def forward_kernel(parts, joined, plane_ref, *refs):
    sources, outs, refs = refs[: 4 * parts], refs[4 * parts : 4 * parts + 3], refs[4 * parts + 3 :]
    sems, out_sems, rows_ref, gate_ref, up_ref, down_ref = refs[:6]
    stage_ref, hidden_ref, by_gate_ref, by_up_ref = refs[6:]
    units, span = gate_ref.shape[0], gate_ref.shape[2]
    targets = [
        *by_plane(rows_ref, plane_ref, parts),
        *shares(gate_ref, parts, joined),
        *shares(up_ref, parts, joined),
        *shares(down_ref, parts, joined, 0),
    ]
    copies = fetch(sources, targets, sems)
    for copy in copies[: 3 * parts]:
        copy.wait()
    for i in range(units):
        for cut in chunks(span):
            pre_gate = dot(rows_ref[...], gate_ref[i, :, cut], (1, 0))
            pre_up = dot(rows_ref[...], up_ref[i, :, cut], (1, 0))
            sig = 0.5 + 0.5 * jnp.tanh(0.5 * pre_gate)
            act = pre_gate * sig
            hidden_ref[i, :, cut] = (act * pre_up).astype(BF16)
            by_gate_ref[i, :, cut] = pre_up * (sig + act * (1.0 - sig))
            by_up_ref[i, :, cut] = act
    sent = fetch([by_gate_ref, by_up_ref], outs[1:], out_sems)
    for copy in copies[3 * parts :]:
        copy.wait()
    for d, columns in enumerate(tiles(stage_ref.shape[1])):
        stage_ref[:, columns] = sum(
            dot(hidden_ref[i], down_ref[i, :, columns], (1, 0)) for i in range(units)
        ).astype(BF16)
        sent.append(store(stage_ref.at[:, columns], outs[0].at[:, columns], out_sems.at[2 + d]))
    for copy in sent:
        copy.wait()


def backward_kernel(parts, joined, plane_ref, *refs):
    sources, refs = refs[: 2 + 4 * parts], refs[2 + 4 * parts :]
    out_ref, sems, out_sems, rows_ref, down_ref, by_gate_ref, by_up_ref, gate_ref, up_ref = refs[:9]
    stage_ref, back_gate_ref, back_up_ref = refs[9:]
    units, span = down_ref.shape[:2]
    targets = [
        *by_plane(rows_ref, plane_ref, parts),
        *shares(down_ref, parts, joined, 0),
        by_gate_ref,
        by_up_ref,
        *shares(gate_ref, parts, joined),
        *shares(up_ref, parts, joined),
    ]
    copies = fetch(sources, targets, sems)
    for copy in copies[: 2 + 2 * parts]:
        copy.wait()
    for i in range(units):
        for cut in chunks(span):
            back_hidden = dot(rows_ref[...], down_ref[i, cut, :], (1, 1))
            back_gate_ref[i, :, cut] = (back_hidden * by_gate_ref[i, :, cut]).astype(BF16)
            back_up_ref[i, :, cut] = (back_hidden * by_up_ref[i, :, cut]).astype(BF16)
    for copy in copies[2 + 2 * parts :]:
        copy.wait()
    sent = []
    for d, columns in enumerate(tiles(stage_ref.shape[1])):
        stage_ref[:, columns] = sum(
            dot(back_gate_ref[i], gate_ref[i, columns, :], (1, 1))
            + dot(back_up_ref[i], up_ref[i, columns, :], (1, 1))
            for i in range(units)
        ).astype(BF16)
        sent.append(store(stage_ref.at[:, columns], out_ref.at[:, columns], out_sems.at[d]))
    for copy in sent:
        copy.wait()


def mix_kernel(place_ref, gates_ref, cotangent_ref, slots_ref, mixed_ref, gate_grad_ref):
    tok_rows, top_count = gates_ref.shape
    total, grads = None, []
    for k in range(top_count):
        raw = dot(place_ref[k * tok_rows : (k + 1) * tok_rows, :], slots_ref[...], (1, 0))
        grads.append(jnp.sum(raw * cotangent_ref[...].astype(F32), axis=1, keepdims=True))
        term = raw * gates_ref[:, k : k + 1]
        total = term if total is None else total + term
    mixed_ref[...] = total.astype(BF16)
    gate_grad_ref[...] = jnp.concatenate(grads, axis=1)


def sum_kernel(place_ref, gates_ref, slots_ref, out_ref):
    tok_rows, top_count = gates_ref.shape
    total = None
    for k in range(top_count):
        raw = dot(place_ref[k * tok_rows : (k + 1) * tok_rows, :], slots_ref[...], (1, 0))
        term = raw * gates_ref[:, k : k + 1]
        total = term if total is None else total + term
    out_ref[...] = total.astype(BF16)


def call(kernel, outs, flops, scratch=(), far=(), pinned=(), out_spaces=None, vmem=SMALL_VMEM):
    def run(*args):
        moved = sum(a.size * a.dtype.itemsize for a in (*args, *outs))
        spaces = [
            pltpu.SMEM
            if a.shape == (1,)
            else pl.ANY
            if i in far
            else pltpu.HBM
            if i in pinned
            else pltpu.VMEM
            for i, a in enumerate(args)
        ]
        return pl.pallas_call(
            kernel,
            out_shape=tuple(outs),
            in_specs=[pl.BlockSpec(memory_space=space) for space in spaces],
            out_specs=tuple(
                pl.BlockSpec(memory_space=space)
                for space in out_spaces or [pltpu.VMEM] * len(outs)
            ),
            scratch_shapes=scratch,
            compiler_params=pltpu.CompilerParams(vmem_limit_bytes=vmem),
            cost_estimate=pl.CostEstimate(flops=flops, bytes_accessed=moved, transcendentals=0),
        )(*args)

    return run


def body(tokens, cotangent, routes, gates, w_gate, w_up, w_down):
    tok_rows, width = tokens.shape
    top_count = routes.shape[1]
    parts, experts = lax.axis_size("dp"), lax.axis_size("expert")
    hidden = w_gate.shape[2]
    capacity = max(2, 3 * tok_rows * top_count // (2 * experts))
    slots = experts * capacity
    axes = ("dp", "expert")

    def device(g, j):
        return g * experts + j

    sets = experts // parts

    def home(e, c):
        return device((e + 1) % parts, e // parts * parts + c)

    swap = [(device(g, e), home(e, g)) for g in range(parts) for e in range(experts)]
    planes = [
        [[device(g, parts * q + c) for q in range(sets)] for g in range(parts)] for c in range(parts)
    ]
    everywhere = [[d for plane in planes[c] for d in plane] for c in range(parts)]
    near_sets = sets // 2
    in_half = [
        plane[start : start + near_sets]
        for c in range(parts)
        for plane in planes[c]
        for start in (0, near_sets)
    ]
    across = [(j, (j + experts // 2) % experts) for j in range(experts)]

    def swapped(weight):
        return lax.ppermute(weight[0], axes, swap)

    def whole_expert(own):
        held = [own]
        for step in range(1, parts):
            turn = [(j, j // parts * parts + (j + step) % parts) for j in range(experts)]
            held.append(lax.ppermute(own, "expert", turn))
        return held

    def far_side(array):
        return lax.ppermute(array, "expert", across)

    def to_sets(rows):
        rows = rows.reshape(near_sets, rows.shape[0] // near_sets, width)
        return lax.all_to_all(rows, axes, 0, 0, axis_index_groups=in_half, tiled=True)

    def to_planes(array, own, far, after=()):
        own = own.reshape(near_sets, 2, parts, capacity, width)
        far = far.reshape(near_sets, parts, capacity, width)

        def cut(numbers, space):
            return call(
                functools.partial(cut_kernel, array, numbers),
                [jax.ShapeDtypeStruct((2, near_sets, capacity, width), BF16)] * len(numbers),
                0,
                [sems(len(numbers) * sets)],
                far=(1, 2),
                pinned=range(3, 3 + len(after)),
                out_spaces=[space] * len(numbers),
            )(half, own, far, *after)

        leaving = cut(range(1, parts), pl.ANY)
        crossed = []
        for i, rows in enumerate([*cut(range(1), pltpu.HBM), *leaving]):
            rows = rows.reshape(sets * capacity, width)
            if i > 0:
                rows = lax.ppermute(rows, "dp", [(g, (g + i) % parts) for g in range(parts)])
            crossed.append(rows)
        return crossed

    def send_back(rows):
        rows = rows.reshape(experts, capacity, width)
        return lax.all_to_all(
            rows, axes, 0, 0, axis_index_groups=everywhere, tiled=True
        ).reshape(slots, width)

    spread_flops = 2 * slots * tok_rows * width
    dot_flops = 2 * slots * width * hidden * parts
    slot_shape = jax.ShapeDtypeStruct((slots, width), BF16)
    place_shape = jax.ShapeDtypeStruct((top_count * tok_rows, slots), BF16)
    joined = hidden % 128 == 0
    units, span = (1, parts * hidden) if joined else (parts, hidden)
    unit_shape = jax.ShapeDtypeStruct((units, slots, span), F32)
    token_shape = jax.ShapeDtypeStruct((tok_rows, width), BF16)
    hidden_scratch = pltpu.VMEM((units, slots, span), BF16)
    unit_scratch = pltpu.VMEM((units, slots, span), F32)
    row_scratch = pltpu.VMEM((slots, width), BF16)
    in_scratch = pltpu.VMEM((units, width, span), BF16)
    down_scratch = pltpu.VMEM((units, span, width), BF16)
    pieces = len(tiles(width))

    def sems(number):
        return pltpu.SemaphoreType.DMA((number,))

    far_tokens, far_routes = far_side(tokens), far_side(routes)
    gate_own, up_own, down_own = swapped(w_gate), swapped(w_up), swapped(w_down)
    far_cotangent = far_side(cotangent)
    gate_w, up_w, down_w = whole_expert(gate_own), whole_expert(up_own), whole_expert(down_own)
    plane = lax.axis_index("dp").astype(jnp.int32).reshape(1)
    half = (lax.axis_index("expert") // (experts // 2)).astype(jnp.int32).reshape(1)
    far_shape = jax.ShapeDtypeStruct((slots // 2, width), BF16)
    far_scratch = pltpu.VMEM((slots // 2, width), BF16)
    own_slots, place = call(
        functools.partial(place_kernel, experts, parts),
        [slot_shape, place_shape],
        2 * spread_flops,
        [sems(2), sems(pieces), pltpu.VMEM((2 * tok_rows, width), BF16)]
        + [pltpu.VMEM((2 * tok_rows, slots), BF16), row_scratch],
        pinned=(3, 4),
        out_spaces=[pltpu.HBM, pltpu.VMEM],
    )(plane, half, routes, tokens, cotangent)
    own_rows = to_sets(own_slots)
    far_x_slots, near = call(
        functools.partial(far_kernel, experts, parts),
        [far_shape, jax.ShapeDtypeStruct((tok_rows, slots // 2), BF16)],
        spread_flops,
        [sems(pieces), far_scratch],
        far=(4,),
        out_spaces=[pltpu.HBM, pltpu.VMEM],
    )(plane, half, far_routes, far_tokens, own_rows)
    x_shares = to_planes(0, own_rows, to_sets(far_x_slots))
    (far_dy_slots,) = call(
        spread_kernel,
        [far_shape],
        256 * spread_flops,
        [sems(pieces), far_scratch],
        pinned=(2, 3),
        out_spaces=[pltpu.HBM],
    )(near, far_cotangent, gate_own, up_own)
    far_dy_rows = to_sets(far_dy_slots)
    out_rows, by_gate, by_up = call(
        functools.partial(forward_kernel, parts, joined),
        [slot_shape, unit_shape, unit_shape],
        3 * dot_flops,
        [sems(4 * parts), sems(2 + pieces), row_scratch, in_scratch, in_scratch, down_scratch]
        + [row_scratch, hidden_scratch, unit_scratch, unit_scratch],
        far=range(1, 1 + 4 * parts),
        out_spaces=[pltpu.HBM] * 3,
        vmem=LARGE_VMEM,
    )(plane, *x_shares, *gate_w, *up_w, *down_w)
    dy_shares = to_planes(1, own_rows, far_dy_rows, (out_rows,))
    out_slots = send_back(out_rows)
    (grad_rows,) = call(
        functools.partial(backward_kernel, parts, joined),
        [slot_shape],
        64 * dot_flops,
        [sems(2 + 4 * parts), sems(pieces), row_scratch, down_scratch, unit_scratch, unit_scratch]
        + [in_scratch, in_scratch, row_scratch, hidden_scratch, hidden_scratch],
        far=range(1, 3 + 4 * parts),
        out_spaces=[pltpu.HBM],
        vmem=LARGE_VMEM,
    )(plane, *dy_shares, *down_w, by_gate, by_up, *gate_w, *up_w)
    grad_slots = send_back(grad_rows)
    mixed, gate_grad = call(
        mix_kernel, [token_shape, jax.ShapeDtypeStruct(gates.shape, F32)], 2 * spread_flops
    )(place, gates, cotangent, out_slots)
    (token_grad,) = call(sum_kernel, [token_shape], 2 * spread_flops)(place, gates, grad_slots)
    return (mixed, token_grad, gate_grad)


def solution(mesh):
    rows, weights = P(("dp", "expert"), None), P("expert", None, "dp")
    return jax.shard_map(
        body,
        mesh=mesh,
        in_specs=(rows, rows, rows, rows, weights, weights, P("expert", "dp", None)),
        out_specs=(rows, rows, rows),
        check_vma=False,
    )
```

```python
import functools

import jax
import jax.numpy as jnp
from jax import lax
from jax.experimental import pallas as pl
from jax.experimental.pallas import tpu as pltpu
from jax.sharding import PartitionSpec as P

BF16 = jnp.bfloat16
F32 = jnp.float32
SMALL_VMEM, LARGE_VMEM = 12 << 20, 62_300_000


def dot(a, b, dims):
    return lax.dot_general(a, b, ((dims[:1], dims[1:]), ((), ())), preferred_element_type=F32)


def tiles(width):
    tile = min(512, width)
    return [slice(d, d + tile) for d in range(0, width, tile)]


def fetch(sources, targets, sems):
    copies = [pltpu.make_async_copy(s, t, sems.at[i]) for i, (s, t) in enumerate(zip(sources, targets))]
    for copy in copies:
        copy.start()
    return copies


def store(stage_ref, out_ref, sem):
    copy = pltpu.make_async_copy(stage_ref, out_ref, sem)
    copy.start()
    return copy


def shares(unit_ref, parts, joined, axis=1):
    if not joined:
        return [unit_ref.at[i] for i in range(parts)]
    size = unit_ref.shape[1 + axis] // parts
    cuts = [pl.ds(i * size, size) for i in range(parts)]
    return [unit_ref.at[0, cut] if axis == 0 else unit_ref.at[0, :, cut] for cut in cuts]


def ranks(routes, experts):
    tok_rows, top_count = routes.shape
    numbers = lax.broadcasted_iota(jnp.int32, (tok_rows, experts), 1)
    named = [numbers == routes[:, k : k + 1] for k in range(top_count)]
    chosen = sum(n.astype(F32) for n in named)
    earlier = (
        lax.broadcasted_iota(jnp.int32, (tok_rows, tok_rows), 1)
        < lax.broadcasted_iota(jnp.int32, (tok_rows, tok_rows), 0)
    ).astype(F32)
    rank = dot(earlier.astype(BF16), chosen.astype(BF16), (1, 0))
    return jnp.concatenate(
        [jnp.sum(jnp.where(n, rank, 0.0), axis=1, keepdims=True) for n in named], axis=1
    ).astype(jnp.int32)


def lanes_of(routes, experts, parts, plane, half):
    sets = experts // parts
    home_plane, home_set = lax.rem(routes + 1, parts), lax.div(routes, parts)
    local = home_set - half * (sets // 2)
    inside = (local >= 0) & (local < sets // 2)
    return home_plane * sets + home_set, local, lax.rem(home_plane + (parts - plane), parts), inside


def marks(slot, count):
    tok_rows, top_count = slot.shape
    numbers = lax.broadcasted_iota(jnp.int32, (tok_rows, count), 1)
    return [(numbers == slot[:, k : k + 1]).astype(F32) for k in range(top_count)]


def place_kernel(experts, parts, plane_ref, half_ref, routes_ref, tokens_ref, cotangent_ref, *refs):
    slots_ref, place_ref, sems, out_sems, rows_ref, near_ref, stage_ref = refs
    slots = slots_ref.shape[0]
    capacity = slots // experts
    tok_rows = routes_ref.shape[0]
    copies = fetch(
        [tokens_ref, cotangent_ref],
        [rows_ref.at[pl.ds(0, tok_rows)], rows_ref.at[pl.ds(tok_rows, tok_rows)]],
        sems,
    )
    routes = routes_ref[...]
    rank = ranks(routes, experts)
    back, local, ahead, inside = lanes_of(routes, experts, parts, plane_ref[0], half_ref[0])
    for k, mark in enumerate(marks(back * capacity + rank, slots)):
        place_ref[k * tok_rows : (k + 1) * tok_rows, :] = mark.astype(BF16)
    for i in range(2):
        slot = ((local * 2 + i) * parts + ahead) * capacity + rank
        near = sum(marks(jnp.where(inside, slot, -1), slots))
        near_ref[i * tok_rows : (i + 1) * tok_rows, :] = near.astype(BF16)
    for copy in copies:
        copy.wait()
    spread(near_ref, rows_ref, stage_ref, slots_ref, out_sems)


def far_kernel(experts, parts, plane_ref, half_ref, routes_ref, rows_ref, *refs):
    slots_ref, near_ref, out_sems, stage_ref = refs
    slots = slots_ref.shape[0]
    routes = routes_ref[...]
    _, local, ahead, inside = lanes_of(routes, experts, parts, plane_ref[0], half_ref[0])
    slot = (local * parts + ahead) * (2 * slots // experts) + ranks(routes, experts)
    near_ref[...] = sum(marks(jnp.where(inside, slot, -1), slots)).astype(BF16)
    spread(near_ref, rows_ref, stage_ref, slots_ref, out_sems)


def spread(near_ref, rows_ref, stage_ref, slots_ref, sems):
    sent = []
    for d, columns in enumerate(tiles(rows_ref.shape[1])):
        stage_ref[:, columns] = dot(near_ref[...], rows_ref[:, columns], (0, 0)).astype(BF16)
        sent.append(store(stage_ref.at[:, columns], slots_ref.at[:, columns], sems.at[d]))
    for copy in sent:
        copy.wait()


def spread_kernel(near_ref, rows_ref, *refs):
    slots_ref, out_sems, stage_ref = refs[-3:]
    spread(near_ref, rows_ref, stage_ref, slots_ref, out_sems)


def in_place_kernel(*refs):
    pass


def cut_kernel(array, numbers, half_ref, own_ref, far_ref, *refs):
    out_refs, sems = refs[-1 - len(numbers) : -1], refs[-1]
    sets = range(own_ref.shape[0])
    sources = [own_ref.at[q, array, i] for i in numbers for q in sets]
    targets = [out_ref.at[half_ref[0], q] for out_ref in out_refs for q in sets]
    sources += [far_ref.at[q, i] for i in numbers for q in sets]
    targets += [out_ref.at[1 - half_ref[0], q] for out_ref in out_refs for q in sets]
    for copy in fetch(sources, targets, sems):
        copy.wait()


def by_plane(rows_ref, plane_ref, parts):
    size = rows_ref.shape[0] // parts
    starts = [lax.rem(plane_ref[0] + (parts - i), parts) * size for i in range(parts)]
    return [rows_ref.at[pl.ds(pl.multiple_of(start, size), size)] for start in starts]


def chunks(span):
    size = 256 if span % 256 == 0 else span
    return [pl.ds(start, size) for start in range(0, span, size)]


def forward_kernel(parts, joined, plane_ref, *refs):
    sources, outs, refs = refs[: 4 * parts], refs[4 * parts : 4 * parts + 3], refs[4 * parts + 3 :]
    sems, out_sems, rows_ref, gate_ref, up_ref, down_ref = refs[:6]
    stage_ref, hidden_ref, by_gate_ref, by_up_ref = refs[6:]
    units, span = gate_ref.shape[0], gate_ref.shape[2]
    targets = [
        *by_plane(rows_ref, plane_ref, parts),
        *shares(gate_ref, parts, joined),
        *shares(up_ref, parts, joined),
        *shares(down_ref, parts, joined, 0),
    ]
    copies = fetch(sources, targets, sems)
    for copy in copies[: 3 * parts]:
        copy.wait()
    for i in range(units):
        for cut in chunks(span):
            pre_gate = dot(rows_ref[...], gate_ref[i, :, cut], (1, 0))
            pre_up = dot(rows_ref[...], up_ref[i, :, cut], (1, 0))
            sig = 0.5 + 0.5 * jnp.tanh(0.5 * pre_gate)
            act = pre_gate * sig
            hidden_ref[i, :, cut] = (act * pre_up).astype(BF16)
            by_gate_ref[i, :, cut] = pre_up * (sig + act * (1.0 - sig))
            by_up_ref[i, :, cut] = act
    sent = fetch([by_gate_ref, by_up_ref], outs[1:], out_sems)
    for copy in copies[3 * parts :]:
        copy.wait()
    for d, columns in enumerate(tiles(stage_ref.shape[1])):
        stage_ref[:, columns] = sum(
            dot(hidden_ref[i], down_ref[i, :, columns], (1, 0)) for i in range(units)
        ).astype(BF16)
        sent.append(store(stage_ref.at[:, columns], outs[0].at[:, columns], out_sems.at[2 + d]))
    for copy in sent:
        copy.wait()


def backward_kernel(parts, joined, plane_ref, *refs):
    sources, refs = refs[: 2 + 4 * parts], refs[2 + 4 * parts :]
    out_ref, sems, out_sems, rows_ref, down_ref, by_gate_ref, by_up_ref, gate_ref, up_ref = refs[:9]
    stage_ref, back_gate_ref, back_up_ref = refs[9:]
    units, span = down_ref.shape[:2]
    targets = [
        *by_plane(rows_ref, plane_ref, parts),
        *shares(down_ref, parts, joined, 0),
        by_gate_ref,
        by_up_ref,
        *shares(gate_ref, parts, joined),
        *shares(up_ref, parts, joined),
    ]
    copies = fetch(sources, targets, sems)
    for copy in copies[: 2 + 2 * parts]:
        copy.wait()
    for i in range(units):
        for cut in chunks(span):
            back_hidden = dot(rows_ref[...], down_ref[i, cut, :], (1, 1))
            back_gate_ref[i, :, cut] = (back_hidden * by_gate_ref[i, :, cut]).astype(BF16)
            back_up_ref[i, :, cut] = (back_hidden * by_up_ref[i, :, cut]).astype(BF16)
    for copy in copies[2 + 2 * parts :]:
        copy.wait()
    sent = []
    for d, columns in enumerate(tiles(stage_ref.shape[1])):
        stage_ref[:, columns] = sum(
            dot(back_gate_ref[i], gate_ref[i, columns, :], (1, 1))
            + dot(back_up_ref[i], up_ref[i, columns, :], (1, 1))
            for i in range(units)
        ).astype(BF16)
        sent.append(store(stage_ref.at[:, columns], out_ref.at[:, columns], out_sems.at[d]))
    for copy in sent:
        copy.wait()


def mix_kernel(place_ref, gates_ref, cotangent_ref, slots_ref, mixed_ref, gate_grad_ref):
    tok_rows, top_count = gates_ref.shape
    total, grads = None, []
    for k in range(top_count):
        raw = dot(place_ref[k * tok_rows : (k + 1) * tok_rows, :], slots_ref[...], (1, 0))
        grads.append(jnp.sum(raw * cotangent_ref[...].astype(F32), axis=1, keepdims=True))
        term = raw * gates_ref[:, k : k + 1]
        total = term if total is None else total + term
    mixed_ref[...] = total.astype(BF16)
    gate_grad_ref[...] = jnp.concatenate(grads, axis=1)


def sum_kernel(place_ref, gates_ref, slots_ref, out_ref):
    tok_rows, top_count = gates_ref.shape
    total = None
    for k in range(top_count):
        raw = dot(place_ref[k * tok_rows : (k + 1) * tok_rows, :], slots_ref[...], (1, 0))
        term = raw * gates_ref[:, k : k + 1]
        total = term if total is None else total + term
    out_ref[...] = total.astype(BF16)


def call(kernel, outs, flops, scratch=(), far=(), pinned=(), out_spaces=None, vmem=SMALL_VMEM, aliases=None):
    def run(*args):
        moved = sum(a.size * a.dtype.itemsize for a in (*args, *outs))
        spaces = [
            pltpu.SMEM
            if a.shape == (1,)
            else pl.ANY
            if i in far
            else pltpu.HBM
            if i in pinned
            else pltpu.VMEM
            for i, a in enumerate(args)
        ]
        return pl.pallas_call(
            kernel,
            out_shape=tuple(outs),
            in_specs=[pl.BlockSpec(memory_space=space) for space in spaces],
            out_specs=tuple(
                pl.BlockSpec(memory_space=space)
                for space in out_spaces or [pltpu.VMEM] * len(outs)
            ),
            scratch_shapes=scratch,
            input_output_aliases=aliases or {},
            compiler_params=pltpu.CompilerParams(vmem_limit_bytes=vmem),
            cost_estimate=pl.CostEstimate(flops=flops, bytes_accessed=moved, transcendentals=0),
        )(*args)

    return run


def body(tokens, cotangent, routes, gates, w_gate, w_up, w_down):
    tok_rows, width = tokens.shape
    top_count = routes.shape[1]
    parts, experts = lax.axis_size("dp"), lax.axis_size("expert")
    hidden = w_gate.shape[2]
    capacity = max(2, 3 * tok_rows * top_count // (2 * experts))
    slots = experts * capacity
    axes = ("dp", "expert")

    def device(g, j):
        return g * experts + j

    sets = experts // parts

    def home(e, c):
        return device((e + 1) % parts, e // parts * parts + c)

    swap = [(device(g, e), home(e, g)) for g in range(parts) for e in range(experts)]
    planes = [
        [[device(g, parts * q + c) for q in range(sets)] for g in range(parts)] for c in range(parts)
    ]
    everywhere = [[d for plane in planes[c] for d in plane] for c in range(parts)]
    near_sets = sets // 2
    in_half = [
        plane[start : start + near_sets]
        for c in range(parts)
        for plane in planes[c]
        for start in (0, near_sets)
    ]
    across = [(j, (j + experts // 2) % experts) for j in range(experts)]

    def swapped(weight):
        return lax.ppermute(weight[0], axes, swap)

    def whole_expert(own):
        held = [own]
        for step in range(1, parts):
            turn = [(j, j // parts * parts + (j + step) % parts) for j in range(experts)]
            held.append(lax.ppermute(own, "expert", turn))
        return held

    def far_side(array):
        return lax.ppermute(array, "expert", across)

    def to_sets(rows):
        rows = rows.reshape(near_sets, rows.shape[0] // near_sets, width)
        return lax.all_to_all(rows, axes, 0, 0, axis_index_groups=in_half, tiled=True)

    def to_planes(array, own, far, after=()):
        own = own.reshape(near_sets, 2, parts, capacity, width)
        far = far.reshape(near_sets, parts, capacity, width)

        def cut(numbers, space):
            return call(
                functools.partial(cut_kernel, array, numbers),
                [jax.ShapeDtypeStruct((2, near_sets, capacity, width), BF16)] * len(numbers),
                0,
                [sems(len(numbers) * sets)],
                far=(1, 2),
                pinned=range(3, 3 + len(after)),
                out_spaces=[space] * len(numbers),
            )(half, own, far, *after)

        leaving = cut(range(1, parts), pl.ANY)
        crossed = []
        for i, rows in enumerate([*cut(range(1), pltpu.HBM), *leaving]):
            rows = rows.reshape(sets * capacity, width)
            if i > 0:
                rows = lax.ppermute(rows, "dp", [(g, (g + i) % parts) for g in range(parts)])
            crossed.append(rows)
        return crossed

    def send_back(rows):
        rows = rows.reshape(experts, capacity, width)
        return lax.all_to_all(
            rows, axes, 0, 0, axis_index_groups=everywhere, tiled=True
        ).reshape(slots, width)

    spread_flops = 2 * slots * tok_rows * width
    dot_flops = 2 * slots * width * hidden * parts
    slot_shape = jax.ShapeDtypeStruct((slots, width), BF16)
    place_shape = jax.ShapeDtypeStruct((top_count * tok_rows, slots), BF16)
    joined = hidden % 128 == 0
    units, span = (1, parts * hidden) if joined else (parts, hidden)
    unit_shape = jax.ShapeDtypeStruct((units, slots, span), F32)
    token_shape = jax.ShapeDtypeStruct((tok_rows, width), BF16)
    hidden_scratch = pltpu.VMEM((units, slots, span), BF16)
    unit_scratch = pltpu.VMEM((units, slots, span), F32)
    row_scratch = pltpu.VMEM((slots, width), BF16)
    in_scratch = pltpu.VMEM((units, width, span), BF16)
    down_scratch = pltpu.VMEM((units, span, width), BF16)
    pieces = len(tiles(width))

    def sems(number):
        return pltpu.SemaphoreType.DMA((number,))

    def behind(arrays, last):
        return call(
            in_place_kernel,
            [jax.ShapeDtypeStruct(a.shape, a.dtype) for a in arrays],
            0,
            pinned=range(len(arrays) + 1),
            out_spaces=[pltpu.HBM] * len(arrays),
            aliases={i: i for i in range(len(arrays))},
        )(*arrays, last)

    far_tokens, far_routes = far_side(tokens), far_side(routes)
    gate_own, up_own, down_own = swapped(w_gate), swapped(w_up), swapped(w_down)
    far_cotangent = far_side(cotangent)
    plane = lax.axis_index("dp").astype(jnp.int32).reshape(1)
    half = (lax.axis_index("expert") // (experts // 2)).astype(jnp.int32).reshape(1)
    far_shape = jax.ShapeDtypeStruct((slots // 2, width), BF16)
    far_scratch = pltpu.VMEM((slots // 2, width), BF16)
    own_slots, place = call(
        functools.partial(place_kernel, experts, parts),
        [slot_shape, place_shape],
        2 * spread_flops,
        [sems(2), sems(pieces), pltpu.VMEM((2 * tok_rows, width), BF16)]
        + [pltpu.VMEM((2 * tok_rows, slots), BF16), row_scratch],
        pinned=(3, 4),
        out_spaces=[pltpu.HBM, pltpu.VMEM],
    )(plane, half, routes, tokens, cotangent)
    own_rows = to_sets(own_slots)
    far_x_slots, near = call(
        functools.partial(far_kernel, experts, parts),
        [far_shape, jax.ShapeDtypeStruct((tok_rows, slots // 2), BF16)],
        256 * spread_flops,
        [sems(pieces), far_scratch],
        out_spaces=[pltpu.HBM, pltpu.VMEM],
    )(plane, half, far_routes, far_tokens)
    (far_x_slots,) = behind([far_x_slots], own_rows)
    x_shares = to_planes(0, own_rows, to_sets(far_x_slots))
    (far_dy_slots,) = call(
        spread_kernel,
        [far_shape],
        256 * spread_flops,
        [sems(pieces), far_scratch],
        pinned=(2, 3),
        out_spaces=[pltpu.HBM],
    )(near, far_cotangent, gate_own, up_own)
    far_dy_rows = to_sets(far_dy_slots)
    gate_w, up_w, down_w = map(whole_expert, behind([gate_own, up_own, down_own], far_dy_slots))
    out_rows, by_gate, by_up = call(
        functools.partial(forward_kernel, parts, joined),
        [slot_shape, unit_shape, unit_shape],
        3 * dot_flops,
        [sems(4 * parts), sems(2 + pieces), row_scratch, in_scratch, in_scratch, down_scratch]
        + [row_scratch, hidden_scratch, unit_scratch, unit_scratch],
        far=range(1, 1 + 4 * parts),
        out_spaces=[pltpu.HBM] * 3,
        vmem=LARGE_VMEM,
    )(plane, *x_shares, *gate_w, *up_w, *down_w)
    dy_shares = to_planes(1, own_rows, far_dy_rows, (out_rows,))
    out_slots = send_back(out_rows)
    (grad_rows,) = call(
        functools.partial(backward_kernel, parts, joined),
        [slot_shape],
        64 * dot_flops,
        [sems(2 + 4 * parts), sems(pieces), row_scratch, down_scratch, unit_scratch, unit_scratch]
        + [in_scratch, in_scratch, row_scratch, hidden_scratch, hidden_scratch],
        far=range(1, 3 + 4 * parts),
        out_spaces=[pltpu.HBM],
        vmem=LARGE_VMEM,
    )(plane, *dy_shares, *down_w, by_gate, by_up, *gate_w, *up_w)
    grad_slots = send_back(grad_rows)
    mixed, gate_grad = call(
        mix_kernel, [token_shape, jax.ShapeDtypeStruct(gates.shape, F32)], 2 * spread_flops
    )(place, gates, cotangent, out_slots)
    (token_grad,) = call(sum_kernel, [token_shape], 2 * spread_flops)(place, gates, grad_slots)
    return (mixed, token_grad, gate_grad)


def solution(mesh):
    rows, weights = P(("dp", "expert"), None), P("expert", None, "dp")
    return jax.shard_map(
        body,
        mesh=mesh,
        in_specs=(rows, rows, rows, rows, weights, weights, P("expert", "dp", None)),
        out_specs=(rows, rows, rows),
        check_vma=False,
    )
```

```python
import functools

import jax
import jax.numpy as jnp
from jax import lax
from jax.experimental import pallas as pl
from jax.experimental.pallas import tpu as pltpu
from jax.sharding import PartitionSpec as P

BF16 = jnp.bfloat16
F32 = jnp.float32
SMALL_VMEM, LARGE_VMEM = 12 << 20, 62_300_000


def dot(a, b, dims):
    return lax.dot_general(a, b, ((dims[:1], dims[1:]), ((), ())), preferred_element_type=F32)


def tiles(width):
    tile = min(512, width)
    return [slice(d, d + tile) for d in range(0, width, tile)]


def fetch(sources, targets, sems):
    copies = [pltpu.make_async_copy(s, t, sems.at[i]) for i, (s, t) in enumerate(zip(sources, targets))]
    for copy in copies:
        copy.start()
    return copies


def store(stage_ref, out_ref, sem):
    copy = pltpu.make_async_copy(stage_ref, out_ref, sem)
    copy.start()
    return copy


def shares(unit_ref, parts, joined, axis=1):
    if not joined:
        return [unit_ref.at[i] for i in range(parts)]
    size = unit_ref.shape[1 + axis] // parts
    cuts = [pl.ds(i * size, size) for i in range(parts)]
    return [unit_ref.at[0, cut] if axis == 0 else unit_ref.at[0, :, cut] for cut in cuts]


def place_kernel(experts, parts, plane_ref, routes_ref, tokens_ref, slots_ref, near_ref, *refs):
    place_ref, sems, out_sems, rows_ref, stage_ref = refs
    slots, width = slots_ref.shape
    capacity = slots // experts
    top_count, tok_rows = routes_ref.shape
    (copy,) = fetch([tokens_ref], [rows_ref], sems)
    same = lax.broadcasted_iota(jnp.int32, (tok_rows, tok_rows), 0) == lax.broadcasted_iota(
        jnp.int32, (tok_rows, tok_rows), 1
    )
    routes = dot(same.astype(F32).astype(BF16), routes_ref[...].astype(F32).astype(BF16), (1, 1))
    routes = routes.astype(jnp.int32)
    home_plane, home_set = lax.rem(routes + 1, parts), lax.div(routes, parts)
    lanes = home_plane * (experts // parts) + home_set
    near_lanes = home_set * parts + lax.rem(home_plane + (parts - plane_ref[0]), parts)
    numbers = lax.broadcasted_iota(jnp.int32, (tok_rows, experts), 1)
    named = [numbers == routes[:, k : k + 1] for k in range(top_count)]
    chosen = sum(n.astype(F32) for n in named)
    earlier = (
        lax.broadcasted_iota(jnp.int32, (tok_rows, tok_rows), 1)
        < lax.broadcasted_iota(jnp.int32, (tok_rows, tok_rows), 0)
    ).astype(F32)
    rank = dot(earlier.astype(BF16), chosen.astype(BF16), (1, 0))
    slot_numbers = lax.broadcasted_iota(jnp.int32, (tok_rows, slots), 1)
    near = None
    for k in range(top_count):
        own = jnp.sum(jnp.where(named[k], rank, 0.0), axis=1, keepdims=True).astype(jnp.int32)
        mark, near_mark = (
            (slot_numbers == order[:, k : k + 1] * capacity + own).astype(F32)
            for order in (lanes, near_lanes)
        )
        place_ref[k * tok_rows : (k + 1) * tok_rows, :] = mark.astype(BF16)
        near = near_mark if near is None else near + near_mark
    near_ref[...] = near.astype(BF16)
    copy.wait()
    spread(near_ref, rows_ref, stage_ref, slots_ref, out_sems)


def spread(near_ref, rows_ref, stage_ref, slots_ref, sems):
    sent = []
    for d, columns in enumerate(tiles(rows_ref.shape[1])):
        stage_ref[:, columns] = dot(near_ref[...], rows_ref[:, columns], (0, 0)).astype(BF16)
        sent.append(store(stage_ref.at[:, columns], slots_ref.at[:, columns], sems.at[d]))
    for copy in sent:
        copy.wait()


def spread_kernel(near_ref, rows_ref, _, slots_ref, out_sems, stage_ref):
    spread(near_ref, rows_ref, stage_ref, slots_ref, out_sems)


def cut_kernel(numbers, rows_ref, *refs):
    out_refs, sems = refs[-1 - len(numbers) : -1], refs[-1]
    sets = rows_ref.shape[0]
    for copy in fetch(
        [rows_ref.at[q, i] for i in numbers for q in range(sets)],
        [out_ref.at[q] for out_ref in out_refs for q in range(sets)],
        sems,
    ):
        copy.wait()


def by_plane(rows_ref, plane_ref, parts):
    size = rows_ref.shape[0] // parts
    starts = [lax.rem(plane_ref[0] + (parts - i), parts) * size for i in range(parts)]
    return [rows_ref.at[pl.ds(pl.multiple_of(start, size), size)] for start in starts]


def chunks(span):
    size = 256 if span % 256 == 0 else span
    return [pl.ds(start, size) for start in range(0, span, size)]


def forward_kernel(parts, joined, plane_ref, *refs):
    sources, outs, refs = refs[: 4 * parts], refs[4 * parts : 4 * parts + 3], refs[4 * parts + 3 :]
    sems, out_sems, rows_ref, gate_ref, up_ref, down_ref = refs[:6]
    stage_ref, hidden_ref, by_gate_ref, by_up_ref = refs[6:]
    units, span = gate_ref.shape[0], gate_ref.shape[2]
    targets = [
        *by_plane(rows_ref, plane_ref, parts),
        *shares(gate_ref, parts, joined),
        *shares(up_ref, parts, joined),
        *shares(down_ref, parts, joined, 0),
    ]
    copies = fetch(sources, targets, sems)
    for copy in copies[: 3 * parts]:
        copy.wait()
    for i in range(units):
        for cut in chunks(span):
            pre_gate = dot(rows_ref[...], gate_ref[i, :, cut], (1, 0))
            pre_up = dot(rows_ref[...], up_ref[i, :, cut], (1, 0))
            sig = 0.5 + 0.5 * jnp.tanh(0.5 * pre_gate)
            act = pre_gate * sig
            hidden_ref[i, :, cut] = (act * pre_up).astype(BF16)
            by_gate_ref[i, :, cut] = pre_up * (sig + act * (1.0 - sig))
            by_up_ref[i, :, cut] = act
    sent = fetch([by_gate_ref, by_up_ref], outs[1:], out_sems)
    for copy in copies[3 * parts :]:
        copy.wait()
    for d, columns in enumerate(tiles(stage_ref.shape[1])):
        stage_ref[:, columns] = sum(
            dot(hidden_ref[i], down_ref[i, :, columns], (1, 0)) for i in range(units)
        ).astype(BF16)
        sent.append(store(stage_ref.at[:, columns], outs[0].at[:, columns], out_sems.at[2 + d]))
    for copy in sent:
        copy.wait()


def backward_kernel(parts, joined, plane_ref, *refs):
    sources, refs = refs[: 2 + 4 * parts], refs[2 + 4 * parts :]
    out_ref, sems, out_sems, rows_ref, down_ref, by_gate_ref, by_up_ref, gate_ref, up_ref = refs[:9]
    stage_ref, back_gate_ref, back_up_ref = refs[9:]
    units, span = down_ref.shape[:2]
    targets = [
        *by_plane(rows_ref, plane_ref, parts),
        *shares(down_ref, parts, joined, 0),
        by_gate_ref,
        by_up_ref,
        *shares(gate_ref, parts, joined),
        *shares(up_ref, parts, joined),
    ]
    copies = fetch(sources, targets, sems)
    for copy in copies[: 2 + 2 * parts]:
        copy.wait()
    for i in range(units):
        for cut in chunks(span):
            back_hidden = dot(rows_ref[...], down_ref[i, cut, :], (1, 1))
            back_gate_ref[i, :, cut] = (back_hidden * by_gate_ref[i, :, cut]).astype(BF16)
            back_up_ref[i, :, cut] = (back_hidden * by_up_ref[i, :, cut]).astype(BF16)
    for copy in copies[2 + 2 * parts :]:
        copy.wait()
    sent = []
    for d, columns in enumerate(tiles(stage_ref.shape[1])):
        stage_ref[:, columns] = sum(
            dot(back_gate_ref[i], gate_ref[i, columns, :], (1, 1))
            + dot(back_up_ref[i], up_ref[i, columns, :], (1, 1))
            for i in range(units)
        ).astype(BF16)
        sent.append(store(stage_ref.at[:, columns], out_ref.at[:, columns], out_sems.at[d]))
    for copy in sent:
        copy.wait()


def mix_kernel(place_ref, gates_ref, cotangent_ref, slots_ref, mixed_ref, gate_grad_ref):
    tok_rows, top_count = gates_ref.shape
    total, grads = None, []
    for k in range(top_count):
        raw = dot(place_ref[k * tok_rows : (k + 1) * tok_rows, :], slots_ref[...], (1, 0))
        grads.append(jnp.sum(raw * cotangent_ref[...].astype(F32), axis=1, keepdims=True))
        term = raw * gates_ref[:, k : k + 1]
        total = term if total is None else total + term
    mixed_ref[...] = total.astype(BF16)
    gate_grad_ref[...] = jnp.concatenate(grads, axis=1)


def sum_kernel(place_ref, gates_ref, slots_ref, out_ref):
    tok_rows, top_count = gates_ref.shape
    total = None
    for k in range(top_count):
        raw = dot(place_ref[k * tok_rows : (k + 1) * tok_rows, :], slots_ref[...], (1, 0))
        term = raw * gates_ref[:, k : k + 1]
        total = term if total is None else total + term
    out_ref[...] = total.astype(BF16)


def call(kernel, outs, flops, scratch=(), far=(), pinned=(), out_spaces=None, vmem=SMALL_VMEM):
    def run(*args):
        moved = sum(a.size * a.dtype.itemsize for a in (*args, *outs))
        spaces = [
            pltpu.SMEM
            if a.shape == (1,)
            else pl.ANY
            if i in far
            else pltpu.HBM
            if i in pinned
            else pltpu.VMEM
            for i, a in enumerate(args)
        ]
        return pl.pallas_call(
            kernel,
            out_shape=tuple(outs),
            in_specs=[pl.BlockSpec(memory_space=space) for space in spaces],
            out_specs=tuple(
                pl.BlockSpec(memory_space=space)
                for space in out_spaces or [pltpu.VMEM] * len(outs)
            ),
            scratch_shapes=scratch,
            compiler_params=pltpu.CompilerParams(vmem_limit_bytes=vmem),
            cost_estimate=pl.CostEstimate(flops=flops, bytes_accessed=moved, transcendentals=0),
        )(*args)

    return run


def body(tokens, cotangent, routes, gates, w_gate, w_up, w_down):
    tok_rows, width = tokens.shape
    top_count = routes.shape[1]
    parts, experts = lax.axis_size("dp"), lax.axis_size("expert")
    hidden = w_gate.shape[2]
    capacity = max(2, 3 * tok_rows * top_count // (2 * experts))
    slots = experts * capacity
    axes = ("dp", "expert")

    def device(g, j):
        return g * experts + j

    sets = experts // parts

    def home(e, c):
        return device((e + 1) % parts, e // parts * parts + c)

    swap = [(device(g, e), home(e, g)) for g in range(parts) for e in range(experts)]
    planes = [
        [[device(g, parts * q + c) for q in range(sets)] for g in range(parts)] for c in range(parts)
    ]
    everywhere = [[d for plane in planes[c] for d in plane] for c in range(parts)]
    in_plane = [plane for c in range(parts) for plane in planes[c]]

    def swapped(weight):
        return lax.ppermute(weight[0], axes, swap)

    def whole_expert(own):
        held = [own]
        for step in range(1, parts):
            turn = [(j, j // parts * parts + (j + step) % parts) for j in range(experts)]
            held.append(lax.ppermute(own, "expert", turn))
        return held

    def dispatch(rows, after=()):
        rows = rows.reshape(sets, parts * capacity, width)
        rows = lax.all_to_all(rows, axes, 0, 0, axis_index_groups=in_plane, tiled=True)
        rows = rows.reshape(sets, parts, capacity, width)

        def cut(numbers, space):
            return call(
                functools.partial(cut_kernel, numbers),
                [jax.ShapeDtypeStruct((sets, capacity, width), BF16)] * len(numbers),
                0,
                [sems(len(numbers) * sets)],
                far=(0,),
                pinned=range(1, 1 + len(after)),
                out_spaces=[space] * len(numbers),
            )(rows, *after)

        leaving = cut(range(1, parts), pl.ANY)
        cuts = [*cut(range(1), pltpu.HBM), *leaving]
        crossed = []
        for i, rows in enumerate(cuts):
            rows = rows.reshape(sets * capacity, width)
            if i > 0:
                rows = lax.ppermute(rows, "dp", [(g, (g + i) % parts) for g in range(parts)])
            crossed.append(rows)
        return crossed

    def send_back(rows):
        rows = rows.reshape(experts, capacity, width)
        return lax.all_to_all(
            rows, axes, 0, 0, axis_index_groups=everywhere, tiled=True
        ).reshape(slots, width)

    spread_flops = 2 * slots * tok_rows * width
    dot_flops = 2 * slots * width * hidden * parts
    slot_shape = jax.ShapeDtypeStruct((slots, width), BF16)
    place_shape = jax.ShapeDtypeStruct((top_count * tok_rows, slots), BF16)
    joined = hidden % 128 == 0
    units, span = (1, parts * hidden) if joined else (parts, hidden)
    unit_shape = jax.ShapeDtypeStruct((units, slots, span), F32)
    token_shape = jax.ShapeDtypeStruct((tok_rows, width), BF16)
    hidden_scratch = pltpu.VMEM((units, slots, span), BF16)
    unit_scratch = pltpu.VMEM((units, slots, span), F32)
    row_scratch = pltpu.VMEM((slots, width), BF16)
    in_scratch = pltpu.VMEM((units, width, span), BF16)
    down_scratch = pltpu.VMEM((units, span, width), BF16)
    pieces = len(tiles(width))

    def sems(number):
        return pltpu.SemaphoreType.DMA((number,))

    gate_own, up_own, down_own = swapped(w_gate), swapped(w_up), swapped(w_down)
    gate_w, up_w, down_w = whole_expert(gate_own), whole_expert(up_own), whole_expert(down_own)
    plane = lax.axis_index("dp").astype(jnp.int32).reshape(1)
    x_slots, near, place = call(
        functools.partial(place_kernel, experts, parts),
        [slot_shape, jax.ShapeDtypeStruct((tok_rows, slots), BF16), place_shape],
        spread_flops,
        [sems(1), sems(pieces), pltpu.VMEM((tok_rows, width), BF16), row_scratch],
        pinned=(2,),
        out_spaces=[pltpu.HBM, pltpu.VMEM, pltpu.VMEM],
        vmem=LARGE_VMEM,
    )(plane, routes.T, tokens)
    x_shares = dispatch(x_slots)
    (dy_slots,) = call(
        spread_kernel,
        [slot_shape],
        256 * spread_flops,
        [sems(pieces), row_scratch],
        pinned=(2,),
        out_spaces=[pltpu.HBM],
    )(near, cotangent, gate_own)
    out_rows, by_gate, by_up = call(
        functools.partial(forward_kernel, parts, joined),
        [slot_shape, unit_shape, unit_shape],
        3 * dot_flops,
        [sems(4 * parts), sems(2 + pieces), row_scratch, in_scratch, in_scratch, down_scratch]
        + [row_scratch, hidden_scratch, unit_scratch, unit_scratch],
        far=range(1, 1 + 4 * parts),
        out_spaces=[pltpu.HBM] * 3,
        vmem=LARGE_VMEM,
    )(plane, *x_shares, *gate_w, *up_w, *down_w)
    dy_shares = dispatch(dy_slots, (out_rows,))
    out_slots = send_back(out_rows)
    (grad_rows,) = call(
        functools.partial(backward_kernel, parts, joined),
        [slot_shape],
        64 * dot_flops,
        [sems(2 + 4 * parts), sems(pieces), row_scratch, down_scratch, unit_scratch, unit_scratch]
        + [in_scratch, in_scratch, row_scratch, hidden_scratch, hidden_scratch],
        far=range(1, 3 + 4 * parts),
        out_spaces=[pltpu.HBM],
        vmem=LARGE_VMEM,
    )(plane, *dy_shares, *down_w, by_gate, by_up, *gate_w, *up_w)
    grad_slots = send_back(grad_rows)
    mixed, gate_grad = call(
        mix_kernel, [token_shape, jax.ShapeDtypeStruct(gates.shape, F32)], 2 * spread_flops
    )(place, gates, cotangent, out_slots)
    (token_grad,) = call(sum_kernel, [token_shape], 2 * spread_flops)(place, gates, grad_slots)
    return (mixed, token_grad, gate_grad)


def solution(mesh):
    rows, weights = P(("dp", "expert"), None), P("expert", None, "dp")
    return jax.shard_map(
        body,
        mesh=mesh,
        in_specs=(rows, rows, rows, rows, weights, weights, P("expert", "dp", None)),
        out_specs=(rows, rows, rows),
        check_vma=False,
    )
```

```python
import functools

import jax
import jax.numpy as jnp
from jax import lax
from jax.experimental import pallas as pl
from jax.experimental.pallas import tpu as pltpu
from jax.sharding import PartitionSpec as P

BF16 = jnp.bfloat16
F32 = jnp.float32
SMALL_VMEM, LARGE_VMEM = 12 << 20, 62_300_000


def dot(a, b, dims):
    return lax.dot_general(a, b, ((dims[:1], dims[1:]), ((), ())), preferred_element_type=F32)


def tiles(width):
    tile = min(512, width)
    return [slice(d, d + tile) for d in range(0, width, tile)]


def fetch(sources, targets, sems):
    copies = [pltpu.make_async_copy(s, t, sems.at[i]) for i, (s, t) in enumerate(zip(sources, targets))]
    for copy in copies:
        copy.start()
    return copies


def store(stage_ref, out_ref, sem):
    copy = pltpu.make_async_copy(stage_ref, out_ref, sem)
    copy.start()
    return copy


def shares(unit_ref, parts, joined, axis=1):
    if not joined:
        return [unit_ref.at[i] for i in range(parts)]
    size = unit_ref.shape[1 + axis] // parts
    cuts = [pl.ds(i * size, size) for i in range(parts)]
    return [unit_ref.at[0, cut] if axis == 0 else unit_ref.at[0, :, cut] for cut in cuts]


def place_kernel(experts, parts, plane_ref, routes_ref, tokens_ref, slots_ref, near_ref, *refs):
    place_ref, sems, out_sems, rows_ref, stage_ref = refs
    slots, width = slots_ref.shape
    capacity = slots // experts
    tok_rows, top_count = routes_ref.shape
    (copy,) = fetch([tokens_ref], [rows_ref], sems)
    routes = routes_ref[...]
    home_plane, home_set = lax.rem(routes + 1, parts), lax.div(routes, parts)
    lanes = home_plane * (experts // parts) + home_set
    near_lanes = home_set * parts + lax.rem(home_plane + (parts - plane_ref[0]), parts)
    numbers = lax.broadcasted_iota(jnp.int32, (tok_rows, experts), 1)
    named = [numbers == routes[:, k : k + 1] for k in range(top_count)]
    chosen = sum(n.astype(F32) for n in named)
    earlier = (
        lax.broadcasted_iota(jnp.int32, (tok_rows, tok_rows), 1)
        < lax.broadcasted_iota(jnp.int32, (tok_rows, tok_rows), 0)
    ).astype(F32)
    rank = dot(earlier.astype(BF16), chosen.astype(BF16), (1, 0))
    slot_numbers = lax.broadcasted_iota(jnp.int32, (tok_rows, slots), 1)
    near = None
    for k in range(top_count):
        own = jnp.sum(jnp.where(named[k], rank, 0.0), axis=1, keepdims=True).astype(jnp.int32)
        mark, near_mark = (
            (slot_numbers == order[:, k : k + 1] * capacity + own).astype(F32)
            for order in (lanes, near_lanes)
        )
        place_ref[k * tok_rows : (k + 1) * tok_rows, :] = mark.astype(BF16)
        near = near_mark if near is None else near + near_mark
    near_ref[...] = near.astype(BF16)
    copy.wait()
    spread(near_ref, rows_ref, stage_ref, slots_ref, out_sems)


def spread(near_ref, rows_ref, stage_ref, slots_ref, sems):
    sent = []
    for d, columns in enumerate(tiles(rows_ref.shape[1])):
        stage_ref[:, columns] = dot(near_ref[...], rows_ref[:, columns], (0, 0)).astype(BF16)
        sent.append(store(stage_ref.at[:, columns], slots_ref.at[:, columns], sems.at[d]))
    for copy in sent:
        copy.wait()


def spread_kernel(near_ref, rows_ref, _, slots_ref, out_sems, stage_ref):
    spread(near_ref, rows_ref, stage_ref, slots_ref, out_sems)


def cut_kernel(numbers, rows_ref, *refs):
    out_refs, sems = refs[-1 - len(numbers) : -1], refs[-1]
    sets = rows_ref.shape[0]
    for copy in fetch(
        [rows_ref.at[q, i] for i in numbers for q in range(sets)],
        [out_ref.at[q] for out_ref in out_refs for q in range(sets)],
        sems,
    ):
        copy.wait()


def plane_rows(plane_ref, parts, size, i):
    start = lax.rem(plane_ref[0] + (parts - i), parts) * size
    return pl.ds(pl.multiple_of(start, size), size)


def by_plane(rows_ref, plane_ref, parts):
    size = rows_ref.shape[0] // parts
    return [rows_ref.at[plane_rows(plane_ref, parts, size, i)] for i in range(parts)]


def chunks(span):
    size = 256 if span % 256 == 0 else span
    return [pl.ds(start, size) for start in range(0, span, size)]


def forward_kernel(parts, joined, plane_ref, *refs):
    sources, outs, refs = refs[: 4 * parts], refs[4 * parts : 4 * parts + 3], refs[4 * parts + 3 :]
    sems, out_sems, rows_ref, gate_ref, up_ref, down_ref = refs[:6]
    stage_ref, hidden_ref, by_gate_ref, by_up_ref = refs[6:]
    units, span = gate_ref.shape[0], gate_ref.shape[2]
    targets = [
        *by_plane(rows_ref, plane_ref, parts),
        *shares(gate_ref, parts, joined),
        *shares(up_ref, parts, joined),
        *shares(down_ref, parts, joined, 0),
    ]
    copies = fetch(sources, targets, sems)
    for copy in copies[: 3 * parts]:
        copy.wait()
    for i in range(units):
        for cut in chunks(span):
            pre_gate = dot(rows_ref[...], gate_ref[i, :, cut], (1, 0))
            pre_up = dot(rows_ref[...], up_ref[i, :, cut], (1, 0))
            sig = 0.5 + 0.5 * jnp.tanh(0.5 * pre_gate)
            act = pre_gate * sig
            hidden_ref[i, :, cut] = (act * pre_up).astype(BF16)
            by_gate_ref[i, :, cut] = pre_up * (sig + act * (1.0 - sig))
            by_up_ref[i, :, cut] = act
    sent = fetch([by_gate_ref, by_up_ref], outs[1:], out_sems)
    for copy in copies[3 * parts :]:
        copy.wait()
    for d, columns in enumerate(tiles(stage_ref.shape[1])):
        stage_ref[:, columns] = sum(
            dot(hidden_ref[i], down_ref[i, :, columns], (1, 0)) for i in range(units)
        ).astype(BF16)
        sent.append(store(stage_ref.at[:, columns], outs[0].at[:, columns], out_sems.at[2 + d]))
    for copy in sent:
        copy.wait()


def backward_kernel(parts, joined, numbers, plane_ref, *refs):
    count = len(numbers)
    sources, refs = refs[: count + 2 + 3 * parts], refs[count + 2 + 3 * parts :]
    out_ref, sems, out_sems, rows_ref, down_ref, by_gate_ref, by_up_ref, gate_ref, up_ref = refs[-12:-3]
    stage_ref, back_gate_ref, back_up_ref = refs[-3:]
    units, span = down_ref.shape[:2]
    size = out_ref.shape[0] // parts
    there = [plane_rows(plane_ref, parts, size, i) for i in numbers]
    here = [pl.ds(n * size, size) for n in range(count)]
    first = fetch(
        [*sources[:count], *sources[count : count + parts]]
        + [ref.at[:, rows] for ref in sources[count + parts : count + parts + 2] for rows in there],
        [*(rows_ref.at[rows] for rows in here), *shares(down_ref, parts, joined, 0)]
        + [ref.at[:, rows] for ref in (by_gate_ref, by_up_ref) for rows in here],
        sems.at[pl.ds(0, 3 * count + parts)],
    )
    second = fetch(
        sources[count + parts + 2 :],
        [*shares(gate_ref, parts, joined), *shares(up_ref, parts, joined)],
        sems.at[pl.ds(3 * count + parts, 2 * parts)],
    )
    for copy in first:
        copy.wait()
    for i in range(units):
        for cut in chunks(span):
            back_hidden = dot(rows_ref[...], down_ref[i, cut, :], (1, 1))
            back_gate_ref[i, :, cut] = (back_hidden * by_gate_ref[i, :, cut]).astype(BF16)
            back_up_ref[i, :, cut] = (back_hidden * by_up_ref[i, :, cut]).astype(BF16)
    for copy in second:
        copy.wait()
    sent = []
    for d, columns in enumerate(tiles(stage_ref.shape[1])):
        stage_ref[:, columns] = sum(
            dot(back_gate_ref[i], gate_ref[i, columns, :], (1, 1))
            + dot(back_up_ref[i], up_ref[i, columns, :], (1, 1))
            for i in range(units)
        ).astype(BF16)
        for n in range(count):
            target = out_ref.at[there[n], columns]
            sent.append(store(stage_ref.at[here[n], columns], target, out_sems.at[d * count + n]))
    for copy in sent:
        copy.wait()


def mix_kernel(place_ref, gates_ref, cotangent_ref, slots_ref, mixed_ref, gate_grad_ref):
    tok_rows, top_count = gates_ref.shape
    total, grads = None, []
    for k in range(top_count):
        raw = dot(place_ref[k * tok_rows : (k + 1) * tok_rows, :], slots_ref[...], (1, 0))
        grads.append(jnp.sum(raw * cotangent_ref[...].astype(F32), axis=1, keepdims=True))
        term = raw * gates_ref[:, k : k + 1]
        total = term if total is None else total + term
    mixed_ref[...] = total.astype(BF16)
    gate_grad_ref[...] = jnp.concatenate(grads, axis=1)


def sum_kernel(place_ref, gates_ref, slots_ref, out_ref):
    tok_rows, top_count = gates_ref.shape
    total = None
    for k in range(top_count):
        raw = dot(place_ref[k * tok_rows : (k + 1) * tok_rows, :], slots_ref[...], (1, 0))
        term = raw * gates_ref[:, k : k + 1]
        total = term if total is None else total + term
    out_ref[...] = total.astype(BF16)


def call(kernel, outs, flops, scratch=(), far=(), pinned=(), out_spaces=None, vmem=SMALL_VMEM, aliases=None):
    def run(*args):
        moved = sum(a.size * a.dtype.itemsize for a in (*args, *outs))
        spaces = [
            pltpu.SMEM
            if a.shape == (1,)
            else pl.ANY
            if i in far
            else pltpu.HBM
            if i in pinned
            else pltpu.VMEM
            for i, a in enumerate(args)
        ]
        return pl.pallas_call(
            kernel,
            out_shape=tuple(outs),
            in_specs=[pl.BlockSpec(memory_space=space) for space in spaces],
            out_specs=tuple(
                pl.BlockSpec(memory_space=space)
                for space in out_spaces or [pltpu.VMEM] * len(outs)
            ),
            scratch_shapes=scratch,
            input_output_aliases=aliases or {},
            compiler_params=pltpu.CompilerParams(vmem_limit_bytes=vmem),
            cost_estimate=pl.CostEstimate(flops=flops, bytes_accessed=moved, transcendentals=0),
        )(*args)

    return run


def body(tokens, cotangent, routes, gates, w_gate, w_up, w_down):
    tok_rows, width = tokens.shape
    top_count = routes.shape[1]
    parts, experts = lax.axis_size("dp"), lax.axis_size("expert")
    hidden = w_gate.shape[2]
    capacity = max(2, 3 * tok_rows * top_count // (2 * experts))
    slots = experts * capacity
    axes = ("dp", "expert")

    def device(g, j):
        return g * experts + j

    sets = experts // parts

    def home(e, c):
        return device((e + 1) % parts, e // parts * parts + c)

    swap = [(device(g, e), home(e, g)) for g in range(parts) for e in range(experts)]
    planes = [
        [[device(g, parts * q + c) for q in range(sets)] for g in range(parts)] for c in range(parts)
    ]
    everywhere = [[d for plane in planes[c] for d in plane] for c in range(parts)]
    in_plane = [plane for c in range(parts) for plane in planes[c]]

    def swapped(weight):
        return lax.ppermute(weight[0], axes, swap)

    def whole_expert(own):
        held = [own]
        for step in range(1, parts):
            turn = [(j, j // parts * parts + (j + step) % parts) for j in range(experts)]
            held.append(lax.ppermute(own, "expert", turn))
        return held

    def dispatch(rows, after=()):
        rows = rows.reshape(sets, parts * capacity, width)
        rows = lax.all_to_all(rows, axes, 0, 0, axis_index_groups=in_plane, tiled=True)
        rows = rows.reshape(sets, parts, capacity, width)

        def cut(numbers, space):
            return call(
                functools.partial(cut_kernel, numbers),
                [jax.ShapeDtypeStruct((sets, capacity, width), BF16)] * len(numbers),
                0,
                [sems(len(numbers) * sets)],
                far=(0,),
                pinned=range(1, 1 + len(after)),
                out_spaces=[space] * len(numbers),
            )(rows, *after)

        leaving = cut(range(1, parts), pl.ANY)
        cuts = [*cut(range(1), pltpu.HBM), *leaving]
        crossed = []
        for i, rows in enumerate(cuts):
            rows = rows.reshape(sets * capacity, width)
            if i > 0:
                rows = lax.ppermute(rows, "dp", [(g, (g + i) % parts) for g in range(parts)])
            crossed.append(rows)
        return crossed

    def send_back(rows):
        rows = rows.reshape(experts, capacity, width)
        return lax.all_to_all(
            rows, axes, 0, 0, axis_index_groups=everywhere, tiled=True
        ).reshape(slots, width)

    spread_flops = 2 * slots * tok_rows * width
    dot_flops = 2 * slots * width * hidden * parts
    slot_shape = jax.ShapeDtypeStruct((slots, width), BF16)
    place_shape = jax.ShapeDtypeStruct((top_count * tok_rows, slots), BF16)
    joined = hidden % 128 == 0
    units, span = (1, parts * hidden) if joined else (parts, hidden)
    unit_shape = jax.ShapeDtypeStruct((units, slots, span), F32)
    token_shape = jax.ShapeDtypeStruct((tok_rows, width), BF16)
    hidden_scratch = pltpu.VMEM((units, slots, span), BF16)
    unit_scratch = pltpu.VMEM((units, slots, span), F32)
    row_scratch = pltpu.VMEM((slots, width), BF16)
    in_scratch = pltpu.VMEM((units, width, span), BF16)
    down_scratch = pltpu.VMEM((units, span, width), BF16)
    pieces = len(tiles(width))

    def sems(number):
        return pltpu.SemaphoreType.DMA((number,))

    gate_own, up_own, down_own = swapped(w_gate), swapped(w_up), swapped(w_down)
    gate_w, up_w, down_w = whole_expert(gate_own), whole_expert(up_own), whole_expert(down_own)
    plane = lax.axis_index("dp").astype(jnp.int32).reshape(1)
    x_slots, near, place = call(
        functools.partial(place_kernel, experts, parts),
        [slot_shape, jax.ShapeDtypeStruct((tok_rows, slots), BF16), place_shape],
        spread_flops,
        [sems(1), sems(pieces), pltpu.VMEM((tok_rows, width), BF16), row_scratch],
        pinned=(2,),
        out_spaces=[pltpu.HBM, pltpu.VMEM, pltpu.VMEM],
    )(plane, routes, tokens)
    x_shares = dispatch(x_slots)
    (dy_slots,) = call(
        spread_kernel,
        [slot_shape],
        256 * spread_flops,
        [sems(pieces), row_scratch],
        pinned=(2,),
        out_spaces=[pltpu.HBM],
    )(near, cotangent, gate_own)
    out_rows, by_gate, by_up = call(
        functools.partial(forward_kernel, parts, joined),
        [slot_shape, unit_shape, unit_shape],
        3 * dot_flops,
        [sems(4 * parts), sems(2 + pieces), row_scratch, in_scratch, in_scratch, down_scratch]
        + [row_scratch, hidden_scratch, unit_scratch, unit_scratch],
        far=range(1, 1 + 4 * parts),
        out_spaces=[pltpu.HBM] * 3,
        vmem=LARGE_VMEM,
    )(plane, *x_shares, *gate_w, *up_w, *down_w)
    dy_shares = dispatch(dy_slots, (out_rows,))
    out_slots = send_back(out_rows)
    def backward(numbers, *into):
        count = len(numbers)
        rows = count * slots // parts
        unit = pltpu.VMEM((units, rows, span), F32)
        hidden_unit = pltpu.VMEM((units, rows, span), BF16)
        row_unit = pltpu.VMEM((rows, width), BF16)
        last = 1 + count + 2 + 3 * parts
        return call(
            functools.partial(backward_kernel, parts, joined, numbers),
            [slot_shape],
            3 * dot_flops * count // parts,
            [sems(3 * count + 3 * parts), sems(pieces * count), row_unit, down_scratch]
            + [unit, unit, in_scratch, in_scratch, row_unit, hidden_unit, hidden_unit],
            far=range(1, last),
            pinned=(last,),
            out_spaces=[pltpu.HBM],
            vmem=LARGE_VMEM,
            aliases={last: 0} if into else {},
        )(plane, *(dy_shares[i] for i in numbers), *down_w, by_gate, by_up, *gate_w, *up_w, *into)

    (grad_rows,) = backward(range(1, parts), *backward(range(1)))
    grad_slots = send_back(grad_rows)
    mixed, gate_grad = call(
        mix_kernel, [token_shape, jax.ShapeDtypeStruct(gates.shape, F32)], 2 * spread_flops
    )(place, gates, cotangent, out_slots)
    (token_grad,) = call(sum_kernel, [token_shape], 2 * spread_flops)(place, gates, grad_slots)
    return (mixed, token_grad, gate_grad)


def solution(mesh):
    rows, weights = P(("dp", "expert"), None), P("expert", None, "dp")
    return jax.shard_map(
        body,
        mesh=mesh,
        in_specs=(rows, rows, rows, rows, weights, weights, P("expert", "dp", None)),
        out_specs=(rows, rows, rows),
        check_vma=False,
    )
```

```python
import functools

import jax
import jax.numpy as jnp
from jax import lax
from jax.experimental import pallas as pl
from jax.experimental.pallas import tpu as pltpu
from jax.sharding import PartitionSpec as P

BF16 = jnp.bfloat16
F32 = jnp.float32
SMALL_VMEM, LARGE_VMEM = 12 << 20, 62_300_000


def dot(a, b, dims):
    return lax.dot_general(a, b, ((dims[:1], dims[1:]), ((), ())), preferred_element_type=F32)


def tiles(width):
    tile = min(512, width)
    return [slice(d, d + tile) for d in range(0, width, tile)]


def fetch(sources, targets, sems):
    copies = [pltpu.make_async_copy(s, t, sems.at[i]) for i, (s, t) in enumerate(zip(sources, targets))]
    for copy in copies:
        copy.start()
    return copies


def store(stage_ref, out_ref, sem):
    copy = pltpu.make_async_copy(stage_ref, out_ref, sem)
    copy.start()
    return copy


def shares(unit_ref, parts, joined, axis=1):
    if not joined:
        return [unit_ref.at[i] for i in range(parts)]
    size = unit_ref.shape[1 + axis] // parts
    cuts = [pl.ds(i * size, size) for i in range(parts)]
    return [unit_ref.at[0, cut] if axis == 0 else unit_ref.at[0, :, cut] for cut in cuts]


def place_kernel(experts, parts, plane_ref, routes_ref, tokens_ref, slots_ref, near_ref, *refs):
    place_ref, out_sems, stage_ref = refs
    slots, width = slots_ref.shape
    capacity = slots // experts
    top_count, tok_rows = routes_ref.shape
    same = lax.broadcasted_iota(jnp.int32, (tok_rows, tok_rows), 0) == lax.broadcasted_iota(
        jnp.int32, (tok_rows, tok_rows), 1
    )
    routes = dot(same.astype(F32).astype(BF16), routes_ref[...].astype(F32).astype(BF16), (1, 1))
    routes = routes.astype(jnp.int32)
    home_plane, home_set = lax.rem(routes + 1, parts), lax.div(routes, parts)
    lanes = home_plane * (experts // parts) + home_set
    near_lanes = home_set * parts + lax.rem(home_plane + (parts - plane_ref[0]), parts)
    numbers = lax.broadcasted_iota(jnp.int32, (tok_rows, experts), 1)
    named = [numbers == routes[:, k : k + 1] for k in range(top_count)]
    chosen = sum(n.astype(F32) for n in named)
    earlier = (
        lax.broadcasted_iota(jnp.int32, (tok_rows, tok_rows), 1)
        < lax.broadcasted_iota(jnp.int32, (tok_rows, tok_rows), 0)
    ).astype(F32)
    rank = dot(earlier.astype(BF16), chosen.astype(BF16), (1, 0))
    slot_numbers = lax.broadcasted_iota(jnp.int32, (tok_rows, slots), 1)
    near = None
    for k in range(top_count):
        own = jnp.sum(jnp.where(named[k], rank, 0.0), axis=1, keepdims=True).astype(jnp.int32)
        mark, near_mark = (
            (slot_numbers == order[:, k : k + 1] * capacity + own).astype(F32)
            for order in (lanes, near_lanes)
        )
        place_ref[k * tok_rows : (k + 1) * tok_rows, :] = mark.astype(BF16)
        near = near_mark if near is None else near + near_mark
    near_ref[...] = near.astype(BF16)
    spread(near_ref, tokens_ref, stage_ref, slots_ref, out_sems)


def spread(near_ref, rows_ref, stage_ref, slots_ref, sems):
    sent = []
    for d, columns in enumerate(tiles(rows_ref.shape[1])):
        stage_ref[:, columns] = dot(near_ref[...], rows_ref[:, columns], (0, 0)).astype(BF16)
        sent.append(store(stage_ref.at[:, columns], slots_ref.at[:, columns], sems.at[d]))
    for copy in sent:
        copy.wait()


def spread_kernel(near_ref, rows_ref, _, slots_ref, out_sems, stage_ref):
    spread(near_ref, rows_ref, stage_ref, slots_ref, out_sems)


def cut_kernel(numbers, rows_ref, *refs):
    out_refs, sems = refs[-1 - len(numbers) : -1], refs[-1]
    sets = rows_ref.shape[0]
    for copy in fetch(
        [rows_ref.at[q, i] for i in numbers for q in range(sets)],
        [out_ref.at[q] for out_ref in out_refs for q in range(sets)],
        sems,
    ):
        copy.wait()


def by_plane(rows_ref, plane_ref, parts):
    size = rows_ref.shape[0] // parts
    starts = [lax.rem(plane_ref[0] + (parts - i), parts) * size for i in range(parts)]
    return [rows_ref.at[pl.ds(pl.multiple_of(start, size), size)] for start in starts]


def chunks(span):
    size = 256 if span % 256 == 0 else span
    return [pl.ds(start, size) for start in range(0, span, size)]


def forward_kernel(parts, joined, plane_ref, *refs):
    sources, outs, refs = refs[: 4 * parts], refs[4 * parts : 4 * parts + 3], refs[4 * parts + 3 :]
    sems, out_sems, rows_ref, gate_ref, up_ref, down_ref = refs[:6]
    stage_ref, hidden_ref, by_gate_ref, by_up_ref = refs[6:]
    units, span = gate_ref.shape[0], gate_ref.shape[2]
    targets = [
        *by_plane(rows_ref, plane_ref, parts),
        *shares(gate_ref, parts, joined),
        *shares(up_ref, parts, joined),
        *shares(down_ref, parts, joined, 0),
    ]
    copies = fetch(sources, targets, sems)
    for copy in copies[: 3 * parts]:
        copy.wait()
    for i in range(units):
        for cut in chunks(span):
            pre_gate = dot(rows_ref[...], gate_ref[i, :, cut], (1, 0))
            pre_up = dot(rows_ref[...], up_ref[i, :, cut], (1, 0))
            sig = 0.5 + 0.5 * jnp.tanh(0.5 * pre_gate)
            act = pre_gate * sig
            hidden_ref[i, :, cut] = (act * pre_up).astype(BF16)
            by_gate_ref[i, :, cut] = pre_up * (sig + act * (1.0 - sig))
            by_up_ref[i, :, cut] = act
    sent = fetch([by_gate_ref, by_up_ref], outs[1:], out_sems)
    for copy in copies[3 * parts :]:
        copy.wait()
    for d, columns in enumerate(tiles(stage_ref.shape[1])):
        stage_ref[:, columns] = sum(
            dot(hidden_ref[i], down_ref[i, :, columns], (1, 0)) for i in range(units)
        ).astype(BF16)
        sent.append(store(stage_ref.at[:, columns], outs[0].at[:, columns], out_sems.at[2 + d]))
    for copy in sent:
        copy.wait()


def backward_kernel(parts, joined, plane_ref, *refs):
    sources, refs = refs[: 2 + 4 * parts], refs[2 + 4 * parts :]
    out_ref, sems, out_sems, rows_ref, down_ref, by_gate_ref, by_up_ref, gate_ref, up_ref = refs[:9]
    stage_ref, back_gate_ref, back_up_ref = refs[9:]
    units, span = down_ref.shape[:2]
    targets = [
        *by_plane(rows_ref, plane_ref, parts),
        *shares(down_ref, parts, joined, 0),
        by_gate_ref,
        by_up_ref,
        *shares(gate_ref, parts, joined),
        *shares(up_ref, parts, joined),
    ]
    copies = fetch(sources, targets, sems)
    for copy in copies[: 2 + 2 * parts]:
        copy.wait()
    for i in range(units):
        for cut in chunks(span):
            back_hidden = dot(rows_ref[...], down_ref[i, cut, :], (1, 1))
            back_gate_ref[i, :, cut] = (back_hidden * by_gate_ref[i, :, cut]).astype(BF16)
            back_up_ref[i, :, cut] = (back_hidden * by_up_ref[i, :, cut]).astype(BF16)
    for copy in copies[2 + 2 * parts :]:
        copy.wait()
    sent = []
    for d, columns in enumerate(tiles(stage_ref.shape[1])):
        stage_ref[:, columns] = sum(
            dot(back_gate_ref[i], gate_ref[i, columns, :], (1, 1))
            + dot(back_up_ref[i], up_ref[i, columns, :], (1, 1))
            for i in range(units)
        ).astype(BF16)
        sent.append(store(stage_ref.at[:, columns], out_ref.at[:, columns], out_sems.at[d]))
    for copy in sent:
        copy.wait()


def mix_kernel(place_ref, gates_ref, cotangent_ref, slots_ref, mixed_ref, gate_grad_ref):
    tok_rows, top_count = gates_ref.shape
    total, grads = None, []
    for k in range(top_count):
        raw = dot(place_ref[k * tok_rows : (k + 1) * tok_rows, :], slots_ref[...], (1, 0))
        grads.append(jnp.sum(raw * cotangent_ref[...].astype(F32), axis=1, keepdims=True))
        term = raw * gates_ref[:, k : k + 1]
        total = term if total is None else total + term
    mixed_ref[...] = total.astype(BF16)
    gate_grad_ref[...] = jnp.concatenate(grads, axis=1)


def sum_kernel(place_ref, gates_ref, slots_ref, out_ref, sems, stage_ref):
    tok_rows, top_count = gates_ref.shape
    sent = []
    for d, columns in enumerate(tiles(out_ref.shape[1])):
        raw = dot(place_ref[...], slots_ref[:, columns], (1, 0))
        total = None
        for k in range(top_count):
            term = raw[k * tok_rows : (k + 1) * tok_rows, :] * gates_ref[:, k : k + 1]
            total = term if total is None else total + term
        stage_ref[:, columns] = total.astype(BF16)
        sent.append(store(stage_ref.at[:, columns], out_ref.at[:, columns], sems.at[d]))
    for copy in sent:
        copy.wait()


def call(kernel, outs, flops, scratch=(), far=(), pinned=(), out_spaces=None, vmem=SMALL_VMEM):
    def run(*args):
        moved = sum(a.size * a.dtype.itemsize for a in (*args, *outs))
        spaces = [
            pltpu.SMEM
            if a.shape == (1,)
            else pl.ANY
            if i in far
            else pltpu.HBM
            if i in pinned
            else pltpu.VMEM
            for i, a in enumerate(args)
        ]
        return pl.pallas_call(
            kernel,
            out_shape=tuple(outs),
            in_specs=[pl.BlockSpec(memory_space=space) for space in spaces],
            out_specs=tuple(
                pl.BlockSpec(memory_space=space)
                for space in out_spaces or [pltpu.VMEM] * len(outs)
            ),
            scratch_shapes=scratch,
            compiler_params=pltpu.CompilerParams(vmem_limit_bytes=vmem),
            cost_estimate=pl.CostEstimate(flops=flops, bytes_accessed=moved, transcendentals=0),
        )(*args)

    return run


def body(tokens, cotangent, routes, gates, w_gate, w_up, w_down):
    tok_rows, width = tokens.shape
    top_count = routes.shape[1]
    parts, experts = lax.axis_size("dp"), lax.axis_size("expert")
    hidden = w_gate.shape[2]
    capacity = max(2, 3 * tok_rows * top_count // (2 * experts))
    slots = experts * capacity
    axes = ("dp", "expert")

    def device(g, j):
        return g * experts + j

    sets = experts // parts

    def home(e, c):
        return device((e + 1) % parts, e // parts * parts + c)

    swap = [(device(g, e), home(e, g)) for g in range(parts) for e in range(experts)]
    planes = [
        [[device(g, parts * q + c) for q in range(sets)] for g in range(parts)] for c in range(parts)
    ]
    everywhere = [[d for plane in planes[c] for d in plane] for c in range(parts)]
    in_plane = [plane for c in range(parts) for plane in planes[c]]

    def swapped(weight):
        return lax.ppermute(weight[0], axes, swap)

    def whole_expert(own):
        held = [own]
        for step in range(1, parts):
            turn = [(j, j // parts * parts + (j + step) % parts) for j in range(experts)]
            held.append(lax.ppermute(own, "expert", turn))
        return held

    def dispatch(rows, after=()):
        rows = rows.reshape(sets, parts * capacity, width)
        rows = lax.all_to_all(rows, axes, 0, 0, axis_index_groups=in_plane, tiled=True)
        rows = rows.reshape(sets, parts, capacity, width)

        def cut(numbers, space):
            return call(
                functools.partial(cut_kernel, numbers),
                [jax.ShapeDtypeStruct((sets, capacity, width), BF16)] * len(numbers),
                0,
                [sems(len(numbers) * sets)],
                far=(0,),
                pinned=range(1, 1 + len(after)),
                out_spaces=[space] * len(numbers),
            )(rows, *after)

        leaving = cut(range(1, parts), pl.ANY)
        cuts = [*cut(range(1), pltpu.HBM), *leaving]
        crossed = []
        for i, rows in enumerate(cuts):
            rows = rows.reshape(sets * capacity, width)
            if i > 0:
                rows = lax.ppermute(rows, "dp", [(g, (g + i) % parts) for g in range(parts)])
            crossed.append(rows)
        return crossed

    def send_back(rows):
        rows = rows.reshape(experts, capacity, width)
        return lax.all_to_all(
            rows, axes, 0, 0, axis_index_groups=everywhere, tiled=True
        ).reshape(slots, width)

    spread_flops = 2 * slots * tok_rows * width
    dot_flops = 2 * slots * width * hidden * parts
    slot_shape = jax.ShapeDtypeStruct((slots, width), BF16)
    place_shape = jax.ShapeDtypeStruct((top_count * tok_rows, slots), BF16)
    joined = hidden % 128 == 0
    units, span = (1, parts * hidden) if joined else (parts, hidden)
    unit_shape = jax.ShapeDtypeStruct((units, slots, span), F32)
    token_shape = jax.ShapeDtypeStruct((tok_rows, width), BF16)
    hidden_scratch = pltpu.VMEM((units, slots, span), BF16)
    unit_scratch = pltpu.VMEM((units, slots, span), F32)
    row_scratch = pltpu.VMEM((slots, width), BF16)
    in_scratch = pltpu.VMEM((units, width, span), BF16)
    down_scratch = pltpu.VMEM((units, span, width), BF16)
    pieces = len(tiles(width))

    def sems(number):
        return pltpu.SemaphoreType.DMA((number,))

    gate_own, up_own, down_own = swapped(w_gate), swapped(w_up), swapped(w_down)
    gate_w, up_w, down_w = whole_expert(gate_own), whole_expert(up_own), whole_expert(down_own)
    plane = lax.axis_index("dp").astype(jnp.int32).reshape(1)
    x_slots, near, place = call(
        functools.partial(place_kernel, experts, parts),
        [slot_shape, jax.ShapeDtypeStruct((tok_rows, slots), BF16), place_shape],
        spread_flops,
        [sems(pieces), row_scratch],
        out_spaces=[pltpu.HBM, pltpu.VMEM, pltpu.VMEM],
    )(plane, routes.T, tokens)
    x_shares = dispatch(x_slots)
    (dy_slots,) = call(
        spread_kernel,
        [slot_shape],
        256 * spread_flops,
        [sems(pieces), row_scratch],
        pinned=(2,),
        out_spaces=[pltpu.HBM],
    )(near, cotangent, gate_own)
    out_rows, by_gate, by_up = call(
        functools.partial(forward_kernel, parts, joined),
        [slot_shape, unit_shape, unit_shape],
        3 * dot_flops,
        [sems(4 * parts), sems(2 + pieces), row_scratch, in_scratch, in_scratch, down_scratch]
        + [row_scratch, hidden_scratch, unit_scratch, unit_scratch],
        far=range(1, 1 + 4 * parts),
        out_spaces=[pltpu.HBM] * 3,
        vmem=LARGE_VMEM,
    )(plane, *x_shares, *gate_w, *up_w, *down_w)
    dy_shares = dispatch(dy_slots, (out_rows,))
    out_slots = send_back(out_rows)
    (grad_rows,) = call(
        functools.partial(backward_kernel, parts, joined),
        [slot_shape],
        64 * dot_flops,
        [sems(2 + 4 * parts), sems(pieces), row_scratch, down_scratch, unit_scratch, unit_scratch]
        + [in_scratch, in_scratch, row_scratch, hidden_scratch, hidden_scratch],
        far=range(1, 3 + 4 * parts),
        out_spaces=[pltpu.HBM],
        vmem=LARGE_VMEM,
    )(plane, *dy_shares, *down_w, by_gate, by_up, *gate_w, *up_w)
    grad_slots = send_back(grad_rows)
    mixed, gate_grad = call(
        mix_kernel, [token_shape, jax.ShapeDtypeStruct(gates.shape, F32)], 2 * spread_flops
    )(place, gates, cotangent, out_slots)
    (token_grad,) = call(
        sum_kernel,
        [token_shape],
        2 * spread_flops,
        [sems(pieces), pltpu.VMEM((tok_rows, width), BF16)],
        out_spaces=[pltpu.HBM],
    )(place, gates, grad_slots)
    return (mixed, token_grad, gate_grad)


def solution(mesh):
    rows, weights = P(("dp", "expert"), None), P("expert", None, "dp")
    return jax.shard_map(
        body,
        mesh=mesh,
        in_specs=(rows, rows, rows, rows, weights, weights, P("expert", "dp", None)),
        out_specs=(rows, rows, rows),
        check_vma=False,
    )
```
